32 devices in a mesh: row: 8 (over z, core), col: 4 (over y, x).
Axes of the slice: x: 2, y: 2, z: 4, core: 2. Of those that a mesh axis runs over, the one named last changes fastest.
Arguments:
- pre_silu: bfloat16 [2, 24, 24, 256], P(None, 'row', 'col'), may hold values from -6 to 6
- out_grad: bfloat16 [2, 24, 24, 256], P(None, 'row', 'col'), may hold values from -6 to 6
- query_heads: bfloat16 [8, 576, 64], P('col', 'row'), may hold values from -10 to 10
- key_heads: bfloat16 [8, 576, 64], P('col', 'row'), may hold values from -10 to 10
- value_heads: bfloat16 [8, 576, 64], P('col', 'row'), may hold values from -6 to 6
- conv_weight: bfloat16 [3, 3, 256, 256], replicated, may hold values from -0.125 to 0.125
- out_weight: bfloat16 [256, 256], replicated, may hold values from -0.375 to 0.375
- input_weight: bfloat16 [256, 768], replicated, may hold values from -0.375 to 0.375
Outputs:
- grad_input: bfloat16 [2, 24, 24, 256], P(None, 'row', 'col')
The draws below stay inside these ranges and needn't reach their ends.
All inputs are finite; a program needn't handle non-finite values.
Results may differ from the reference program's by a relative error of at most 0.0095.
Values may be sent and summed in bfloat16 or wider, within the bound.
No kernel may reach another device: no remote copies, remote signals or barrier semaphores. Data moves between devices by JAX's collectives and lax.ppermute only.
A program may use at most 64 MiB of HBM per device.

```python
import jax
import jax.numpy as jnp
from jax import lax

C = 256
HEADS = 4
HD = 64
TR = 3
SAMPLES = 2
HGT = 24
WID = 24
TOKENS = 576
COMBOS = 8
N_ROW = 8


def drawn_pair(key):
    folded = jax.random.fold_in(key, 4242)
    key_one, key_two = jax.random.split(folded, 2)
    full_shape = (COMBOS, TOKENS, HD)
    queries = jnp.clip(1.4 * jax.random.normal(key_one, full_shape), -8.0, 8.0)
    keys_all = jnp.clip(1.4 * jax.random.normal(key_two, full_shape), -8.0, 8.0)
    return (queries, keys_all)


def draw_query_heads(key, part):
    return drawn_pair(key)[0].astype(jnp.bfloat16)


def draw_key_heads(key, part):
    return drawn_pair(key)[1].astype(jnp.bfloat16)


def steps_of(key, extent, cuts, smallest, top_value):
    def one(position, blocks):
        steps = jax.random.uniform(jax.random.fold_in(jax.random.fold_in(key, 6), position), (blocks,), jnp.float32, smallest / len(cuts), top_value / len(cuts))
        return jnp.repeat(jnp.exp(steps), extent[position] // blocks).reshape((-1,) + (1,) * (len(extent) - position - 1))

    loudness = one(*cuts[0])
    for cut in cuts[1:]:
        loudness = loudness * one(*cut)
    return loudness


def centred(rng, extent, scale, reach, cuts=(), kind=jnp.bfloat16):
    result = jax.random.normal(rng, extent, jnp.float32) * scale
    if len(cuts) > 0:
        result = steps_of(rng, extent, cuts, -0.22, 0.18) * result
    return jnp.clip(result, min=-reach, max=reach).astype(kind)


def setup_inputs(seed: int = 0) -> dict:
    splits = jax.random.split(jax.random.key(seed), 9)
    return {
        "pre_silu": centred(splits[0], (SAMPLES, HGT, WID, C), 1.5, 6.0, ((1, 8), (2, 4))),
        "out_grad": centred(splits[1], (SAMPLES, HGT, WID, C), 1.0, 6.0, ((1, 8), (2, 4))),
        "query_heads": draw_query_heads(jax.random.fold_in(splits[8], 71), 0),
        "key_heads": draw_key_heads(jax.random.fold_in(splits[8], 71), 0),
        "value_heads": centred(splits[4], (COMBOS, TOKENS, HD), 1.0, 6.0, ((0, 4), (1, 8))),
        "conv_weight": centred(splits[5], (3, 3, C, C), (9 * C) ** -0.5, 0.125),
        "out_weight": centred(splits[6], (C, C), C ** -0.5, 0.375),
        "input_weight": centred(splits[7], (C, 3 * C), C ** -0.5, 0.375),
    }


def reference(pre_silu, out_grad, query_heads, key_heads, value_heads, conv_weight, out_weight, input_weight):
    factor = HD ** -0.5
    padded = jnp.pad(out_grad.astype(jnp.float32), ((0, 0), (1, 1), (1, 1), (0, 0)))
    kernel = conv_weight.astype(jnp.float32)
    conv_sum = jnp.zeros((SAMPLES, HGT, WID, C), jnp.float32)
    for shift_r in (-1, 0, 1):
        for shift_c in (-1, 0, 1):
            window = padded[:, 1 - shift_r:1 - shift_r + HGT, 1 - shift_c:1 - shift_c + WID, :]
            conv_sum = conv_sum + jnp.einsum('srcd,ed->srce', window, kernel[shift_r + 1, shift_c + 1])
    z_float = pre_silu.astype(jnp.float32)
    sigmoid_z = jax.nn.sigmoid(z_float)
    grad_z = (conv_sum * sigmoid_z * (1.0 + z_float * (1.0 - sigmoid_z))).astype(jnp.bfloat16)
    grad_attn = jnp.einsum('srcd,hed->shrce', grad_z.astype(jnp.float32),
                           out_weight.astype(jnp.float32).reshape(HEADS, HD, C)).astype(jnp.bfloat16)
    grad_attn = grad_attn.reshape(COMBOS, TOKENS, HD)
    strip_rows = TR * WID

    def one_combo(operands):
        queries, keys_all, values, grad_out = operands

        def strip_step(running, pieces):
            grad_key, grad_value = running
            query_strip, grad_strip = pieces
            scores = jnp.dot(query_strip, keys_all.T, preferred_element_type=jnp.float32) * factor
            log_norm = jax.scipy.special.logsumexp(scores, axis=1)
            prob_block = jnp.exp(scores - log_norm[:, None])
            grad_probs = jnp.dot(grad_strip, values.T, preferred_element_type=jnp.float32)
            row_dot = jnp.sum(prob_block * grad_probs, axis=1)
            grad_scores = (prob_block * (grad_probs - row_dot[:, None])).astype(jnp.bfloat16)
            grad_query = jnp.dot(grad_scores, keys_all, preferred_element_type=jnp.float32) * factor
            grad_key = grad_key + jnp.dot(grad_scores.T, query_strip, preferred_element_type=jnp.float32) * factor
            grad_value = grad_value + jnp.dot(prob_block.astype(jnp.bfloat16).T, grad_strip,
                                              preferred_element_type=jnp.float32)
            return (grad_key, grad_value), grad_query

        zero_rows = jnp.zeros((TOKENS, HD), jnp.float32)
        finals, grad_query = lax.scan(strip_step, (zero_rows, zero_rows),
                                      (queries.reshape(N_ROW, strip_rows, HD), grad_out.reshape(N_ROW, strip_rows, HD)))
        return jnp.stack([grad_query.reshape(TOKENS, HD), finals[0], finals[1]]).astype(jnp.bfloat16)

    grads = lax.map(one_combo, (query_heads, key_heads, value_heads, grad_attn))
    stacked = grads.reshape(SAMPLES, HEADS, 3, HGT, WID, HD).astype(jnp.float32)
    projected = jnp.einsum('shkrce,dkhe->srcd', stacked, input_weight.astype(jnp.float32).reshape(C, 3, HEADS, HD))
    return (grad_z.astype(jnp.float32) + projected).astype(jnp.bfloat16)
```

```python
import functools

import jax
import jax.numpy as jnp
import numpy as np
from jax import lax
from jax.experimental import pallas as pl
from jax.experimental.pallas import tpu as pltpu
from jax.sharding import PartitionSpec as P

HEADS = 4
VMEM_BYTES = 60 * 1024 * 1024
UNROLLED_CHUNKS = 16
F32 = jnp.float32
BF16 = jnp.bfloat16


def dot(left, right, left_dim=1, right_dim=0):
    return lax.dot_general(
        left, right, (((left_dim,), (right_dim,)), ((), ())), preferred_element_type=F32
    )


def call(kernel, out_shape, scratch=(), scalars=1):
    whole = pl.BlockSpec(memory_space=pltpu.VMEM)
    scalar = pl.BlockSpec(memory_space=pltpu.SMEM)

    def run(*operands):
        return pl.pallas_call(
            kernel,
            out_shape=out_shape,
            in_specs=[scalar] * scalars + [whole] * (len(operands) - scalars),
            out_specs=jax.tree.map(lambda _: whole, out_shape),
            scratch_shapes=list(scratch),
            compiler_params=pltpu.CompilerParams(vmem_limit_bytes=VMEM_BYTES),
        )(*operands)

    return run


def pad8(amount):
    return -(-amount // 8) * 8


def shift_selector(rows, cols, tiles):
    width, padded = tiles * cols, pad8(cols)
    select = np.zeros((3, rows, width, tiles, rows, padded), np.float32)
    for shift in (-1, 0, 1):
        for j in range(max(0, shift), min(width, width + shift)):
            tile, inner = divmod(j - shift, cols)
            for i in range(rows):
                select[shift + 1, i, j, tile, i, inner] = 1
    return select.reshape(3, rows * width, tiles * rows * padded)


def tile_selector(rows, cols, tiles):
    width, padded = tiles * cols, pad8(cols)
    select = np.zeros((tiles, rows, padded, rows, width), np.float32)
    for tile in range(tiles):
        for i in range(rows):
            for inner in range(cols):
                select[tile, i, inner, i, tile * cols + inner] = 1
    return select.reshape(tiles, rows * padded, rows * width)


def strip_kernel(n_col, per_sample, *refs):
    (place, own_grad, own_silu, *rest) = refs
    received, rest = rest[: n_col - 1], rest[n_col - 1 :]
    (
        halo_core,
        halo_chip,
        kv_own,
        kv_other,
        queries,
        conv_weight,
        out_weight,
        shifts,
        middle,
        dkv_own,
        dkv_other,
        dq_ref,
        gz_ref,
        grads,
        silus,
    ) = rest
    col, core = place[0], place[1]
    sample = col // per_sample
    rows, cols, channels = own_grad.shape[1:]
    width = n_col * cols
    strip = rows * width

    grads[...] = jnp.zeros_like(grads)
    silus[...] = jnp.zeros_like(silus)
    lower = jnp.where(core == 0, rows + 1, 0)
    upper = jnp.where(core == 0, 0, rows + 1)
    for k in range(n_col):
        tile = col ^ k
        for i in range(rows):
            grad = own_grad[sample, i] if k == 0 else received[k - 1][0, i]
            silu = own_silu[sample, i] if k == 0 else received[k - 1][1, i]
            grads[tile, i + 1, :cols] = grad.astype(F32)
            silus[tile, i, :cols] = silu.astype(F32)
        grads[tile, lower, :cols] = halo_core[k].astype(F32)
        grads[tile, upper, :cols] = halo_chip[k].astype(F32)
    flat = grads[...].reshape(-1, channels).astype(BF16)
    conv = jnp.zeros((strip, channels), F32)
    for b in (-1, 0, 1):
        shifted = dot(shifts[b + 1], flat)
        for a in (-1, 0, 1):
            window = shifted[(1 - a) * width : (1 - a) * width + strip].astype(BF16)
            conv = conv + dot(window, conv_weight[a + 1, b + 1], 1, 1)
    z = dot(middle[...], silus[...].reshape(-1, channels).astype(BF16))
    sigma = 1.0 / (1.0 + jnp.exp(-z))
    grad_z = (conv * sigma * (1.0 + z * (1.0 - sigma))).astype(BF16)
    gz_ref[...] = grad_z

    lanes = queries.shape[1]
    half = lanes // 2
    first = col % per_sample * lanes
    grad_out = dot(grad_z, out_weight[pl.ds(pl.multiple_of(first, lanes), lanes), :], 1, 1)
    grad_out = grad_out.astype(BF16)
    low = lax.broadcasted_iota(jnp.int32, (strip, lanes), 1) < half
    factor = half**-0.5
    query = queries[...] * jnp.asarray(factor, BF16)
    none = jnp.zeros_like(query)
    padded_query = (jnp.where(low, none, query), jnp.where(low, query, none))
    padded_grad = (jnp.where(low, grad_out, none), jnp.where(low, none, grad_out))

    blocks = kv_own.shape[0]
    sources = ((kv_own, dkv_own), (kv_other, dkv_other))
    small = 2 * blocks <= UNROLLED_CHUNKS
    grad_query = []
    for head in (0, 1):
        ask, cot = padded_query[head], padded_grad[head]

        def products(kv):
            return dot(kv, ask, 1, 1), dot(kv, cot, 1, 1)

        def finish(kv, scores, probs_grad, top, scale, row_dot):
            probs = jnp.exp(scores - top) * scale
            grad_scores = (probs * (probs_grad - row_dot)).astype(BF16)
            dkv = dot(grad_scores, ask) + dot(probs.astype(BF16), cot)
            return dkv, dot(grad_scores, kv, 0, 0)

        if small:
            chunks = [(src[j, head], dst, j) for src, dst in sources for j in range(blocks)]
            both = [products(kv) for kv, _, _ in chunks]
            top = functools.reduce(jnp.maximum, [s for s, _ in both])
            top = jnp.max(top, axis=0, keepdims=True)
            exps = [jnp.exp(s - top) for s, _ in both]
            norm = jnp.sum(sum(exps), axis=0, keepdims=True)
            weighted = sum(e * p for e, (_, p) in zip(exps, both))
            scale = 1.0 / norm
            row_dot = jnp.sum(weighted, axis=0, keepdims=True) * scale
            total = jnp.zeros((strip, lanes), F32)
            for (kv, dst, j), e, (_, probs_grad) in zip(chunks, exps, both):
                probs = e * scale
                grad_scores = (probs * (probs_grad - row_dot)).astype(BF16)
                dkv = dot(grad_scores, ask) + dot(probs.astype(BF16), cot)
                dst[j, head] = dkv.astype(BF16)
                total = total + dot(grad_scores, kv, 0, 0)
        else:
            stats = (
                jnp.full((1, strip), -jnp.inf, F32),
                jnp.zeros((1, strip), F32),
                jnp.zeros((1, strip), F32),
            )
            for src, _ in sources:

                def gather(j, carry, src=src):
                    top, norm, weighted = carry
                    scores, probs_grad = products(src[j, head])
                    new = jnp.maximum(top, jnp.max(scores, axis=0, keepdims=True))
                    exps = jnp.exp(scores - new)
                    rescale = jnp.exp(top - new)
                    return (
                        new,
                        norm * rescale + jnp.sum(exps, axis=0, keepdims=True),
                        weighted * rescale + jnp.sum(exps * probs_grad, axis=0, keepdims=True),
                    )

                stats = lax.fori_loop(0, blocks, gather, stats)
            top, norm, weighted = stats
            scale = 1.0 / norm
            row_dot = weighted * scale
            total = jnp.zeros((strip, lanes), F32)
            for src, dst in sources:

                def spread(j, total, src=src, dst=dst):
                    kv = src[j, head]
                    scores, probs_grad = products(kv)
                    dkv, dq = finish(kv, scores, probs_grad, top, scale, row_dot)
                    dst[j, head] = dkv.astype(BF16)
                    return total + dq

                total = lax.fori_loop(0, blocks, spread, total)
        grad_query.append(total)
    dq_ref[...] = jnp.where(low, grad_query[1], grad_query[0]) * factor


def core_sum_kernel(own, received, *outs):
    for j, out in enumerate(outs):
        out[...] = (own[j].astype(F32) + received[j].astype(F32)).astype(BF16)


def project_kernel(n_col, per_sample, place, *refs):
    n_in = len(refs) - n_col
    *parts, dq_ref, gz_ref, input_weight, tiles = refs[:n_in]
    outs = refs[n_in:]
    col = place[0]
    part = col % per_sample
    total = sum(ref[...].astype(F32) for ref in parts)
    strip, lanes = dq_ref.shape
    half = lanes // 2
    channels = gz_ref.shape[1]
    low = lax.broadcasted_iota(jnp.int32, (strip, lanes), 1) < half
    dv = jnp.where(low, total[0], total[1])
    dk = pltpu.roll(jnp.where(low, total[1], total[0]), half, 1)
    dq = pltpu.roll(dq_ref[...], half, 1)
    grad = jnp.where(part == 0, gz_ref[...].astype(F32), 0.0)
    for kind, value in enumerate((dq, dk, dv)):
        first = pl.multiple_of(kind * channels + part * lanes, lanes)
        weight = input_weight[:, pl.ds(first, lanes)]
        grad = grad + dot(value.astype(BF16), weight, 1, 1)
    grad = grad.astype(BF16)
    for k, out in enumerate(outs):
        out[...] = dot(tiles[col ^ k], grad).astype(BF16)


def output_kernel(per_sample, place, *refs):
    *parts, out = refs
    samples, rows, cols, _ = out.shape
    padded = pad8(cols)
    sample = place[0] // per_sample
    for group in range(samples):
        total = sum(
            ref[...].astype(F32) for ref in parts[group * per_sample : (group + 1) * per_sample]
        )
        for i in range(rows):
            out[sample ^ group, i] = total[i * padded : i * padded + cols].astype(BF16)


def shards(
    pre_silu, out_grad, query_heads, key_heads, value_heads, conv_weight, out_weight, input_weight
):
    samples, rows, cols, channels = pre_silu.shape
    pairs, strip, head_dim = query_heads.shape
    n_row, n_col = lax.axis_size("row"), lax.axis_size("col")
    chips = n_row // 2
    per_sample = HEADS // pairs
    lanes = pairs * head_dim
    row, col = lax.axis_index("row"), lax.axis_index("col")
    core = row % 2
    sample = col // per_sample
    place = jnp.stack([col, core]).astype(jnp.int32)

    def to_col(array, k):
        return lax.ppermute(array, "col", [(i, i ^ k) for i in range(n_col)])

    def to_chip(array, k):
        return lax.ppermute(array, "row", [(i, i ^ (2 * k)) for i in range(n_row)])

    def to_core(array):
        return lax.ppermute(array, "row", [(i, i ^ 1) for i in range(n_row)])

    def to_next_chip(array):
        edge = [(i, i + 1) for i in range(1, n_row - 1, 2)]
        return lax.ppermute(array, "row", edge + [(j, i) for i, j in edge])

    both = jnp.stack([out_grad, pre_silu])
    payload = [
        lax.dynamic_index_in_dim(both, sample ^ group, 1, keepdims=False)
        for group in range(samples)
    ]
    received = [to_col(payload[k // per_sample], k) for k in range(1, n_col)]

    kv = jnp.stack(
        [
            jnp.concatenate([value_heads[0], key_heads[0]], -1),
            jnp.concatenate([key_heads[1], value_heads[1]], -1),
        ]
    )
    kv_own = jnp.stack([kv] + [to_chip(kv, k) for k in range(1, chips)])
    kv_other = to_core(kv_own)
    queries = jnp.concatenate([query_heads[1], query_heads[0]], -1)

    strip_grads = [payload[0][0]] + [piece[0] for piece in received]
    first_row = jnp.stack([piece[0] for piece in strip_grads])
    last_row = jnp.stack([piece[rows - 1] for piece in strip_grads])
    halo_core = to_core(jnp.where(core == 0, last_row, first_row))
    halo_chip = to_next_chip(jnp.where(core == 0, first_row, last_row))

    select = shift_selector(rows + 2, cols, n_col)
    middle = shift_selector(rows, cols, n_col)[1]
    padded = pad8(cols)
    block = jax.ShapeDtypeStruct((chips, pairs, strip, lanes), BF16)
    dkv_own, dkv_other, dq, grad_z = call(
        functools.partial(strip_kernel, n_col, per_sample),
        (
            block,
            block,
            jax.ShapeDtypeStruct((strip, lanes), F32),
            jax.ShapeDtypeStruct((strip, channels), BF16),
        ),
        (
            pltpu.VMEM((n_col, rows + 2, padded, channels), F32),
            pltpu.VMEM((n_col, rows, padded, channels), F32),
        ),
    )(
        place,
        out_grad,
        pre_silu,
        *received,
        halo_core,
        halo_chip,
        kv_own,
        kv_other,
        queries,
        conv_weight,
        out_weight,
        jnp.asarray(select, BF16),
        jnp.asarray(middle, BF16),
    )

    sums = call(
        core_sum_kernel,
        [jax.ShapeDtypeStruct((pairs, strip, lanes), BF16) for _ in range(chips)],
        scalars=0,
    )(dkv_own, to_core(dkv_other))
    parts = [sums[0]] + [to_chip(sums[k], k) for k in range(1, chips)]

    tile = jax.ShapeDtypeStruct((rows * padded, channels), BF16)
    cut = call(functools.partial(project_kernel, n_col, per_sample), [tile] * n_col)(
        place,
        *parts,
        dq,
        grad_z,
        input_weight,
        jnp.asarray(tile_selector(rows, cols, n_col), BF16),
    )
    returned = [cut[0]] + [to_col(cut[k], k) for k in range(1, n_col)]
    return call(
        functools.partial(output_kernel, per_sample),
        jax.ShapeDtypeStruct((samples, rows, cols, channels), BF16),
    )(place, *returned)


def solution(mesh):
    tile = P(None, "row", "col", None)
    heads = P("col", "row", None)
    return jax.shard_map(
        shards,
        mesh=mesh,
        in_specs=(tile, tile, heads, heads, heads, P(), P(), P()),
        out_specs=tile,
        check_vma=False,
    )
```

```python
import functools

import jax
import jax.numpy as jnp
import numpy as np
from jax import lax
from jax.experimental import pallas as pl
from jax.experimental.pallas import tpu as pltpu
from jax.sharding import PartitionSpec as P

HEADS = 4
VMEM_BYTES = 60 * 1024 * 1024
HELD_BYTES = 3 * 512 * 1024
UNROLLED_CHUNKS = 16
F32 = jnp.float32
BF16 = jnp.bfloat16


def dot(left, right, left_dim=1, right_dim=0):
    return lax.dot_general(
        left, right, (((left_dim,), (right_dim,)), ((), ())), preferred_element_type=F32
    )


def call(kernel, out_shape, scratch=(), scalars=1):
    whole = pl.BlockSpec(memory_space=pltpu.VMEM)
    scalar = pl.BlockSpec(memory_space=pltpu.SMEM)

    def run(*operands):
        operands = operands[:scalars] + tuple(
            pltpu.with_memory_space_constraint(operand, pltpu.VMEM)
            if operand.size * operand.dtype.itemsize <= HELD_BYTES
            else operand
            for operand in operands[scalars:]
        )
        return pl.pallas_call(
            kernel,
            out_shape=out_shape,
            in_specs=[scalar] * scalars + [whole] * (len(operands) - scalars),
            out_specs=jax.tree.map(lambda _: whole, out_shape),
            scratch_shapes=list(scratch),
            compiler_params=pltpu.CompilerParams(vmem_limit_bytes=VMEM_BYTES),
        )(*operands)

    return run


def held(shape, dtype):
    small = np.prod(shape) * np.dtype(dtype).itemsize <= HELD_BYTES
    return (pltpu.VMEM if small else jax.ShapeDtypeStruct)(shape, dtype)


def pad8(amount):
    return -(-amount // 8) * 8


def shift_selector(rows, cols, tiles):
    width, padded = tiles * cols, pad8(cols)
    select = np.zeros((3, rows, width, tiles, rows, padded), np.float32)
    for shift in (-1, 0, 1):
        for j in range(max(0, shift), min(width, width + shift)):
            tile, inner = divmod(j - shift, cols)
            for i in range(rows):
                select[shift + 1, i, j, tile, i, inner] = 1
    return select.reshape(3, rows * width, tiles * rows * padded)


def tile_selector(rows, cols, tiles):
    width, padded = tiles * cols, pad8(cols)
    select = np.zeros((tiles, rows, padded, rows, width), np.float32)
    for tile in range(tiles):
        for i in range(rows):
            for inner in range(cols):
                select[tile, i, inner, i, tile * cols + inner] = 1
    return select.reshape(tiles, rows * padded, rows * width)


def strip_kernel(n_col, per_sample, *refs):
    (place, own_grad, own_silu, *rest) = refs
    received, rest = rest[: n_col - 1], rest[n_col - 1 :]
    (
        halo_core,
        halo_chip,
        kv_own,
        kv_other,
        queries,
        conv_weight,
        out_weight,
        shifts,
        middle,
        dkv_own,
        dkv_other,
        dq_ref,
        gz_ref,
        grads,
        silus,
    ) = rest
    col, core = place[0], place[1]
    sample = col // per_sample
    rows, cols, channels = own_grad.shape[1:]
    width = n_col * cols
    strip = rows * width

    grads[...] = jnp.zeros_like(grads)
    silus[...] = jnp.zeros_like(silus)
    lower = jnp.where(core == 0, rows + 1, 0)
    upper = jnp.where(core == 0, 0, rows + 1)
    for k in range(n_col):
        tile = col ^ k
        for i in range(rows):
            grad = own_grad[sample, i] if k == 0 else received[k - 1][0, i]
            silu = own_silu[sample, i] if k == 0 else received[k - 1][1, i]
            grads[tile, i + 1, :cols] = grad.astype(F32)
            silus[tile, i, :cols] = silu.astype(F32)
        grads[tile, lower, :cols] = halo_core[k].astype(F32)
        grads[tile, upper, :cols] = halo_chip[k].astype(F32)
    flat = grads[...].reshape(-1, channels).astype(BF16)
    conv = jnp.zeros((strip, channels), F32)
    for b in (-1, 0, 1):
        shifted = dot(shifts[b + 1], flat)
        for a in (-1, 0, 1):
            window = shifted[(1 - a) * width : (1 - a) * width + strip].astype(BF16)
            conv = conv + dot(window, conv_weight[a + 1, b + 1], 1, 1)
    z = dot(middle[...], silus[...].reshape(-1, channels).astype(BF16))
    sigma = 1.0 / (1.0 + jnp.exp(-z))
    grad_z = (conv * sigma * (1.0 + z * (1.0 - sigma))).astype(BF16)
    gz_ref[...] = grad_z

    lanes = queries.shape[1]
    half = lanes // 2
    first = col % per_sample * lanes
    grad_out = dot(grad_z, out_weight[pl.ds(pl.multiple_of(first, lanes), lanes), :], 1, 1)
    grad_out = grad_out.astype(BF16)
    low = lax.broadcasted_iota(jnp.int32, (strip, lanes), 1) < half
    factor = half**-0.5
    query = queries[...] * jnp.asarray(factor, BF16)
    none = jnp.zeros_like(query)
    padded_query = (jnp.where(low, none, query), jnp.where(low, query, none))
    padded_grad = (jnp.where(low, grad_out, none), jnp.where(low, none, grad_out))

    blocks = kv_own.shape[0]
    sources = ((kv_own, dkv_own), (kv_other, dkv_other))
    small = 2 * blocks <= UNROLLED_CHUNKS
    grad_query = []
    for head in (0, 1):
        ask, cot = padded_query[head], padded_grad[head]

        def products(kv):
            return dot(kv, ask, 1, 1), dot(kv, cot, 1, 1)

        def finish(kv, scores, probs_grad, top, scale, row_dot):
            probs = jnp.exp(scores - top) * scale
            grad_scores = (probs * (probs_grad - row_dot)).astype(BF16)
            dkv = dot(grad_scores, ask) + dot(probs.astype(BF16), cot)
            return dkv, dot(grad_scores, kv, 0, 0)

        if small:
            chunks = [(src[j, head], dst, j) for src, dst in sources for j in range(blocks)]
            both = [products(kv) for kv, _, _ in chunks]
            top = functools.reduce(jnp.maximum, [s for s, _ in both])
            top = jnp.max(top, axis=0, keepdims=True)
            exps = [jnp.exp(s - top) for s, _ in both]
            norm = jnp.sum(sum(exps), axis=0, keepdims=True)
            weighted = sum(e * p for e, (_, p) in zip(exps, both))
            scale = 1.0 / norm
            row_dot = jnp.sum(weighted, axis=0, keepdims=True) * scale
            total = jnp.zeros((strip, lanes), F32)
            for (kv, dst, j), e, (_, probs_grad) in zip(chunks, exps, both):
                probs = e * scale
                grad_scores = (probs * (probs_grad - row_dot)).astype(BF16)
                dkv = dot(grad_scores, ask) + dot(probs.astype(BF16), cot)
                dst[j, head] = dkv.astype(BF16)
                total = total + dot(grad_scores, kv, 0, 0)
        else:
            stats = (
                jnp.full((1, strip), -jnp.inf, F32),
                jnp.zeros((1, strip), F32),
                jnp.zeros((1, strip), F32),
            )
            for src, _ in sources:

                def gather(j, carry, src=src):
                    top, norm, weighted = carry
                    scores, probs_grad = products(src[j, head])
                    new = jnp.maximum(top, jnp.max(scores, axis=0, keepdims=True))
                    exps = jnp.exp(scores - new)
                    rescale = jnp.exp(top - new)
                    return (
                        new,
                        norm * rescale + jnp.sum(exps, axis=0, keepdims=True),
                        weighted * rescale + jnp.sum(exps * probs_grad, axis=0, keepdims=True),
                    )

                stats = lax.fori_loop(0, blocks, gather, stats)
            top, norm, weighted = stats
            scale = 1.0 / norm
            row_dot = weighted * scale
            total = jnp.zeros((strip, lanes), F32)
            for src, dst in sources:

                def spread(j, total, src=src, dst=dst):
                    kv = src[j, head]
                    scores, probs_grad = products(kv)
                    dkv, dq = finish(kv, scores, probs_grad, top, scale, row_dot)
                    dst[j, head] = dkv.astype(BF16)
                    return total + dq

                total = lax.fori_loop(0, blocks, spread, total)
        grad_query.append(total)
    dq_ref[...] = jnp.where(low, grad_query[1], grad_query[0]) * factor


def core_sum_kernel(own, received, *outs):
    for j, out in enumerate(outs):
        out[...] = (own[j].astype(F32) + received[j].astype(F32)).astype(BF16)


def project_kernel(n_col, per_sample, place, *refs):
    n_in = len(refs) - n_col
    *parts, dq_ref, gz_ref, input_weight, tiles = refs[:n_in]
    outs = refs[n_in:]
    col = place[0]
    part = col % per_sample
    total = sum(ref[...].astype(F32) for ref in parts)
    strip, lanes = dq_ref.shape
    half = lanes // 2
    channels = gz_ref.shape[1]
    low = lax.broadcasted_iota(jnp.int32, (strip, lanes), 1) < half
    dv = jnp.where(low, total[0], total[1])
    dk = pltpu.roll(jnp.where(low, total[1], total[0]), half, 1)
    dq = pltpu.roll(dq_ref[...], half, 1)
    grad = jnp.where(part == 0, gz_ref[...].astype(F32), 0.0)
    for kind, value in enumerate((dq, dk, dv)):
        first = pl.multiple_of(kind * channels + part * lanes, lanes)
        weight = input_weight[:, pl.ds(first, lanes)]
        grad = grad + dot(value.astype(BF16), weight, 1, 1)
    grad = grad.astype(BF16)
    for k, out in enumerate(outs):
        out[...] = dot(tiles[col ^ k], grad).astype(BF16)


def output_kernel(per_sample, place, *refs):
    *parts, out = refs
    samples, rows, cols, _ = out.shape
    padded = pad8(cols)
    sample = place[0] // per_sample
    for group in range(samples):
        total = sum(
            ref[...].astype(F32) for ref in parts[group * per_sample : (group + 1) * per_sample]
        )
        for i in range(rows):
            out[sample ^ group, i] = total[i * padded : i * padded + cols].astype(BF16)


def shards(
    pre_silu, out_grad, query_heads, key_heads, value_heads, conv_weight, out_weight, input_weight
):
    samples, rows, cols, channels = pre_silu.shape
    pairs, strip, head_dim = query_heads.shape
    n_row, n_col = lax.axis_size("row"), lax.axis_size("col")
    chips = n_row // 2
    per_sample = HEADS // pairs
    lanes = pairs * head_dim
    row, col = lax.axis_index("row"), lax.axis_index("col")
    core = row % 2
    sample = col // per_sample
    place = jnp.stack([col, core]).astype(jnp.int32)

    def to_col(array, k):
        return lax.ppermute(array, "col", [(i, i ^ k) for i in range(n_col)])

    def to_chip(array, k):
        return lax.ppermute(array, "row", [(i, i ^ (2 * k)) for i in range(n_row)])

    def to_core(array):
        return lax.ppermute(array, "row", [(i, i ^ 1) for i in range(n_row)])

    def to_next_chip(array):
        edge = [(i, i + 1) for i in range(1, n_row - 1, 2)]
        return lax.ppermute(array, "row", edge + [(j, i) for i, j in edge])

    both = jnp.stack([out_grad, pre_silu])
    payload = [
        lax.dynamic_index_in_dim(both, sample ^ group, 1, keepdims=False)
        for group in range(samples)
    ]
    received = [to_col(payload[k // per_sample], k) for k in range(1, n_col)]

    kv = jnp.stack(
        [
            jnp.concatenate([value_heads[0], key_heads[0]], -1),
            jnp.concatenate([key_heads[1], value_heads[1]], -1),
        ]
    )
    kv_own = jnp.stack([kv] + [to_chip(kv, k) for k in range(1, chips)])
    kv_other = to_core(kv_own)
    queries = jnp.concatenate([query_heads[1], query_heads[0]], -1)

    strip_grads = [payload[0][0]] + [piece[0] for piece in received]
    first_row = jnp.stack([piece[0] for piece in strip_grads])
    last_row = jnp.stack([piece[rows - 1] for piece in strip_grads])
    halo_core = to_core(jnp.where(core == 0, last_row, first_row))
    halo_chip = to_next_chip(jnp.where(core == 0, first_row, last_row))

    select = shift_selector(rows + 2, cols, n_col)
    middle = shift_selector(rows, cols, n_col)[1]
    padded = pad8(cols)
    block = held((chips, pairs, strip, lanes), BF16)
    dkv_own, dkv_other, dq, grad_z = call(
        functools.partial(strip_kernel, n_col, per_sample),
        (
            block,
            block,
            held((strip, lanes), F32),
            held((strip, channels), BF16),
        ),
        (
            pltpu.VMEM((n_col, rows + 2, padded, channels), F32),
            pltpu.VMEM((n_col, rows, padded, channels), F32),
        ),
    )(
        place,
        out_grad,
        pre_silu,
        *received,
        halo_core,
        halo_chip,
        kv_own,
        kv_other,
        queries,
        conv_weight,
        out_weight,
        jnp.asarray(select, BF16),
        jnp.asarray(middle, BF16),
    )

    sums = call(
        core_sum_kernel,
        [held((pairs, strip, lanes), BF16) for _ in range(chips)],
        scalars=0,
    )(dkv_own, to_core(dkv_other))
    parts = [sums[0]] + [to_chip(sums[k], k) for k in range(1, chips)]

    tile = held((rows * padded, channels), BF16)
    cut = call(functools.partial(project_kernel, n_col, per_sample), [tile] * n_col)(
        place,
        *parts,
        dq,
        grad_z,
        input_weight,
        jnp.asarray(tile_selector(rows, cols, n_col), BF16),
    )
    returned = [cut[0]] + [to_col(cut[k], k) for k in range(1, n_col)]
    return call(
        functools.partial(output_kernel, per_sample),
        held((samples, rows, cols, channels), BF16),
    )(place, *returned)


def solution(mesh):
    tile = P(None, "row", "col", None)
    heads = P("col", "row", None)
    return jax.shard_map(
        shards,
        mesh=mesh,
        in_specs=(tile, tile, heads, heads, heads, P(), P(), P()),
        out_specs=tile,
        check_vma=False,
    )
```

```python
import functools

import jax
import jax.numpy as jnp
import numpy as np
from jax import lax
from jax.experimental import pallas as pl
from jax.experimental.pallas import tpu as pltpu
from jax.sharding import PartitionSpec as P

HEADS = 4
VMEM_BYTES = 32 * 1024 * 1024
HELD_BYTES = 3 * 512 * 1024
UNROLLED_CHUNKS = 16
F32 = jnp.float32
BF16 = jnp.bfloat16


def dot(left, right, left_dim=1, right_dim=0):
    return lax.dot_general(
        left, right, (((left_dim,), (right_dim,)), ((), ())), preferred_element_type=F32
    )


def call(kernel, out_shape, scratch=(), far=()):
    def run(*operands):
        specs = [pl.BlockSpec(memory_space=pltpu.VMEM)] * len(operands)
        operands = list(operands)
        for i, operand in enumerate(operands):
            if i in far:
                specs[i] = pl.BlockSpec(memory_space=pltpu.HBM)
                operands[i] = pltpu.with_memory_space_constraint(operand, pltpu.HBM)
            elif operand.size * operand.dtype.itemsize <= HELD_BYTES:
                operands[i] = pltpu.with_memory_space_constraint(operand, pltpu.VMEM)
        return pl.pallas_call(
            kernel,
            out_shape=out_shape,
            in_specs=specs,
            out_specs=jax.tree.map(lambda _: pl.BlockSpec(memory_space=pltpu.VMEM), out_shape),
            scratch_shapes=list(scratch),
            compiler_params=pltpu.CompilerParams(vmem_limit_bytes=VMEM_BYTES),
        )(*operands)

    return run


def held(shape, dtype):
    small = np.prod(shape) * np.dtype(dtype).itemsize <= HELD_BYTES
    return (pltpu.VMEM if small else jax.ShapeDtypeStruct)(shape, dtype)


def pad8(amount):
    return -(-amount // 8) * 8


def shift_selector(rows, cols, tiles):
    width, padded = tiles * cols, pad8(cols)
    select = np.zeros((3, rows, width, tiles, rows, padded), np.float32)
    for shift in (-1, 0, 1):
        for j in range(max(0, shift), min(width, width + shift)):
            tile, inner = divmod(j - shift, cols)
            for i in range(rows):
                select[shift + 1, i, j, tile, i, inner] = 1
    return select.reshape(3, rows * width, tiles * rows * padded)


def tile_selector(rows, cols, tiles):
    width, padded = tiles * cols, pad8(cols)
    select = np.zeros((tiles, rows, padded, rows, width), np.float32)
    for tile in range(tiles):
        for i in range(rows):
            for inner in range(cols):
                select[tile, i, inner, i, tile * cols + inner] = 1
    return select.reshape(tiles, rows * padded, rows * width)


def start_copies(pairs, sems):
    copies = [
        pltpu.make_async_copy(src, dst, sems.at[i]) for i, (src, dst) in enumerate(pairs)
    ]
    for copy in copies:
        copy.start()
    return copies


def pack_kernel(out_grad, pre_silu, queries, keys, values, tile, kv, query, q_ref, k_ref, v_ref, sems):
    copies = start_copies(
        [
            (values, v_ref),
            (keys, k_ref),
            (queries, q_ref),
            (out_grad, tile.at[0]),
            (pre_silu, tile.at[1]),
        ],
        sems,
    )

    def beside(left, right):
        return jnp.concatenate([left.astype(F32), right.astype(F32)], 0).T.astype(BF16)

    copies[0].wait()
    copies[1].wait()
    kv[0] = beside(v_ref[0], k_ref[0])
    kv[1] = beside(k_ref[1], v_ref[1])
    copies[2].wait()
    query[...] = beside(q_ref[1], q_ref[0]) * jnp.asarray(q_ref.shape[1] ** -0.5, BF16)
    copies[3].wait()
    copies[4].wait()


def middle_kernel(n_col, *refs):
    tiles, parts = refs[:n_col], refs[n_col:-4]
    query, to_core, to_chip, joined = refs[-4:]
    rows = tiles[0].shape[1]
    inner = jnp.where(lax.axis_index("row") % 2 == 1, rows - 1, 0)
    for k, tile in enumerate(tiles):
        to_core[k] = tile[0, inner]
        to_chip[k] = tile[0, rows - 1 - inner]
    heads = parts[0].shape[0]
    for j, part in enumerate(parts):
        for head in range(heads):
            joined[heads * j + head] = part[head]
    joined[heads * len(parts)] = query[...]


def strip_kernel(n_col, per_sample, *refs):
    tiles, rest = refs[:n_col], refs[n_col:]
    (
        halo_core,
        halo_chip,
        kv_sent,
        kv_kept,
        *far,
        dkv_sent,
        dkv_kept,
        dq_ref,
        gz_ref,
        grads,
        silus,
        conv_weight,
        out_weight,
        shifts,
        middle,
        sems,
    ) = rest
    copies = start_copies(list(zip(far, (shifts, middle, conv_weight, out_weight))), sems)
    col, core = lax.axis_index("col"), lax.axis_index("row") % 2
    sample = col // per_sample
    _, rows, cols, samples, channels = tiles[0].shape
    width = n_col * cols
    strip = rows * width
    chosen = lax.broadcasted_iota(jnp.int32, (cols, samples, channels), 1) == sample

    def pick(cells):
        return jnp.sum(jnp.where(chosen, cells.astype(F32), 0.0), axis=1)

    grads[...] = jnp.zeros_like(grads)
    silus[...] = jnp.zeros_like(silus)
    lower = jnp.where(core == 1, rows + 1, 0)
    upper = jnp.where(core == 1, 0, rows + 1)
    for k in range(n_col):
        tile = col ^ k
        for i in range(rows):
            grads[tile, i + 1, :cols] = pick(tiles[k][0, i])
            silus[tile, i, :cols] = pick(tiles[k][1, i])
        grads[tile, lower, :cols] = pick(halo_core[k])
        grads[tile, upper, :cols] = pick(halo_chip[k])
    lanes = kv_sent.shape[2]
    half = lanes // 2
    factor = half**-0.5
    low = lax.broadcasted_iota(jnp.int32, (strip, lanes), 1) < half
    query = kv_kept[kv_kept.shape[0] - 1]
    none = jnp.zeros_like(query)
    asked = (jnp.where(low, none, query), jnp.where(low, query, none))
    blocks = dkv_kept.shape[0]
    sources = ((kv_sent, dkv_sent), (kv_kept, dkv_kept))
    small = 2 * blocks <= UNROLLED_CHUNKS
    chunks = [(src, dst, j) for src, dst in sources for j in range(blocks)]

    def softmax(head):
        scores = [dot(src[2 * j + head], asked[head], 1, 1) for src, _, j in chunks]
        top = jnp.max(functools.reduce(jnp.maximum, scores), axis=0, keepdims=True)
        exps = [jnp.exp(s - top) for s in scores]
        scale = 1.0 / jnp.sum(sum(exps), axis=0, keepdims=True)
        return [e * scale for e in exps]

    if small:
        probs = [softmax(head) for head in (0, 1)]

    for copy in copies:
        copy.wait()
    flat = grads[...].reshape(-1, channels).astype(BF16)
    conv = jnp.zeros((strip, channels), F32)
    for b in (-1, 0, 1):
        shifted = dot(shifts[b + 1], flat)
        for a in (-1, 0, 1):
            window = shifted[(1 - a) * width : (1 - a) * width + strip].astype(BF16)
            conv = conv + dot(window, conv_weight[a + 1, b + 1], 1, 1)
    z = dot(middle[...], silus[...].reshape(-1, channels).astype(BF16))
    sigma = 1.0 / (1.0 + jnp.exp(-z))
    grad_z = (conv * sigma * (1.0 + z * (1.0 - sigma))).astype(BF16)
    gz_ref[...] = grad_z

    first = col % per_sample * lanes
    grad_out = dot(grad_z, out_weight[pl.ds(pl.multiple_of(first, lanes), lanes), :], 1, 1)
    grad_out = grad_out.astype(BF16)
    cotangent = (jnp.where(low, grad_out, none), jnp.where(low, none, grad_out))

    grad_query = []
    for head in (0, 1):
        ask, cot = asked[head], cotangent[head]

        def finish(kv, chunk_probs, probs_grad, row_dot):
            grad_scores = (chunk_probs * (probs_grad - row_dot)).astype(BF16)
            dkv = dot(grad_scores, ask) + dot(chunk_probs.astype(BF16), cot)
            return dkv.astype(BF16), dot(grad_scores, kv, 0, 0)

        total = jnp.zeros((strip, lanes), F32)
        if small:
            probs_grads = [dot(src[2 * j + head], cot, 1, 1) for src, _, j in chunks]
            weighted = sum(p * g for p, g in zip(probs[head], probs_grads))
            row_dot = jnp.sum(weighted, axis=0, keepdims=True)
            for (src, dst, j), p, g in zip(chunks, probs[head], probs_grads):
                dst[j, head], dq = finish(src[2 * j + head], p, g, row_dot)
                total = total + dq
        else:
            stats = (
                jnp.full((1, strip), -jnp.inf, F32),
                jnp.zeros((1, strip), F32),
                jnp.zeros((1, strip), F32),
            )
            for src, _ in sources:

                def gather(j, carry, src=src):
                    top, norm, weighted = carry
                    kv = src[2 * j + head]
                    scores = dot(kv, ask, 1, 1)
                    new = jnp.maximum(top, jnp.max(scores, axis=0, keepdims=True))
                    exps = jnp.exp(scores - new)
                    rescale = jnp.exp(top - new)
                    weights = jnp.sum(exps * dot(kv, cot, 1, 1), axis=0, keepdims=True)
                    return (
                        new,
                        norm * rescale + jnp.sum(exps, axis=0, keepdims=True),
                        weighted * rescale + weights,
                    )

                stats = lax.fori_loop(0, blocks, gather, stats)
            top, norm, weighted = stats
            scale = 1.0 / norm
            row_dot = weighted * scale
            for src, dst in sources:

                def spread(j, total, src=src, dst=dst):
                    kv = src[2 * j + head]
                    chunk_probs = jnp.exp(dot(kv, ask, 1, 1) - top) * scale
                    dst[j, head], dq = finish(kv, chunk_probs, dot(kv, cot, 1, 1), row_dot)
                    return total + dq

                total = lax.fori_loop(0, blocks, spread, total)
        grad_query.append(total)
    dq_ref[...] = jnp.where(low, grad_query[1], grad_query[0]) * factor


def core_sum_kernel(own, received, *outs):
    for j, out in enumerate(outs):
        out[...] = (own[j].astype(F32) + received[j].astype(F32)).astype(BF16)


def project_kernel(n_col, per_sample, *refs):
    n_in = len(refs) - n_col
    *parts, dq_ref, gz_ref, input_weight, tiles = refs[:n_in]
    outs = refs[n_in:]
    col = lax.axis_index("col")
    part = col % per_sample
    total = sum(ref[...].astype(F32) for ref in parts)
    strip, lanes = dq_ref.shape
    half = lanes // 2
    channels = gz_ref.shape[1]
    low = lax.broadcasted_iota(jnp.int32, (strip, lanes), 1) < half
    dv = jnp.where(low, total[0], total[1])
    dk = pltpu.roll(jnp.where(low, total[1], total[0]), half, 1)
    dq = pltpu.roll(dq_ref[...], half, 1)
    grad = jnp.where(part == 0, gz_ref[...].astype(F32), 0.0)
    for kind, value in enumerate((dq, dk, dv)):
        first = pl.multiple_of(kind * channels + part * lanes, lanes)
        weight = input_weight[:, pl.ds(first, lanes)]
        grad = grad + dot(value.astype(BF16), weight, 1, 1)
    grad = grad.astype(BF16)
    for k, out in enumerate(outs):
        out[...] = dot(tiles[col ^ k], grad).astype(BF16)


def output_kernel(per_sample, *refs):
    *parts, out = refs
    rows, cols, samples, channels = out.shape
    padded = pad8(cols)
    sample = lax.axis_index("col") // per_sample
    place = lax.broadcasted_iota(jnp.int32, (cols, samples, channels), 1)
    for i in range(rows):
        cells = jnp.zeros((cols, samples, channels), F32)
        for group in range(samples):
            total = sum(
                ref[...][i * padded : i * padded + cols].astype(F32)
                for ref in parts[group * per_sample : (group + 1) * per_sample]
            )
            cells = jnp.where(place == (sample ^ group), total[:, None, :], cells)
        out[i] = cells.astype(BF16)


def shards(
    pre_silu, out_grad, query_heads, key_heads, value_heads, conv_weight, out_weight, input_weight
):
    samples, rows, cols, channels = pre_silu.shape
    pairs, strip, head_dim = query_heads.shape
    n_row, n_col = lax.axis_size("row"), lax.axis_size("col")
    chips = n_row // 2
    per_sample = HEADS // pairs
    lanes = pairs * head_dim

    def to_col(array, k):
        pairs_of = [
            (r * n_col + c, (r ^ 1) * n_col + (c ^ k)) for r in range(n_row) for c in range(n_col)
        ]
        return lax.ppermute(array, ("row", "col"), pairs_of)

    def to_chip(array, k):
        return lax.ppermute(array, "row", [(i, i ^ (2 * k + 1)) for i in range(n_row)])

    def to_core(array):
        return lax.ppermute(array, "row", [(i, i ^ 1) for i in range(n_row)])

    def to_next_chip(array):
        edge = [(i, i + 3) for i in range(0, n_row - 2, 2)]
        return lax.ppermute(array, "row", edge + [(j, i) for i, j in edge])

    def cells(array):
        return jnp.transpose(array, (1, 2, 0, 3))

    def turned(array):
        return jnp.transpose(array, (0, 2, 1))

    saved = pltpu.VMEM((pairs, head_dim, strip), BF16)
    tile, kv, query = call(
        pack_kernel,
        (
            held((2, rows, cols, samples, channels), BF16),
            held((pairs, strip, lanes), BF16),
            held((strip, lanes), BF16),
        ),
        (saved, saved, saved, pltpu.SemaphoreType.DMA((5,))),
        range(5),
    )(cells(out_grad), cells(pre_silu), turned(query_heads), turned(key_heads), turned(value_heads))
    kv_parts = [kv] + [to_chip(kv, k) for k in range(1, chips)]
    tiles = [to_col(tile, k) for k in range(n_col)]

    rim = held((n_col, cols, samples, channels), BF16)
    rim_core, rim_chip, kv_sent = call(
        functools.partial(middle_kernel, n_col),
        (rim, rim, held((pairs * chips + 1, strip, lanes), BF16)),
    )(*tiles, *kv_parts, query)
    halo_core, halo_chip, kv_kept = to_core(rim_core), to_next_chip(rim_chip), to_core(kv_sent)

    padded = pad8(cols)
    shifts = jnp.asarray(shift_selector(rows + 2, cols, n_col), BF16)
    middle = jnp.asarray(shift_selector(rows, cols, n_col)[1], BF16)
    far = (shifts, middle, conv_weight, out_weight)
    block = held((chips, pairs, strip, lanes), BF16)
    dkv_sent, dkv_kept, dq, grad_z = call(
        functools.partial(strip_kernel, n_col, per_sample),
        (block, block, held((strip, lanes), F32), held((strip, channels), BF16)),
        (
            pltpu.VMEM((n_col, rows + 2, padded, channels), F32),
            pltpu.VMEM((n_col, rows, padded, channels), F32),
            pltpu.VMEM(conv_weight.shape, BF16),
            pltpu.VMEM(out_weight.shape, BF16),
            pltpu.VMEM(shifts.shape, BF16),
            pltpu.VMEM(middle.shape, BF16),
            pltpu.SemaphoreType.DMA((4,)),
        ),
        range(n_col + 4, n_col + 8),
    )(*tiles, halo_core, halo_chip, kv_sent, kv_kept, *far)

    sums = call(core_sum_kernel, [held((pairs, strip, lanes), BF16) for _ in range(chips)])(
        dkv_kept, to_core(dkv_sent)
    )
    parts = [sums[0]] + [to_chip(sums[k], k) for k in range(1, chips)]

    cut = call(
        functools.partial(project_kernel, n_col, per_sample),
        [held((rows * padded, channels), BF16)] * n_col,
    )(*parts, dq, grad_z, input_weight, jnp.asarray(tile_selector(rows, cols, n_col), BF16))
    grad_input = call(
        functools.partial(output_kernel, per_sample), held((rows, cols, samples, channels), BF16)
    )(*[to_col(cut[k], k) for k in range(n_col)])
    return jnp.transpose(grad_input, (2, 0, 1, 3))


def solution(mesh):
    tile = P(None, "row", "col", None)
    heads = P("col", "row", None)
    return jax.shard_map(
        shards,
        mesh=mesh,
        in_specs=(tile, tile, heads, heads, heads, P(), P(), P()),
        out_specs=tile,
        check_vma=False,
    )
```

```python
import functools

import jax
import jax.numpy as jnp
import numpy as np
from jax import lax
from jax.experimental import pallas as pl
from jax.experimental.pallas import tpu as pltpu
from jax.sharding import PartitionSpec as P

HEADS = 4
VMEM_BYTES = 32 * 1024 * 1024
HELD_BYTES = 3 * 512 * 1024
UNROLLED_CHUNKS = 16
F32 = jnp.float32
BF16 = jnp.bfloat16


def dot(left, right, left_dim=1, right_dim=0):
    return lax.dot_general(
        left, right, (((left_dim,), (right_dim,)), ((), ())), preferred_element_type=F32
    )


def call(kernel, out_shape, scratch=(), far=()):
    def run(*operands):
        specs = [pl.BlockSpec(memory_space=pltpu.VMEM)] * len(operands)
        operands = list(operands)
        for i, operand in enumerate(operands):
            if i in far:
                specs[i] = pl.BlockSpec(memory_space=pltpu.HBM)
                operands[i] = pltpu.with_memory_space_constraint(operand, pltpu.HBM)
            elif operand.size * operand.dtype.itemsize <= HELD_BYTES:
                operands[i] = pltpu.with_memory_space_constraint(operand, pltpu.VMEM)
        return pl.pallas_call(
            kernel,
            out_shape=out_shape,
            in_specs=specs,
            out_specs=jax.tree.map(lambda _: pl.BlockSpec(memory_space=pltpu.VMEM), out_shape),
            scratch_shapes=list(scratch),
            compiler_params=pltpu.CompilerParams(vmem_limit_bytes=VMEM_BYTES),
        )(*operands)

    return run


def held(shape, dtype):
    small = np.prod(shape) * np.dtype(dtype).itemsize <= HELD_BYTES
    return (pltpu.VMEM if small else jax.ShapeDtypeStruct)(shape, dtype)


def pad8(amount):
    return -(-amount // 8) * 8


def shift_selector(rows, cols, tiles):
    width, padded = tiles * cols, pad8(cols)
    select = np.zeros((3, rows, width, tiles, rows, padded), np.float32)
    for shift in (-1, 0, 1):
        for j in range(max(0, shift), min(width, width + shift)):
            tile, inner = divmod(j - shift, cols)
            for i in range(rows):
                select[shift + 1, i, j, tile, i, inner] = 1
    return select.reshape(3, rows * width, tiles * rows * padded)


def tile_selector(rows, cols, tiles):
    width, padded = tiles * cols, pad8(cols)
    select = np.zeros((tiles, rows, padded, rows, width), np.float32)
    for tile in range(tiles):
        for i in range(rows):
            for inner in range(cols):
                select[tile, i, inner, i, tile * cols + inner] = 1
    return select.reshape(tiles, rows * padded, rows * width)


def start_copies(pairs, sems):
    copies = [
        pltpu.make_async_copy(src, dst, sems.at[i]) for i, (src, dst) in enumerate(pairs)
    ]
    for copy in copies:
        copy.start()
    return copies


def pack_kernel(
    out_grad, pre_silu, queries, keys, values, tile, kv, query, q_ref, k_ref, v_ref, sems
):
    copies = start_copies(
        [
            (values, v_ref),
            (keys, k_ref),
            (queries, q_ref),
            (out_grad, tile.at[0]),
            (pre_silu, tile.at[1]),
        ],
        sems,
    )

    def beside(left, right):
        return jnp.concatenate([left.astype(F32), right.astype(F32)], 0).T.astype(BF16)

    copies[0].wait()
    copies[1].wait()
    kv[0] = beside(v_ref[0], k_ref[0])
    kv[1] = beside(k_ref[1], v_ref[1])
    copies[2].wait()
    query[...] = beside(q_ref[1], q_ref[0]) * jnp.asarray(q_ref.shape[1] ** -0.5, BF16)
    copies[3].wait()
    copies[4].wait()


def rim_kernel(*refs):
    *tiles, to_core, to_chip = refs
    rows = tiles[0].shape[1]
    inner = jnp.where(lax.axis_index("row") % 2 == 1, rows - 1, 0)
    for k, tile in enumerate(tiles):
        to_core[k] = tile[0, inner]
        to_chip[k] = tile[0, rows - 1 - inner]


def join_kernel(*refs):
    *parts, out = refs
    first = 0
    for part in parts:
        for j in range(part.shape[0]):
            out[first + j] = part[j]
        first += part.shape[0]


def conv_kernel(n_col, per_sample, *refs):
    tiles, rest = refs[:n_col], refs[n_col:]
    (
        halo_core,
        halo_chip,
        *far,
        gz_ref,
        go_ref,
        grads,
        silus,
        shifts,
        middle,
        conv_weight,
        out_weight,
        sems,
    ) = rest
    copies = start_copies(list(zip(far, (shifts, middle, conv_weight, out_weight))), sems)
    col, core = lax.axis_index("col"), lax.axis_index("row") % 2
    sample = col // per_sample
    _, rows, cols, samples, channels = tiles[0].shape
    width = n_col * cols
    strip = rows * width
    chosen = lax.broadcasted_iota(jnp.int32, (cols, samples, channels), 1) == sample

    def pick(cells):
        return jnp.sum(jnp.where(chosen, cells.astype(F32), 0.0), axis=1)

    grads[...] = jnp.zeros_like(grads)
    silus[...] = jnp.zeros_like(silus)
    lower = jnp.where(core == 1, rows + 1, 0)
    upper = jnp.where(core == 1, 0, rows + 1)
    for k in range(n_col):
        tile = col ^ k
        for i in range(rows):
            grads[tile, i + 1, :cols] = pick(tiles[k][0, i])
            silus[tile, i, :cols] = pick(tiles[k][1, i])
        grads[tile, lower, :cols] = pick(halo_core[k])
        grads[tile, upper, :cols] = pick(halo_chip[k])
    for copy in copies:
        copy.wait()
    flat = grads[...].reshape(-1, channels).astype(BF16)
    conv = jnp.zeros((strip, channels), F32)
    for b in (-1, 0, 1):
        shifted = dot(shifts[b + 1], flat)
        for a in (-1, 0, 1):
            window = shifted[(1 - a) * width : (1 - a) * width + strip].astype(BF16)
            conv = conv + dot(window, conv_weight[a + 1, b + 1], 1, 1)
    z = dot(middle[...], silus[...].reshape(-1, channels).astype(BF16))
    sigma = 1.0 / (1.0 + jnp.exp(-z))
    grad_z = (conv * sigma * (1.0 + z * (1.0 - sigma))).astype(BF16)
    gz_ref[...] = grad_z
    lanes = go_ref.shape[1]
    first = pl.multiple_of(col % per_sample * lanes, lanes)
    go_ref[...] = dot(grad_z, out_weight[pl.ds(first, lanes), :], 1, 1).astype(BF16)


def attention_kernel(offsets, kv_sent, kv_kept, go_ref, dkv_sent, dkv_kept, dq_ref):
    strip, lanes = go_ref.shape
    half = lanes // 2
    factor = half**-0.5
    low = lax.broadcasted_iota(jnp.int32, (strip, lanes), 1) < half
    query, grad_out = kv_kept[kv_kept.shape[0] - 1], go_ref[...]
    none = jnp.zeros_like(query)
    asked = (jnp.where(low, none, query), jnp.where(low, query, none))
    cotangent = (jnp.where(low, grad_out, none), jnp.where(low, none, grad_out))
    chunks = []
    for j, offset in enumerate(offsets):
        even = offset != 0 and offset.bit_count() % 2 == 0
        chunks.append((kv_sent, dkv_kept if even else dkv_sent, j, offset))
        chunks.append((kv_kept, dkv_sent if even else dkv_kept, j, offset))

    grad_query = []
    for head in (0, 1):
        ask, cot = asked[head], cotangent[head]

        def finish(kv, probs, probs_grad, row_dot):
            grad_scores = (probs * (probs_grad - row_dot)).astype(BF16)
            dkv = dot(grad_scores, ask) + dot(probs.astype(BF16), cot)
            return dkv.astype(BF16), dot(grad_scores, kv, 0, 0)

        total = jnp.zeros((strip, lanes), F32)
        if len(chunks) <= UNROLLED_CHUNKS:
            scores = [dot(src[2 * j + head], ask, 1, 1) for src, _, j, _ in chunks]
            top = jnp.max(functools.reduce(jnp.maximum, scores), axis=0, keepdims=True)
            exps = [jnp.exp(s - top) for s in scores]
            scale = 1.0 / jnp.sum(sum(exps), axis=0, keepdims=True)
            probs = [e * scale for e in exps]
            probs_grads = [dot(src[2 * j + head], cot, 1, 1) for src, _, j, _ in chunks]
            weighted = sum(p * g for p, g in zip(probs, probs_grads))
            row_dot = jnp.sum(weighted, axis=0, keepdims=True)
            for (src, dst, j, offset), p, g in zip(chunks, probs, probs_grads):
                dst[offset, head], dq = finish(src[2 * j + head], p, g, row_dot)
                total = total + dq
        else:

            def gather(kv, carry):
                top, norm, weighted = carry
                scores = dot(kv, ask, 1, 1)
                new = jnp.maximum(top, jnp.max(scores, axis=0, keepdims=True))
                exps = jnp.exp(scores - new)
                rescale = jnp.exp(top - new)
                weights = jnp.sum(exps * dot(kv, cot, 1, 1), axis=0, keepdims=True)
                return (
                    new,
                    norm * rescale + jnp.sum(exps, axis=0, keepdims=True),
                    weighted * rescale + weights,
                )

            zero = jnp.zeros((1, strip), F32)
            stats = (jnp.full((1, strip), -jnp.inf, F32), zero, zero)
            for src in (kv_sent, kv_kept):
                stats = lax.fori_loop(
                    0,
                    len(offsets),
                    lambda j, carry, src=src: gather(src[2 * j + head], carry),
                    stats,
                )
            top, norm, weighted = stats
            scale = 1.0 / norm
            for src, dst, j, offset in chunks:
                kv = src[2 * j + head]
                probs = jnp.exp(dot(kv, ask, 1, 1) - top) * scale
                dst[offset, head], dq = finish(kv, probs, dot(kv, cot, 1, 1), weighted * scale)
                total = total + dq
        grad_query.append(total)
    dq_ref[...] = jnp.where(low, grad_query[1], grad_query[0]) * factor


def core_sum_kernel(own, received, *outs):
    for j, out in enumerate(outs):
        out[...] = (own[j].astype(F32) + received[j].astype(F32)).astype(BF16)


def project_kernel(n_col, per_sample, *refs):
    n_in = len(refs) - n_col
    *parts, dq_ref, gz_ref, input_weight, tiles = refs[:n_in]
    outs = refs[n_in:]
    col = lax.axis_index("col")
    part = col % per_sample
    total = sum(ref[...].astype(F32) for ref in parts)
    strip, lanes = dq_ref.shape
    half = lanes // 2
    channels = gz_ref.shape[1]
    low = lax.broadcasted_iota(jnp.int32, (strip, lanes), 1) < half
    dv = jnp.where(low, total[0], total[1])
    dk = pltpu.roll(jnp.where(low, total[1], total[0]), half, 1)
    dq = pltpu.roll(dq_ref[...], half, 1)
    grad = jnp.where(part == 0, gz_ref[...].astype(F32), 0.0)
    for kind, value in enumerate((dq, dk, dv)):
        first = pl.multiple_of(kind * channels + part * lanes, lanes)
        weight = input_weight[:, pl.ds(first, lanes)]
        grad = grad + dot(value.astype(BF16), weight, 1, 1)
    grad = grad.astype(BF16)
    for k, out in enumerate(outs):
        out[...] = dot(tiles[col ^ k], grad).astype(BF16)


def output_kernel(per_sample, *refs):
    *parts, out = refs
    rows, cols, samples, channels = out.shape
    padded = pad8(cols)
    sample = lax.axis_index("col") // per_sample
    place = lax.broadcasted_iota(jnp.int32, (cols, samples, channels), 1)
    for i in range(rows):
        cells = jnp.zeros((cols, samples, channels), F32)
        for group in range(samples):
            total = sum(
                ref[...][i * padded : i * padded + cols].astype(F32)
                for ref in parts[group * per_sample : (group + 1) * per_sample]
            )
            cells = jnp.where(place == (sample ^ group), total[:, None, :], cells)
        out[i] = cells.astype(BF16)


def shards(
    pre_silu, out_grad, query_heads, key_heads, value_heads, conv_weight, out_weight, input_weight
):
    samples, rows, cols, channels = pre_silu.shape
    pairs, strip, head_dim = query_heads.shape
    n_row, n_col = lax.axis_size("row"), lax.axis_size("col")
    chips = n_row // 2
    per_sample = HEADS // pairs
    lanes = pairs * head_dim

    def to_col(array, k):
        pairs_of = [
            (r * n_col + c, (r ^ 1) * n_col + (c ^ k)) for r in range(n_row) for c in range(n_col)
        ]
        return lax.ppermute(array, ("row", "col"), pairs_of)

    def to_chip(array, k):
        return lax.ppermute(array, "row", [(i, i ^ (2 * k + 1)) for i in range(n_row)])

    def to_core(array):
        return lax.ppermute(array, "row", [(i, i ^ 1) for i in range(n_row)])

    def to_next_chip(array):
        edge = [(i, i + 3) for i in range(0, n_row - 2, 2)]
        return lax.ppermute(array, "row", edge + [(j, i) for i, j in edge])

    def cells(array):
        return jnp.transpose(array, (1, 2, 0, 3))

    def turned(array):
        return jnp.transpose(array, (0, 2, 1))

    saved = pltpu.VMEM((pairs, head_dim, strip), BF16)
    tile, kv, query = call(
        pack_kernel,
        (
            held((2, rows, cols, samples, channels), BF16),
            held((pairs, strip, lanes), BF16),
            held((strip, lanes), BF16),
        ),
        (saved, saved, saved, pltpu.SemaphoreType.DMA((5,))),
        range(5),
    )(cells(out_grad), cells(pre_silu), turned(query_heads), turned(key_heads), turned(value_heads))
    tiles = [to_col(tile, k) for k in range(n_col)]

    def doubled(joined, received, *last):
        parts = (joined, received, *last)
        return call(join_kernel, held((sum(p.shape[0] for p in parts), strip, lanes), BF16))(*parts)

    distances = [chips >> (i + 1) for i in range(chips.bit_length() - 1)]
    offsets = [0]
    for distance in distances:
        offsets = offsets + [offset + distance for offset in offsets]
    tiles, received = lax.optimization_barrier((tiles, to_chip(kv, distances[0])))
    joined = doubled(kv, received)

    rim = held((n_col, cols, samples, channels), BF16)
    rim_core, rim_chip = call(rim_kernel, (rim, rim))(*tiles)
    halo_chip, halo_core = to_next_chip(rim_chip), to_core(rim_core)
    for distance in distances[1:-1]:
        joined = doubled(joined, to_chip(joined, distance))
    halo_chip, halo_core, received = lax.optimization_barrier(
        (halo_chip, halo_core, to_chip(joined, distances[-1]))
    )
    joined = doubled(joined, received, query[None])
    received = to_core(joined)

    padded = pad8(cols)
    shifts = jnp.asarray(shift_selector(rows + 2, cols, n_col), BF16)
    middle = jnp.asarray(shift_selector(rows, cols, n_col)[1], BF16)
    far = (shifts, middle, conv_weight, out_weight)
    grad_z, grad_out = call(
        functools.partial(conv_kernel, n_col, per_sample),
        (held((strip, channels), BF16), held((strip, lanes), BF16)),
        (
            pltpu.VMEM((n_col, rows + 2, padded, channels), F32),
            pltpu.VMEM((n_col, rows, padded, channels), F32),
            *(pltpu.VMEM(array.shape, BF16) for array in far),
            pltpu.SemaphoreType.DMA((len(far),)),
        ),
        range(n_col + 2, n_col + 2 + len(far)),
    )(*tiles, halo_core, halo_chip, *far)

    block = held((chips, pairs, strip, lanes), BF16)
    dkv_sent, dkv_kept, dq = call(
        functools.partial(attention_kernel, offsets), (block, block, held((strip, lanes), F32))
    )(joined, received, grad_out)

    sums = call(core_sum_kernel, [held((pairs, strip, lanes), BF16) for _ in range(chips)])(
        dkv_kept, to_core(dkv_sent)
    )
    parts = [sums[0]] + [to_chip(sums[k], k) for k in range(1, chips)]

    cut = call(
        functools.partial(project_kernel, n_col, per_sample),
        [held((rows * padded, channels), BF16)] * n_col,
    )(*parts, dq, grad_z, input_weight, jnp.asarray(tile_selector(rows, cols, n_col), BF16))
    grad_input = call(
        functools.partial(output_kernel, per_sample), held((rows, cols, samples, channels), BF16)
    )(*[to_col(cut[k], k) for k in range(n_col)])
    return jnp.transpose(grad_input, (2, 0, 1, 3))


def solution(mesh):
    tile = P(None, "row", "col", None)
    heads = P("col", "row", None)
    return jax.shard_map(
        shards,
        mesh=mesh,
        in_specs=(tile, tile, heads, heads, heads, P(), P(), P()),
        out_specs=tile,
        check_vma=False,
    )
```

```python
import functools

import jax
import jax.numpy as jnp
import numpy as np
from jax import lax
from jax.experimental import pallas as pl
from jax.experimental.pallas import tpu as pltpu
from jax.sharding import PartitionSpec as P

HEADS = 4
VMEM_BYTES = 32 * 1024 * 1024
HELD_BYTES = 3 * 512 * 1024
UNROLLED_CHUNKS = 16
F32 = jnp.float32
BF16 = jnp.bfloat16


def dot(left, right, left_dim=1, right_dim=0):
    return lax.dot_general(
        left, right, (((left_dim,), (right_dim,)), ((), ())), preferred_element_type=F32
    )


def call(kernel, out_shape, scratch=(), far=()):
    def run(*operands):
        specs = [pl.BlockSpec(memory_space=pltpu.VMEM)] * len(operands)
        operands = list(operands)
        for i, operand in enumerate(operands):
            if i in far:
                specs[i] = pl.BlockSpec(memory_space=pltpu.HBM)
                operands[i] = pltpu.with_memory_space_constraint(operand, pltpu.HBM)
            elif operand.size * operand.dtype.itemsize <= HELD_BYTES:
                operands[i] = pltpu.with_memory_space_constraint(operand, pltpu.VMEM)
        return pl.pallas_call(
            kernel,
            out_shape=out_shape,
            in_specs=specs,
            out_specs=jax.tree.map(lambda _: pl.BlockSpec(memory_space=pltpu.VMEM), out_shape),
            scratch_shapes=list(scratch),
            compiler_params=pltpu.CompilerParams(vmem_limit_bytes=VMEM_BYTES),
        )(*operands)

    return run


def held(shape, dtype):
    small = np.prod(shape) * np.dtype(dtype).itemsize <= HELD_BYTES
    return (pltpu.VMEM if small else jax.ShapeDtypeStruct)(shape, dtype)


def pad8(amount):
    return -(-amount // 8) * 8


def shift_selector(rows, cols, tiles):
    width, padded = tiles * cols, pad8(cols)
    select = np.zeros((3, rows, width, tiles, rows, padded), np.float32)
    for shift in (-1, 0, 1):
        for j in range(max(0, shift), min(width, width + shift)):
            tile, inner = divmod(j - shift, cols)
            for i in range(rows):
                select[shift + 1, i, j, tile, i, inner] = 1
    return select.reshape(3, rows * width, tiles * rows * padded)


def tile_selector(rows, cols, tiles):
    width, padded = tiles * cols, pad8(cols)
    select = np.zeros((tiles, rows, padded, rows, width), np.float32)
    for tile in range(tiles):
        for i in range(rows):
            for inner in range(cols):
                select[tile, i, inner, i, tile * cols + inner] = 1
    return select.reshape(tiles, rows * padded, rows * width)


def start_copies(pairs, sems):
    copies = [
        pltpu.make_async_copy(src, dst, sems.at[i]) for i, (src, dst) in enumerate(pairs)
    ]
    for copy in copies:
        copy.start()
    return copies


def pack_kernel(
    out_grad, pre_silu, queries, keys, values, tile, kv, query, q_ref, k_ref, v_ref, sems
):
    copies = start_copies(
        [
            (values, v_ref),
            (keys, k_ref),
            (queries, q_ref),
            (out_grad, tile.at[0]),
            (pre_silu, tile.at[1]),
        ],
        sems,
    )

    def beside(left, right):
        return jnp.concatenate([left.astype(F32), right.astype(F32)], 0).T.astype(BF16)

    copies[0].wait()
    copies[1].wait()
    kv[0] = beside(v_ref[0], k_ref[0])
    kv[1] = beside(k_ref[1], v_ref[1])
    copies[2].wait()
    query[...] = beside(q_ref[1], q_ref[0]) * jnp.asarray(q_ref.shape[1] ** -0.5, BF16)
    copies[3].wait()
    copies[4].wait()


def rim_kernel(*refs):
    *tiles, to_core, to_chip = refs
    rows = tiles[0].shape[1]
    inner = jnp.where(lax.axis_index("row") % 2 == 1, rows - 1, 0)
    for k, tile in enumerate(tiles):
        to_core[k] = tile[0, inner]
        to_chip[k] = tile[0, rows - 1 - inner]


def join_kernel(*refs):
    *parts, out = refs
    first = 0
    for part in parts:
        for j in range(part.shape[0]):
            out[first + j] = part[j]
        first += part.shape[0]


def load_kernel(*refs):
    *copied, sems = refs
    half = len(copied) // 2
    for copy in start_copies(list(zip(copied[:half], copied[half:])), sems):
        copy.wait()


def pick(cells, sample):
    place = lax.broadcasted_iota(jnp.int32, cells.shape, 1)
    return jnp.sum(jnp.where(place == sample, cells.astype(F32), 0.0), axis=1)


def conv_kernel(n_col, per_sample, *refs):
    tiles, (shifts, conv_weight, conv_ref, gate_ref, grads, silus) = refs[:n_col], refs[n_col:]
    col = lax.axis_index("col")
    sample = col // per_sample
    _, rows, cols, _, channels = tiles[0].shape
    width = n_col * cols
    grads[...] = jnp.zeros_like(grads)
    silus[...] = jnp.zeros_like(silus)
    for k in range(n_col):
        for i in range(rows):
            grads[col ^ k, i, :cols] = pick(tiles[k][0, i], sample)
            silus[col ^ k, i, :cols] = pick(tiles[k][1, i], sample)
    flat = grads[...].reshape(-1, channels).astype(BF16)
    none = jnp.zeros((width, channels), F32)
    conv = jnp.zeros((rows * width, channels), F32)
    for b in (-1, 0, 1):
        here = dot(shifts[b + 1], flat)
        above = jnp.concatenate([none, here[:-width]], 0)
        below = jnp.concatenate([here[width:], none], 0)
        for a, window in ((-1, below), (0, here), (1, above)):
            conv = conv + dot(window.astype(BF16), conv_weight[a + 1, b + 1], 1, 1)
    conv_ref[...] = conv
    z = dot(shifts[1], silus[...].reshape(-1, channels).astype(BF16))
    sigma = 1.0 / (1.0 + jnp.exp(-z))
    gate_ref[...] = sigma * (1.0 + z * (1.0 - sigma))


def rim_conv_kernel(per_sample, *refs):
    halo_core, halo_chip, conv, gate, shifts, conv_weight, out_weight, gz_ref, go_ref, rims = refs
    col, core = lax.axis_index("col"), lax.axis_index("row") % 2
    sample = col // per_sample
    n_col, cols, _, channels = halo_core.shape
    width = n_col * cols
    rims[...] = jnp.zeros_like(rims)
    for k in range(n_col):
        rims[core, col ^ k, :cols] = pick(halo_core[k], sample)
        rims[1 - core, col ^ k, :cols] = pick(halo_chip[k], sample)
    edges = []
    for side, a in ((0, 1), (1, -1)):
        flat = rims[side].reshape(-1, channels).astype(BF16)
        edge = jnp.zeros((width, channels), F32)
        for b in (-1, 0, 1):
            window = dot(shifts[b + 1], flat).astype(BF16)
            edge = edge + dot(window, conv_weight[a + 1, b + 1], 1, 1)
        edges.append(edge)
    between = jnp.zeros((conv.shape[0] - 2 * width, channels), F32)
    total = conv[...] + jnp.concatenate([edges[0], between, edges[1]], 0)
    grad_z = (total * gate[...]).astype(BF16)
    gz_ref[...] = grad_z
    lanes = go_ref.shape[1]
    first = pl.multiple_of(col % per_sample * lanes, lanes)
    go_ref[...] = dot(grad_z, out_weight[pl.ds(first, lanes), :], 1, 1).astype(BF16)


def attention_kernel(offsets, kv_sent, kv_kept, go_ref, dkv_sent, dkv_kept, dq_ref):
    strip, lanes = go_ref.shape
    half = lanes // 2
    factor = half**-0.5
    low = lax.broadcasted_iota(jnp.int32, (strip, lanes), 1) < half
    query, grad_out = kv_kept[kv_kept.shape[0] - 1], go_ref[...]
    none = jnp.zeros_like(query)
    asked = (jnp.where(low, none, query), jnp.where(low, query, none))
    cotangent = (jnp.where(low, grad_out, none), jnp.where(low, none, grad_out))
    chunks = []
    for j, offset in enumerate(offsets):
        even = offset != 0 and offset.bit_count() % 2 == 0
        chunks.append((kv_sent, dkv_kept if even else dkv_sent, j, offset))
        chunks.append((kv_kept, dkv_sent if even else dkv_kept, j, offset))

    grad_query = []
    for head in (0, 1):
        ask, cot = asked[head], cotangent[head]

        def finish(kv, probs, probs_grad, row_dot):
            grad_scores = (probs * (probs_grad - row_dot)).astype(BF16)
            dkv = dot(grad_scores, ask) + dot(probs.astype(BF16), cot)
            return dkv.astype(BF16), dot(grad_scores, kv, 0, 0)

        total = jnp.zeros((strip, lanes), F32)
        if len(chunks) <= UNROLLED_CHUNKS:
            scores = [dot(src[2 * j + head], ask, 1, 1) for src, _, j, _ in chunks]
            top = jnp.max(functools.reduce(jnp.maximum, scores), axis=0, keepdims=True)
            exps = [jnp.exp(s - top) for s in scores]
            scale = 1.0 / jnp.sum(sum(exps), axis=0, keepdims=True)
            probs = [e * scale for e in exps]
            probs_grads = [dot(src[2 * j + head], cot, 1, 1) for src, _, j, _ in chunks]
            weighted = sum(p * g for p, g in zip(probs, probs_grads))
            row_dot = jnp.sum(weighted, axis=0, keepdims=True)
            for (src, dst, j, offset), p, g in zip(chunks, probs, probs_grads):
                dst[offset, head], dq = finish(src[2 * j + head], p, g, row_dot)
                total = total + dq
        else:

            def gather(kv, carry):
                top, norm, weighted = carry
                scores = dot(kv, ask, 1, 1)
                new = jnp.maximum(top, jnp.max(scores, axis=0, keepdims=True))
                exps = jnp.exp(scores - new)
                rescale = jnp.exp(top - new)
                weights = jnp.sum(exps * dot(kv, cot, 1, 1), axis=0, keepdims=True)
                return (
                    new,
                    norm * rescale + jnp.sum(exps, axis=0, keepdims=True),
                    weighted * rescale + weights,
                )

            zero = jnp.zeros((1, strip), F32)
            stats = (jnp.full((1, strip), -jnp.inf, F32), zero, zero)
            for src in (kv_sent, kv_kept):
                stats = lax.fori_loop(
                    0,
                    len(offsets),
                    lambda j, carry, src=src: gather(src[2 * j + head], carry),
                    stats,
                )
            top, norm, weighted = stats
            scale = 1.0 / norm
            for src, dst, j, offset in chunks:
                kv = src[2 * j + head]
                probs = jnp.exp(dot(kv, ask, 1, 1) - top) * scale
                dst[offset, head], dq = finish(kv, probs, dot(kv, cot, 1, 1), weighted * scale)
                total = total + dq
        grad_query.append(total)
    dq_ref[...] = jnp.where(low, grad_query[1], grad_query[0]) * factor


def core_sum_kernel(own, received, *outs):
    for j, out in enumerate(outs):
        out[...] = (own[j].astype(F32) + received[j].astype(F32)).astype(BF16)


def project_kernel(n_col, per_sample, *refs):
    n_in = len(refs) - n_col
    *parts, dq_ref, gz_ref, input_weight, tiles = refs[:n_in]
    outs = refs[n_in:]
    col = lax.axis_index("col")
    part = col % per_sample
    total = sum(ref[...].astype(F32) for ref in parts)
    strip, lanes = dq_ref.shape
    half = lanes // 2
    channels = gz_ref.shape[1]
    low = lax.broadcasted_iota(jnp.int32, (strip, lanes), 1) < half
    dv = jnp.where(low, total[0], total[1])
    dk = pltpu.roll(jnp.where(low, total[1], total[0]), half, 1)
    dq = pltpu.roll(dq_ref[...], half, 1)
    grad = jnp.where(part == 0, gz_ref[...].astype(F32), 0.0)
    for kind, value in enumerate((dq, dk, dv)):
        first = pl.multiple_of(kind * channels + part * lanes, lanes)
        weight = input_weight[:, pl.ds(first, lanes)]
        grad = grad + dot(value.astype(BF16), weight, 1, 1)
    grad = grad.astype(BF16)
    for k, out in enumerate(outs):
        out[...] = dot(tiles[col ^ k], grad).astype(BF16)


def output_kernel(per_sample, *refs):
    *parts, out = refs
    rows, cols, samples, channels = out.shape
    padded = pad8(cols)
    sample = lax.axis_index("col") // per_sample
    place = lax.broadcasted_iota(jnp.int32, (cols, samples, channels), 1)
    for i in range(rows):
        cells = jnp.zeros((cols, samples, channels), F32)
        for group in range(samples):
            total = sum(
                ref[...][i * padded : i * padded + cols].astype(F32)
                for ref in parts[group * per_sample : (group + 1) * per_sample]
            )
            cells = jnp.where(place == (sample ^ group), total[:, None, :], cells)
        out[i] = cells.astype(BF16)


def shards(
    pre_silu, out_grad, query_heads, key_heads, value_heads, conv_weight, out_weight, input_weight
):
    samples, rows, cols, channels = pre_silu.shape
    pairs, strip, head_dim = query_heads.shape
    n_row, n_col = lax.axis_size("row"), lax.axis_size("col")
    chips = n_row // 2
    per_sample = HEADS // pairs
    lanes = pairs * head_dim

    def to_col(array, k):
        pairs_of = [
            (r * n_col + c, (r ^ 1) * n_col + (c ^ k)) for r in range(n_row) for c in range(n_col)
        ]
        return lax.ppermute(array, ("row", "col"), pairs_of)

    def to_chip(array, k):
        return lax.ppermute(array, "row", [(i, i ^ (2 * k + 1)) for i in range(n_row)])

    def to_core(array):
        return lax.ppermute(array, "row", [(i, i ^ 1) for i in range(n_row)])

    def to_next_chip(array):
        edge = [(i, i + 3) for i in range(0, n_row - 2, 2)]
        return lax.ppermute(array, "row", edge + [(j, i) for i, j in edge])

    def cells(array):
        return jnp.transpose(array, (1, 2, 0, 3))

    def turned(array):
        return jnp.transpose(array, (0, 2, 1))

    saved = pltpu.VMEM((pairs, head_dim, strip), BF16)
    tile, kv, query = call(
        pack_kernel,
        (
            held((2, rows, cols, samples, channels), BF16),
            held((pairs, strip, lanes), BF16),
            held((strip, lanes), BF16),
        ),
        (saved, saved, saved, pltpu.SemaphoreType.DMA((5,))),
        range(5),
    )(cells(out_grad), cells(pre_silu), turned(query_heads), turned(key_heads), turned(value_heads))
    tiles = [to_col(tile, k) for k in range(n_col)]

    padded = pad8(cols)
    far = (
        jnp.asarray(shift_selector(rows, cols, n_col), BF16),
        jnp.asarray(shift_selector(1, cols, n_col), BF16),
        conv_weight,
        out_weight,
    )
    loaded = call(
        load_kernel,
        [held(array.shape, BF16) for array in far],
        [pltpu.SemaphoreType.DMA((len(far),))],
        range(len(far)),
    )(*far)

    def doubled(joined, received, *last):
        parts = (joined, received, *last)
        return call(join_kernel, held((sum(p.shape[0] for p in parts), strip, lanes), BF16))(*parts)

    distances = [chips >> (i + 1) for i in range(chips.bit_length() - 1)]
    offsets = [0]
    for distance in distances:
        offsets = offsets + [offset + distance for offset in offsets]
    tiles, received, (shifts, rim_shifts, conv_weight, out_weight) = lax.optimization_barrier(
        (tiles, to_chip(kv, distances[0]), loaded)
    )
    joined = doubled(kv, received)

    rim = held((n_col, cols, samples, channels), BF16)
    rim_core, rim_chip = call(rim_kernel, (rim, rim))(*tiles)
    halo_chip, halo_core = to_next_chip(rim_chip), to_core(rim_core)
    for distance in distances[1:-1]:
        joined = doubled(joined, to_chip(joined, distance))
    received = to_chip(joined, distances[-1])

    whole = held((strip, channels), F32)
    conv, gate = call(
        functools.partial(conv_kernel, n_col, per_sample),
        (whole, whole),
        [pltpu.VMEM((n_col, rows, padded, channels), F32)] * 2,
    )(*tiles, shifts, conv_weight)
    received, conv, halo_chip, halo_core = lax.optimization_barrier(
        (received, conv, halo_chip, halo_core)
    )
    joined = doubled(joined, received, query[None])
    received = to_core(joined)
    grad_z, grad_out = call(
        functools.partial(rim_conv_kernel, per_sample),
        (held((strip, channels), BF16), held((strip, lanes), BF16)),
        [pltpu.VMEM((2, n_col, padded, channels), F32)],
    )(halo_core, halo_chip, conv, gate, rim_shifts, conv_weight, out_weight)

    block = held((chips, pairs, strip, lanes), BF16)
    dkv_sent, dkv_kept, dq = call(
        functools.partial(attention_kernel, offsets), (block, block, held((strip, lanes), F32))
    )(joined, received, grad_out)

    sums = call(core_sum_kernel, [held((pairs, strip, lanes), BF16) for _ in range(chips)])(
        dkv_kept, to_core(dkv_sent)
    )
    parts = [to_chip(sums[k], k) for k in reversed(range(1, chips))] + [sums[0]]

    cut = call(
        functools.partial(project_kernel, n_col, per_sample),
        [held((rows * padded, channels), BF16)] * n_col,
    )(*parts, dq, grad_z, input_weight, jnp.asarray(tile_selector(rows, cols, n_col), BF16))
    grad_input = call(
        functools.partial(output_kernel, per_sample), held((rows, cols, samples, channels), BF16)
    )(*[to_col(cut[k], k) for k in range(n_col)])
    return jnp.transpose(grad_input, (2, 0, 1, 3))


def solution(mesh):
    tile = P(None, "row", "col", None)
    heads = P("col", "row", None)
    return jax.shard_map(
        shards,
        mesh=mesh,
        in_specs=(tile, tile, heads, heads, heads, P(), P(), P()),
        out_specs=tile,
        check_vma=False,
    )
```

```python
import functools

import jax
import jax.numpy as jnp
import numpy as np
from jax import lax
from jax.experimental import pallas as pl
from jax.experimental.pallas import tpu as pltpu
from jax.sharding import PartitionSpec as P

HEADS = 4
VMEM_BYTES = 32 * 1024 * 1024
HELD_BYTES = 3 * 512 * 1024
UNROLLED_CHUNKS = 16
F32 = jnp.float32
BF16 = jnp.bfloat16


def dot(left, right, left_dim=1, right_dim=0):
    return lax.dot_general(
        left, right, (((left_dim,), (right_dim,)), ((), ())), preferred_element_type=F32
    )


def call(kernel, out_shape, scratch=(), far=()):
    def run(*operands):
        specs = [pl.BlockSpec(memory_space=pltpu.VMEM)] * len(operands)
        operands = list(operands)
        for i, operand in enumerate(operands):
            if i in far:
                specs[i] = pl.BlockSpec(memory_space=pltpu.HBM)
                operands[i] = pltpu.with_memory_space_constraint(operand, pltpu.HBM)
            elif operand.size * operand.dtype.itemsize <= HELD_BYTES:
                operands[i] = pltpu.with_memory_space_constraint(operand, pltpu.VMEM)
        return pl.pallas_call(
            kernel,
            out_shape=out_shape,
            in_specs=specs,
            out_specs=jax.tree.map(lambda _: pl.BlockSpec(memory_space=pltpu.VMEM), out_shape),
            scratch_shapes=list(scratch),
            compiler_params=pltpu.CompilerParams(vmem_limit_bytes=VMEM_BYTES),
        )(*operands)

    return run


def held(shape, dtype):
    small = np.prod(shape) * np.dtype(dtype).itemsize <= HELD_BYTES
    return (pltpu.VMEM if small else jax.ShapeDtypeStruct)(shape, dtype)


def pad8(amount):
    return -(-amount // 8) * 8


def shift_selector(rows, cols, tiles):
    width, padded = tiles * cols, pad8(cols)
    select = np.zeros((3, rows, width, tiles, rows, padded), np.float32)
    for shift in (-1, 0, 1):
        for j in range(max(0, shift), min(width, width + shift)):
            tile, inner = divmod(j - shift, cols)
            for i in range(rows):
                select[shift + 1, i, j, tile, i, inner] = 1
    return select.reshape(3, rows * width, tiles * rows * padded)


def tile_selector(rows, cols, tiles):
    width, padded = tiles * cols, pad8(cols)
    select = np.zeros((tiles, rows, padded, rows, width), np.float32)
    for tile in range(tiles):
        for i in range(rows):
            for inner in range(cols):
                select[tile, i, inner, i, tile * cols + inner] = 1
    return select.reshape(tiles, rows * padded, rows * width)


def start_copies(pairs, sems):
    copies = [
        pltpu.make_async_copy(src, dst, sems.at[i]) for i, (src, dst) in enumerate(pairs)
    ]
    for copy in copies:
        copy.start()
    return copies


def pack_kernel(
    out_grad, pre_silu, queries, keys, values, tile, kv, query, q_ref, k_ref, v_ref, sems
):
    copies = start_copies(
        [
            (values, v_ref),
            (keys, k_ref),
            (queries, q_ref),
            (out_grad, tile.at[0]),
            (pre_silu, tile.at[1]),
        ],
        sems,
    )

    def beside(left, right):
        return jnp.concatenate([left.astype(F32), right.astype(F32)], 0).T.astype(BF16)

    copies[0].wait()
    copies[1].wait()
    kv[0] = beside(v_ref[0], k_ref[0])
    kv[1] = beside(k_ref[1], v_ref[1])
    copies[2].wait()
    query[...] = beside(q_ref[1], q_ref[0]) * jnp.asarray(q_ref.shape[1] ** -0.5, BF16)
    copies[3].wait()
    copies[4].wait()


def rim_kernel(n_col, per_sample, *refs):
    tiles, (*parts, to_core, to_chip, joined, rims) = refs[:n_col], refs[n_col:]
    col = lax.axis_index("col")
    rows = tiles[0].shape[1]
    lanes = to_core.shape[1]
    used = rims.shape[1] * rims.shape[2]
    inner = jnp.where(lax.axis_index("row") % 2 == 1, rows - 1, 0)
    cols = tiles[0].shape[2]
    rims[...] = jnp.zeros_like(rims)
    for side, (row, out) in enumerate(((inner, to_core), (rows - 1 - inner, to_chip))):
        for k, tile in enumerate(tiles):
            rims[side, col ^ k, :cols] = pick(tile[0, row], col // per_sample)
        flat = rims[side].reshape(used, -1).astype(BF16)
        out[...] = jnp.zeros_like(out)
        for part in range(flat.shape[1] // lanes):
            out[part * used : (part + 1) * used] = flat[:, part * lanes : (part + 1) * lanes]
    join_kernel([part.shape[0] for part in parts], *parts, joined)
    joined[joined.shape[0] - 1] = to_chip[...]


def join_kernel(counts, *refs):
    *parts, out = refs
    first = 0
    for part, count in zip(parts, counts):
        for j in range(count):
            out[first + j] = part[j]
        first += count


def load_kernel(*refs):
    *copied, sems = refs
    half = len(copied) // 2
    for copy in start_copies(list(zip(copied[:half], copied[half:])), sems):
        copy.wait()


def pick(cells, sample):
    place = lax.broadcasted_iota(jnp.int32, cells.shape, 1)
    return jnp.sum(jnp.where(place == sample, cells.astype(F32), 0.0), axis=1)


def conv_kernel(n_col, per_sample, *refs):
    tiles, (shifts, conv_weight, conv_ref, gate_ref, grads, silus) = refs[:n_col], refs[n_col:]
    col = lax.axis_index("col")
    sample = col // per_sample
    _, rows, cols, _, channels = tiles[0].shape
    width = n_col * cols
    grads[...] = jnp.zeros_like(grads)
    silus[...] = jnp.zeros_like(silus)
    for k in range(n_col):
        for i in range(rows):
            grads[col ^ k, i, :cols] = pick(tiles[k][0, i], sample)
            silus[col ^ k, i, :cols] = pick(tiles[k][1, i], sample)
    flat = grads[...].reshape(-1, channels).astype(BF16)
    none = jnp.zeros((width, channels), F32)
    conv = jnp.zeros((rows * width, channels), F32)
    for b in (-1, 0, 1):
        here = dot(shifts[b + 1], flat)
        above = jnp.concatenate([none, here[:-width]], 0)
        below = jnp.concatenate([here[width:], none], 0)
        for a, window in ((-1, below), (0, here), (1, above)):
            conv = conv + dot(window.astype(BF16), conv_weight[a + 1, b + 1], 1, 1)
    conv_ref[...] = conv
    z = dot(shifts[1], silus[...].reshape(-1, channels).astype(BF16))
    sigma = 1.0 / (1.0 + jnp.exp(-z))
    gate_ref[...] = sigma * (1.0 + z * (1.0 - sigma))


def rim_conv_kernel(halo_core, halo_last, halo_odd, conv, gate, *refs):
    shifts, conv_weight, out_weight, gz_ref, go_ref = refs
    col, row = lax.axis_index("col"), lax.axis_index("row")
    core, chip = row % 2, row // 2
    strip, channels = gz_ref.shape
    lanes = go_ref.shape[1]
    per_sample = out_weight.shape[0] // lanes
    width = shifts.shape[1]
    used = shifts.shape[2]
    last = halo_last[halo_last.shape[0] - 1]
    missing = jnp.logical_or(row == 1, row == lax.axis_size("row") - 2)
    halo_chip = jnp.where(core == chip % 2, last, halo_odd[...])
    halo_chip = jnp.where(missing, jnp.zeros_like(last), halo_chip)
    inner = halo_core[...]
    parts = channels // lanes

    def spread(halo):
        return jnp.concatenate([halo[p * used : (p + 1) * used] for p in range(parts)], 1)

    rims = (
        spread(jnp.where(core == 1, halo_chip, inner)),
        spread(jnp.where(core == 1, inner, halo_chip)),
    )
    edges = []
    for flat, a in zip(rims, (1, -1)):
        edge = jnp.zeros((width, channels), F32)
        for b in (-1, 0, 1):
            window = dot(shifts[b + 1], flat).astype(BF16)
            edge = edge + dot(window, conv_weight[a + 1, b + 1], 1, 1)
        edges.append(edge)
    between = jnp.zeros((strip - 2 * width, channels), F32)
    total = conv[...] + jnp.concatenate([edges[0], between, edges[1]], 0)
    grad_z = (total * gate[...]).astype(BF16)
    gz_ref[...] = grad_z
    first = pl.multiple_of(col % per_sample * lanes, lanes)
    go_ref[...] = dot(grad_z, out_weight[pl.ds(first, lanes), :], 1, 1).astype(BF16)


def attention_kernel(offsets, kv_sent, kv_kept, go_ref, dkv_sent, dkv_kept, dq_ref):
    strip, lanes = go_ref.shape
    half = lanes // 2
    factor = half**-0.5
    low = lax.broadcasted_iota(jnp.int32, (strip, lanes), 1) < half
    query, grad_out = kv_kept[kv_kept.shape[0] - 1], go_ref[...]
    none = jnp.zeros_like(query)
    asked = (jnp.where(low, none, query), jnp.where(low, query, none))
    cotangent = (jnp.where(low, grad_out, none), jnp.where(low, none, grad_out))
    chunks = []
    for j, offset in enumerate(offsets):
        even = offset != 0 and offset.bit_count() % 2 == 0
        chunks.append((kv_sent, dkv_kept if even else dkv_sent, j, offset))
        chunks.append((kv_kept, dkv_sent if even else dkv_kept, j, offset))

    grad_query = []
    for head in (0, 1):
        ask, cot = asked[head], cotangent[head]

        def finish(kv, probs, probs_grad, row_dot):
            grad_scores = (probs * (probs_grad - row_dot)).astype(BF16)
            dkv = dot(grad_scores, ask) + dot(probs.astype(BF16), cot)
            return dkv.astype(BF16), dot(grad_scores, kv, 0, 0)

        total = jnp.zeros((strip, lanes), F32)
        if len(chunks) <= UNROLLED_CHUNKS:
            scores = [dot(src[2 * j + head], ask, 1, 1) for src, _, j, _ in chunks]
            top = jnp.max(functools.reduce(jnp.maximum, scores), axis=0, keepdims=True)
            exps = [jnp.exp(s - top) for s in scores]
            scale = 1.0 / jnp.sum(sum(exps), axis=0, keepdims=True)
            probs = [e * scale for e in exps]
            probs_grads = [dot(src[2 * j + head], cot, 1, 1) for src, _, j, _ in chunks]
            weighted = sum(p * g for p, g in zip(probs, probs_grads))
            row_dot = jnp.sum(weighted, axis=0, keepdims=True)
            for (src, dst, j, offset), p, g in zip(chunks, probs, probs_grads):
                dst[offset, head], dq = finish(src[2 * j + head], p, g, row_dot)
                total = total + dq
        else:

            def gather(kv, carry):
                top, norm, weighted = carry
                scores = dot(kv, ask, 1, 1)
                new = jnp.maximum(top, jnp.max(scores, axis=0, keepdims=True))
                exps = jnp.exp(scores - new)
                rescale = jnp.exp(top - new)
                weights = jnp.sum(exps * dot(kv, cot, 1, 1), axis=0, keepdims=True)
                return (
                    new,
                    norm * rescale + jnp.sum(exps, axis=0, keepdims=True),
                    weighted * rescale + weights,
                )

            zero = jnp.zeros((1, strip), F32)
            stats = (jnp.full((1, strip), -jnp.inf, F32), zero, zero)
            for src in (kv_sent, kv_kept):
                stats = lax.fori_loop(
                    0,
                    len(offsets),
                    lambda j, carry, src=src: gather(src[2 * j + head], carry),
                    stats,
                )
            top, norm, weighted = stats
            scale = 1.0 / norm
            for src, dst, j, offset in chunks:
                kv = src[2 * j + head]
                probs = jnp.exp(dot(kv, ask, 1, 1) - top) * scale
                dst[offset, head], dq = finish(kv, probs, dot(kv, cot, 1, 1), weighted * scale)
                total = total + dq
        grad_query.append(total)
    dq_ref[...] = jnp.where(low, grad_query[1], grad_query[0]) * factor


def core_sum_kernel(own, received, *outs):
    for j, out in enumerate(outs):
        out[...] = (own[j].astype(F32) + received[j].astype(F32)).astype(BF16)


def project_kernel(n_col, per_sample, *refs):
    n_in = len(refs) - n_col
    *parts, dq_ref, gz_ref, input_weight, tiles = refs[:n_in]
    outs = refs[n_in:]
    col = lax.axis_index("col")
    part = col % per_sample
    total = sum(ref[...].astype(F32) for ref in parts)
    strip, lanes = dq_ref.shape
    half = lanes // 2
    channels = gz_ref.shape[1]
    low = lax.broadcasted_iota(jnp.int32, (strip, lanes), 1) < half
    dv = jnp.where(low, total[0], total[1])
    dk = pltpu.roll(jnp.where(low, total[1], total[0]), half, 1)
    dq = pltpu.roll(dq_ref[...], half, 1)
    grad = jnp.where(part == 0, gz_ref[...].astype(F32), 0.0)
    for kind, value in enumerate((dq, dk, dv)):
        first = pl.multiple_of(kind * channels + part * lanes, lanes)
        weight = input_weight[:, pl.ds(first, lanes)]
        grad = grad + dot(value.astype(BF16), weight, 1, 1)
    grad = grad.astype(BF16)
    for k, out in enumerate(outs):
        out[...] = dot(tiles[col ^ k], grad).astype(BF16)


def output_kernel(per_sample, *refs):
    *parts, out = refs
    parts = parts[::-1]
    rows, cols, samples, channels = out.shape
    padded = pad8(cols)
    sample = lax.axis_index("col") // per_sample
    place = lax.broadcasted_iota(jnp.int32, (cols, samples, channels), 1)
    for i in range(rows):
        cells = jnp.zeros((cols, samples, channels), F32)
        for group in range(samples):
            total = sum(
                ref[...][i * padded : i * padded + cols].astype(F32)
                for ref in parts[group * per_sample : (group + 1) * per_sample]
            )
            cells = jnp.where(place == (sample ^ group), total[:, None, :], cells)
        out[i] = cells.astype(BF16)


def shards(
    pre_silu, out_grad, query_heads, key_heads, value_heads, conv_weight, out_weight, input_weight
):
    samples, rows, cols, channels = pre_silu.shape
    pairs, strip, head_dim = query_heads.shape
    n_row, n_col = lax.axis_size("row"), lax.axis_size("col")
    chips = n_row // 2
    per_sample = HEADS // pairs
    lanes = pairs * head_dim

    def to_col(array, k):
        pairs_of = [
            (r * n_col + c, (r ^ 1) * n_col + (c ^ k)) for r in range(n_row) for c in range(n_col)
        ]
        return lax.ppermute(array, ("row", "col"), pairs_of)

    def to_chip(array, k):
        return lax.ppermute(array, "row", [(i, i ^ (2 * k + 1)) for i in range(n_row)])

    def to_core(array):
        return lax.ppermute(array, "row", [(i, i ^ 1) for i in range(n_row)])

    def to_odd_chip(array):
        both = [(0, 1), (n_row - 2, n_row - 1)]
        for i in range(2, n_row - 2, 4):
            both += [(i, i + 3), (i + 1, i + 2)]
        return lax.ppermute(array, "row", both + [(j, i) for i, j in both])

    def cells(array):
        return jnp.transpose(array, (1, 2, 0, 3))

    def turned(array):
        return jnp.transpose(array, (0, 2, 1))

    saved = pltpu.VMEM((pairs, head_dim, strip), BF16)
    tile, kv, query = call(
        pack_kernel,
        (
            held((2, rows, cols, samples, channels), BF16),
            held((pairs, strip, lanes), BF16),
            held((strip, lanes), BF16),
        ),
        (saved, saved, saved, pltpu.SemaphoreType.DMA((5,))),
        range(5),
    )(cells(out_grad), cells(pre_silu), turned(query_heads), turned(key_heads), turned(value_heads))
    tiles = [to_col(tile, k) for k in range(n_col)]

    padded = pad8(cols)
    far = (
        jnp.asarray(shift_selector(rows, cols, n_col), BF16),
        jnp.asarray(shift_selector(1, cols, n_col), BF16),
        conv_weight,
        out_weight,
    )
    loaded = call(
        load_kernel,
        [held(array.shape, BF16) for array in far],
        [pltpu.SemaphoreType.DMA((len(far),))],
        range(len(far)),
    )(*far)

    def doubled(*parts, counts=None):
        counts = counts or [part.shape[0] for part in parts]
        return call(
            functools.partial(join_kernel, counts), held((sum(counts), strip, lanes), BF16)
        )(*parts)

    distances = [chips >> (i + 1) for i in range(chips.bit_length() - 1)]
    offsets = [0]
    for distance in distances:
        offsets = offsets + [offset + distance for offset in offsets]
    tiles, received, (shifts, rim_shifts, conv_weight, out_weight) = lax.optimization_barrier(
        (tiles, to_chip(kv, distances[0]), loaded)
    )
    parts = (kv, received)
    for distance in distances[1:-1]:
        joined = doubled(*parts)
        parts = (joined, to_chip(joined, distance))

    rim = held((strip, lanes), BF16)
    blocks = sum(part.shape[0] for part in parts)
    rim_core, rim_chip, sent = call(
        functools.partial(rim_kernel, n_col, per_sample),
        (rim, rim, held((blocks + 1, strip, lanes), BF16)),
        [pltpu.VMEM((2, n_col, padded, channels), F32)],
    )(*tiles, *parts)
    received = to_chip(sent, distances[-1])
    halo_odd, halo_core = to_odd_chip(rim_chip), to_core(rim_core)

    whole = held((strip, channels), F32)
    conv, gate = call(
        functools.partial(conv_kernel, n_col, per_sample),
        (whole, whole),
        [pltpu.VMEM((n_col, rows, padded, channels), F32)] * 2,
    )(*tiles, shifts, conv_weight)
    received, conv, halo_odd, halo_core = lax.optimization_barrier(
        (received, conv, halo_odd, halo_core)
    )
    joined = doubled(sent, received, query[None], counts=(blocks, blocks, 1))
    other = to_core(joined)
    grad_z, grad_out = call(
        rim_conv_kernel,
        (held((strip, channels), BF16), held((strip, lanes), BF16)),
    )(halo_core, received, halo_odd, conv, gate, rim_shifts, conv_weight, out_weight)

    block = held((chips, pairs, strip, lanes), BF16)
    dkv_sent, dkv_kept, dq = call(
        functools.partial(attention_kernel, offsets), (block, block, held((strip, lanes), F32))
    )(joined, other, grad_out)

    sums = call(core_sum_kernel, [held((pairs, strip, lanes), BF16) for _ in range(chips)])(
        dkv_kept, to_core(dkv_sent)
    )
    parts = [to_chip(sums[k], k) for k in reversed(range(1, chips))] + [sums[0]]

    cut = call(
        functools.partial(project_kernel, n_col, per_sample),
        [held((rows * padded, channels), BF16)] * n_col,
    )(*parts, dq, grad_z, input_weight, jnp.asarray(tile_selector(rows, cols, n_col), BF16))
    grad_input = call(
        functools.partial(output_kernel, per_sample), held((rows, cols, samples, channels), BF16)
    )(*[to_col(cut[k], k) for k in reversed(range(n_col))])
    return jnp.transpose(grad_input, (2, 0, 1, 3))


def solution(mesh):
    tile = P(None, "row", "col", None)
    heads = P("col", "row", None)
    return jax.shard_map(
        shards,
        mesh=mesh,
        in_specs=(tile, tile, heads, heads, heads, P(), P(), P()),
        out_specs=tile,
        check_vma=False,
    )
```

```python
import functools

import jax
import jax.numpy as jnp
import numpy as np
from jax import lax
from jax.experimental import pallas as pl
from jax.experimental.pallas import tpu as pltpu
from jax.sharding import PartitionSpec as P

HEADS = 4
VMEM_BYTES = 32 * 1024 * 1024
HELD_BYTES = 3 * 512 * 1024
UNROLLED_CHUNKS = 16
F32 = jnp.float32
BF16 = jnp.bfloat16


def dot(left, right, left_dim=1, right_dim=0):
    return lax.dot_general(
        left, right, (((left_dim,), (right_dim,)), ((), ())), preferred_element_type=F32
    )


def call(kernel, out_shape, scratch=(), far=()):
    def run(*operands):
        specs = [pl.BlockSpec(memory_space=pltpu.VMEM)] * len(operands)
        operands = list(operands)
        for i, operand in enumerate(operands):
            if i in far:
                specs[i] = pl.BlockSpec(memory_space=pltpu.HBM)
                operands[i] = pltpu.with_memory_space_constraint(operand, pltpu.HBM)
            elif operand.size * operand.dtype.itemsize <= HELD_BYTES:
                operands[i] = pltpu.with_memory_space_constraint(operand, pltpu.VMEM)
        return pl.pallas_call(
            kernel,
            out_shape=out_shape,
            in_specs=specs,
            out_specs=jax.tree.map(
                lambda out: pl.BlockSpec(
                    memory_space=pltpu.HBM
                    if getattr(out, "memory_space", None) == pltpu.HBM
                    else pltpu.VMEM
                ),
                out_shape,
            ),
            scratch_shapes=list(scratch),
            compiler_params=pltpu.CompilerParams(vmem_limit_bytes=VMEM_BYTES),
        )(*operands)

    return run


def held(shape, dtype):
    small = np.prod(shape) * np.dtype(dtype).itemsize <= HELD_BYTES
    return (pltpu.VMEM if small else jax.ShapeDtypeStruct)(shape, dtype)


def pad8(amount):
    return -(-amount // 8) * 8


def shift_selector(rows, cols, tiles):
    width, padded = tiles * cols, pad8(cols)
    select = np.zeros((3, rows, width, tiles, rows, padded), np.float32)
    for shift in (-1, 0, 1):
        for j in range(max(0, shift), min(width, width + shift)):
            tile, inner = divmod(j - shift, cols)
            for i in range(rows):
                select[shift + 1, i, j, tile, i, inner] = 1
    return select.reshape(3, rows * width, tiles * rows * padded)


def tile_selector(rows, cols, tiles):
    width, padded = tiles * cols, pad8(cols)
    select = np.zeros((tiles, rows, padded, rows, width), np.float32)
    for tile in range(tiles):
        for i in range(rows):
            for inner in range(cols):
                select[tile, i, inner, i, tile * cols + inner] = 1
    return select.reshape(tiles, rows * padded, rows * width)


def start_copies(pairs, sems):
    copies = [
        pltpu.make_async_copy(src, dst, sems.at[i]) for i, (src, dst) in enumerate(pairs)
    ]
    for copy in copies:
        copy.start()
    return copies


def pack_kernel(
    out_grad, pre_silu, queries, keys, values, tile, kv, query, q_ref, k_ref, v_ref, sems
):
    copies = start_copies(
        [
            (values, v_ref),
            (keys, k_ref),
            (queries, q_ref),
            (out_grad, tile.at[0]),
            (pre_silu, tile.at[1]),
        ],
        sems,
    )

    def beside(left, right):
        return jnp.concatenate([left.astype(F32), right.astype(F32)], 0).T.astype(BF16)

    copies[0].wait()
    copies[1].wait()
    kv[0] = beside(v_ref[0], k_ref[0])
    kv[1] = beside(k_ref[1], v_ref[1])
    copies[2].wait()
    query[...] = beside(q_ref[1], q_ref[0]) * jnp.asarray(q_ref.shape[1] ** -0.5, BF16)
    copies[3].wait()
    copies[4].wait()


def rim_kernel(n_col, per_sample, *refs):
    tiles, (*parts, to_core, to_chip, joined, rims) = refs[:n_col], refs[n_col:]
    col = lax.axis_index("col")
    rows = tiles[0].shape[1]
    lanes = to_core.shape[1]
    used = rims.shape[1] * rims.shape[2]
    inner = jnp.where(lax.axis_index("row") % 2 == 1, rows - 1, 0)
    cols = tiles[0].shape[2]
    rims[...] = jnp.zeros_like(rims)
    for side, (row, out) in enumerate(((inner, to_core), (rows - 1 - inner, to_chip))):
        for k, tile in enumerate(tiles):
            rims[side, col ^ k, :cols] = pick(tile[0, row], col // per_sample)
        flat = rims[side].reshape(used, -1).astype(BF16)
        out[...] = jnp.zeros_like(out)
        for part in range(flat.shape[1] // lanes):
            out[part * used : (part + 1) * used] = flat[:, part * lanes : (part + 1) * lanes]
    join_kernel([part.shape[0] for part in parts], *parts, joined)
    joined[joined.shape[0] - 1] = to_chip[...]


def join_kernel(counts, *refs):
    *parts, out = refs
    first = 0
    for part, count in zip(parts, counts):
        for j in range(count):
            out[first + j] = part[j]
        first += count


def load_kernel(*refs):
    *copied, sems = refs
    half = len(copied) // 2
    for copy in start_copies(list(zip(copied[:half], copied[half:])), sems):
        copy.wait()


def pick(cells, sample):
    place = lax.broadcasted_iota(jnp.int32, cells.shape, 1)
    return jnp.sum(jnp.where(place == sample, cells.astype(F32), 0.0), axis=1)


def conv_kernel(n_col, per_sample, *refs):
    tiles, (shifts, conv_weight, conv_ref, gate_ref, grads, silus) = refs[:n_col], refs[n_col:]
    col = lax.axis_index("col")
    sample = col // per_sample
    _, rows, cols, _, channels = tiles[0].shape
    width = n_col * cols
    grads[...] = jnp.zeros_like(grads)
    silus[...] = jnp.zeros_like(silus)
    for k in range(n_col):
        for i in range(rows):
            grads[col ^ k, i, :cols] = pick(tiles[k][0, i], sample)
            silus[col ^ k, i, :cols] = pick(tiles[k][1, i], sample)
    flat = grads[...].reshape(-1, channels).astype(BF16)
    none = jnp.zeros((width, channels), F32)
    conv = jnp.zeros((rows * width, channels), F32)
    for b in (-1, 0, 1):
        here = dot(shifts[b + 1], flat)
        above = jnp.concatenate([none, here[:-width]], 0)
        below = jnp.concatenate([here[width:], none], 0)
        for a, window in ((-1, below), (0, here), (1, above)):
            conv = conv + dot(window.astype(BF16), conv_weight[a + 1, b + 1], 1, 1)
    conv_ref[...] = conv
    z = dot(shifts[1], silus[...].reshape(-1, channels).astype(BF16))
    sigma = 1.0 / (1.0 + jnp.exp(-z))
    gate_ref[...] = sigma * (1.0 + z * (1.0 - sigma))


def rim_conv_kernel(halo_core, halo_last, halo_odd, conv, gate, *refs):
    shifts, conv_weight, out_weight, gz_ref, go_ref = refs
    col, row = lax.axis_index("col"), lax.axis_index("row")
    core, chip = row % 2, row // 2
    strip, channels = gz_ref.shape
    lanes = go_ref.shape[1]
    per_sample = out_weight.shape[0] // lanes
    width = shifts.shape[1]
    used = shifts.shape[2]
    last = halo_last[halo_last.shape[0] - 1]
    missing = jnp.logical_or(row == 1, row == lax.axis_size("row") - 2)
    halo_chip = jnp.where(core == chip % 2, last, halo_odd[...])
    halo_chip = jnp.where(missing, jnp.zeros_like(last), halo_chip)
    inner = halo_core[...]
    parts = channels // lanes

    def spread(halo):
        return jnp.concatenate([halo[p * used : (p + 1) * used] for p in range(parts)], 1)

    rims = (
        spread(jnp.where(core == 1, halo_chip, inner)),
        spread(jnp.where(core == 1, inner, halo_chip)),
    )
    edges = []
    for flat, a in zip(rims, (1, -1)):
        edge = jnp.zeros((width, channels), F32)
        for b in (-1, 0, 1):
            window = dot(shifts[b + 1], flat).astype(BF16)
            edge = edge + dot(window, conv_weight[a + 1, b + 1], 1, 1)
        edges.append(edge)
    between = jnp.zeros((strip - 2 * width, channels), F32)
    total = conv[...] + jnp.concatenate([edges[0], between, edges[1]], 0)
    grad_z = (total * gate[...]).astype(BF16)
    gz_ref[...] = grad_z
    first = pl.multiple_of(col % per_sample * lanes, lanes)
    go_ref[...] = dot(grad_z, out_weight[pl.ds(first, lanes), :], 1, 1).astype(BF16)


def attention_kernel(offsets, kv_sent, kv_kept, go_ref, dkv_sent, dkv_kept, dq_ref):
    strip, lanes = go_ref.shape
    half = lanes // 2
    factor = half**-0.5
    low = lax.broadcasted_iota(jnp.int32, (strip, lanes), 1) < half
    query, grad_out = kv_kept[kv_kept.shape[0] - 1], go_ref[...]
    none = jnp.zeros_like(query)
    asked = (jnp.where(low, none, query), jnp.where(low, query, none))
    cotangent = (jnp.where(low, grad_out, none), jnp.where(low, none, grad_out))
    chunks = []
    for j, offset in enumerate(offsets):
        even = offset != 0 and offset.bit_count() % 2 == 0
        chunks.append((kv_sent, dkv_kept if even else dkv_sent, j, offset))
        chunks.append((kv_kept, dkv_sent if even else dkv_kept, j, offset))

    heads = (0, 1)
    if len(chunks) <= UNROLLED_CHUNKS:
        kvs = [
            jnp.concatenate([src[2 * j + h].astype(F32) for src, _, j, _ in chunks], 0).astype(BF16)
            for h in heads
        ]
        scores = [dot(kvs[h], asked[h], 1, 1) for h in heads]
        probs_grads = [dot(kvs[h], cotangent[h], 1, 1) for h in heads]
        exps = [jnp.exp(s - jnp.max(s, axis=0, keepdims=True)) for s in scores]
        scales = [1.0 / jnp.sum(e, axis=0, keepdims=True) for e in exps]
        row_dots = [
            jnp.sum(e * g, axis=0, keepdims=True) * s for e, g, s in zip(exps, probs_grads, scales)
        ]
        probs = [e * s for e, s in zip(exps, scales)]
        grad_scores = [
            (p * (g - r)).astype(BF16) for p, g, r in zip(probs, probs_grads, row_dots)
        ]
        grad_query = [dot(grad_scores[h], kvs[h], 0, 0) for h in heads]
        for h in heads:
            given = jnp.concatenate([grad_scores[h], probs[h].astype(BF16)], 1)
            dkv = dot(given, jnp.concatenate([asked[h], cotangent[h]], 0))
            for i, (_, dst, _, offset) in enumerate(chunks):
                dst[offset, h] = dkv[i * strip : (i + 1) * strip].astype(BF16)
    else:
        grad_query = []
        for head in heads:
            ask, cot = asked[head], cotangent[head]

            def gather(kv, carry):
                top, norm, weighted = carry
                scores = dot(kv, ask, 1, 1)
                new = jnp.maximum(top, jnp.max(scores, axis=0, keepdims=True))
                exps = jnp.exp(scores - new)
                rescale = jnp.exp(top - new)
                weights = jnp.sum(exps * dot(kv, cot, 1, 1), axis=0, keepdims=True)
                return (
                    new,
                    norm * rescale + jnp.sum(exps, axis=0, keepdims=True),
                    weighted * rescale + weights,
                )

            zero = jnp.zeros((1, strip), F32)
            stats = (jnp.full((1, strip), -jnp.inf, F32), zero, zero)
            for src in (kv_sent, kv_kept):
                stats = lax.fori_loop(
                    0,
                    len(offsets),
                    lambda j, carry, src=src: gather(src[2 * j + head], carry),
                    stats,
                )
            top, norm, weighted = stats
            scale = 1.0 / norm
            total = jnp.zeros((strip, lanes), F32)
            for src, dst, j, offset in chunks:
                kv = src[2 * j + head]
                probs = jnp.exp(dot(kv, ask, 1, 1) - top) * scale
                grad_scores = (probs * (dot(kv, cot, 1, 1) - weighted * scale)).astype(BF16)
                dkv = dot(grad_scores, ask) + dot(probs.astype(BF16), cot)
                dst[offset, head] = dkv.astype(BF16)
                total = total + dot(grad_scores, kv, 0, 0)
            grad_query.append(total)
    dq_ref[...] = jnp.where(low, grad_query[1], grad_query[0]) * factor


def core_sum_kernel(own, received, *outs):
    for j, out in enumerate(outs):
        out[...] = (own[j].astype(F32) + received[j].astype(F32)).astype(BF16)


def project_kernel(n_col, per_sample, *refs):
    *refs, cut = refs
    n_in = len(refs) - n_col
    *parts, dq_ref, gz_ref, input_weight, tiles = refs[:n_in]
    outs = refs[n_in:]
    col = lax.axis_index("col")
    part = col % per_sample
    total = sum(ref[...].astype(F32) for ref in parts)
    strip, lanes = dq_ref.shape
    half = lanes // 2
    channels = gz_ref.shape[1]
    low = lax.broadcasted_iota(jnp.int32, (strip, lanes), 1) < half
    dv = jnp.where(low, total[0], total[1])
    dk = pltpu.roll(jnp.where(low, total[1], total[0]), half, 1)
    dq = pltpu.roll(dq_ref[...], half, 1)
    grad = jnp.where(part == 0, gz_ref[...].astype(F32), 0.0)
    for kind, value in enumerate((dq, dk, dv)):
        first = pl.multiple_of(kind * channels + part * lanes, lanes)
        weight = input_weight[:, pl.ds(first, lanes)]
        grad = grad + dot(value.astype(BF16), weight, 1, 1)
    cut[...] = dot(tiles[...], grad.astype(BF16)).reshape(cut.shape)
    for k, out in enumerate(outs):
        out[...] = cut[col ^ k].astype(BF16)


def output_kernel(per_sample, *refs):
    *parts, far_out, out, sem = refs
    parts = parts[::-1]
    rows, cols, samples, channels = out.shape
    padded = pad8(cols)
    sample = lax.axis_index("col") // per_sample
    place = lax.broadcasted_iota(jnp.int32, (cols, samples, channels), 1)
    for i in range(rows):
        cells = jnp.zeros((cols, samples, channels), F32)
        for group in range(samples):
            total = sum(
                ref[...][i * padded : i * padded + cols].astype(F32)
                for ref in parts[group * per_sample : (group + 1) * per_sample]
            )
            cells = jnp.where(place == (sample ^ group), total[:, None, :], cells)
        out[i] = cells.astype(BF16)
    copy = pltpu.make_async_copy(out, far_out, sem)
    copy.start()
    copy.wait()


def shards(
    pre_silu, out_grad, query_heads, key_heads, value_heads, conv_weight, out_weight, input_weight
):
    samples, rows, cols, channels = pre_silu.shape
    pairs, strip, head_dim = query_heads.shape
    n_row, n_col = lax.axis_size("row"), lax.axis_size("col")
    chips = n_row // 2
    per_sample = HEADS // pairs
    lanes = pairs * head_dim

    def to_col(array, k):
        pairs_of = [
            (r * n_col + c, (r ^ 1) * n_col + (c ^ k)) for r in range(n_row) for c in range(n_col)
        ]
        return lax.ppermute(array, ("row", "col"), pairs_of)

    def to_chip(array, k):
        return lax.ppermute(array, "row", [(i, i ^ (2 * k + 1)) for i in range(n_row)])

    def to_core(array):
        return lax.ppermute(array, "row", [(i, i ^ 1) for i in range(n_row)])

    def to_odd_chip(array):
        both = [(0, 1), (n_row - 2, n_row - 1)]
        for i in range(2, n_row - 2, 4):
            both += [(i, i + 3), (i + 1, i + 2)]
        return lax.ppermute(array, "row", both + [(j, i) for i, j in both])

    def cells(array):
        return jnp.transpose(array, (1, 2, 0, 3))

    def turned(array):
        return jnp.transpose(array, (0, 2, 1))

    saved = pltpu.VMEM((pairs, head_dim, strip), BF16)
    tile, kv, query = call(
        pack_kernel,
        (
            held((2, rows, cols, samples, channels), BF16),
            held((pairs, strip, lanes), BF16),
            held((strip, lanes), BF16),
        ),
        (saved, saved, saved, pltpu.SemaphoreType.DMA((5,))),
        range(5),
    )(cells(out_grad), cells(pre_silu), turned(query_heads), turned(key_heads), turned(value_heads))
    tiles = [to_col(tile, k) for k in range(n_col)]

    padded = pad8(cols)
    far = (
        jnp.asarray(shift_selector(rows, cols, n_col), BF16),
        jnp.asarray(shift_selector(1, cols, n_col), BF16),
        conv_weight,
        out_weight,
    )
    loaded = call(
        load_kernel,
        [held(array.shape, BF16) for array in far],
        [pltpu.SemaphoreType.DMA((len(far),))],
        range(len(far)),
    )(*far)

    def doubled(*parts, counts=None):
        counts = counts or [part.shape[0] for part in parts]
        return call(
            functools.partial(join_kernel, counts), held((sum(counts), strip, lanes), BF16)
        )(*parts)

    distances = [chips >> (i + 1) for i in range(chips.bit_length() - 1)]
    offsets = [0]
    for distance in distances:
        offsets = offsets + [offset + distance for offset in offsets]
    tiles, received, (shifts, rim_shifts, conv_weight, out_weight) = lax.optimization_barrier(
        (tiles, to_chip(kv, distances[0]), loaded)
    )
    parts = (kv, received)
    for distance in distances[1:-1]:
        joined = doubled(*parts)
        parts = (joined, to_chip(joined, distance))

    rim = held((strip, lanes), BF16)
    blocks = sum(part.shape[0] for part in parts)
    rim_core, rim_chip, sent = call(
        functools.partial(rim_kernel, n_col, per_sample),
        (rim, rim, held((blocks + 1, strip, lanes), BF16)),
        [pltpu.VMEM((2, n_col, padded, channels), F32)],
    )(*tiles, *parts)
    received = to_chip(sent, distances[-1])
    halo_odd, halo_core = to_odd_chip(rim_chip), to_core(rim_core)

    whole = held((strip, channels), F32)
    conv, gate = call(
        functools.partial(conv_kernel, n_col, per_sample),
        (whole, whole),
        [pltpu.VMEM((n_col, rows, padded, channels), F32)] * 2,
    )(*tiles, shifts, conv_weight)
    received, conv, halo_odd, halo_core = lax.optimization_barrier(
        (received, conv, halo_odd, halo_core)
    )
    joined = doubled(sent, received, query[None], counts=(blocks, blocks, 1))
    other = to_core(joined)
    grad_z, grad_out = call(
        rim_conv_kernel,
        (held((strip, channels), BF16), held((strip, lanes), BF16)),
    )(halo_core, received, halo_odd, conv, gate, rim_shifts, conv_weight, out_weight)

    block = held((chips, pairs, strip, lanes), BF16)
    dkv_sent, dkv_kept, dq = call(
        functools.partial(attention_kernel, offsets), (block, block, held((strip, lanes), F32))
    )(joined, other, grad_out)

    sums = call(core_sum_kernel, [held((pairs, strip, lanes), BF16) for _ in range(chips)])(
        dkv_kept, to_core(dkv_sent)
    )
    parts = [to_chip(sums[k], k) for k in reversed(range(1, chips))] + [sums[0]]

    selected = tile_selector(rows, cols, n_col).reshape(n_col * rows * padded, -1)
    cut = call(
        functools.partial(project_kernel, n_col, per_sample),
        [held((rows * padded, channels), BF16)] * n_col,
        [pltpu.VMEM((n_col, rows * padded, channels), F32)],
    )(*parts, dq, grad_z, input_weight, jnp.asarray(selected, BF16))
    grad_input = call(
        functools.partial(output_kernel, per_sample),
        pltpu.HBM((rows, cols, samples, channels), BF16),
        [pltpu.VMEM((rows, cols, samples, channels), BF16), pltpu.SemaphoreType.DMA],
    )(*[to_col(cut[k], k) for k in reversed(range(n_col))])
    return jnp.transpose(grad_input, (2, 0, 1, 3))


def solution(mesh):
    tile = P(None, "row", "col", None)
    heads = P("col", "row", None)
    return jax.shard_map(
        shards,
        mesh=mesh,
        in_specs=(tile, tile, heads, heads, heads, P(), P(), P()),
        out_specs=tile,
        check_vma=False,
    )
```

```python
import functools

import jax
import jax.numpy as jnp
import numpy as np
from jax import lax
from jax.experimental import pallas as pl
from jax.experimental.pallas import tpu as pltpu
from jax.sharding import PartitionSpec as P

HEADS = 4
VMEM_BYTES = 32 * 1024 * 1024
HELD_BYTES = 3 * 512 * 1024
UNROLLED_CHUNKS = 16
F32 = jnp.float32
BF16 = jnp.bfloat16


def dot(left, right, left_dim=1, right_dim=0):
    return lax.dot_general(
        left, right, (((left_dim,), (right_dim,)), ((), ())), preferred_element_type=F32
    )


def call(kernel, out_shape, scratch=(), far=()):
    def run(*operands):
        specs = [pl.BlockSpec(memory_space=pltpu.VMEM)] * len(operands)
        operands = list(operands)
        for i, operand in enumerate(operands):
            if i in far:
                specs[i] = pl.BlockSpec(memory_space=pltpu.HBM)
                operands[i] = pltpu.with_memory_space_constraint(operand, pltpu.HBM)
            elif operand.size * operand.dtype.itemsize <= HELD_BYTES:
                operands[i] = pltpu.with_memory_space_constraint(operand, pltpu.VMEM)
        return pl.pallas_call(
            kernel,
            out_shape=out_shape,
            in_specs=specs,
            out_specs=jax.tree.map(
                lambda out: pl.BlockSpec(
                    memory_space=pltpu.HBM
                    if getattr(out, "memory_space", None) == pltpu.HBM
                    else pltpu.VMEM
                ),
                out_shape,
            ),
            scratch_shapes=list(scratch),
            compiler_params=pltpu.CompilerParams(vmem_limit_bytes=VMEM_BYTES),
        )(*operands)

    return run


def held(shape, dtype):
    small = np.prod(shape) * np.dtype(dtype).itemsize <= HELD_BYTES
    return (pltpu.VMEM if small else jax.ShapeDtypeStruct)(shape, dtype)


def pad8(amount):
    return -(-amount // 8) * 8


def shift_selector(rows, cols, tiles):
    width, padded = tiles * cols, pad8(cols)
    select = np.zeros((3, rows, width, tiles, rows, padded), np.float32)
    for shift in (-1, 0, 1):
        for j in range(max(0, shift), min(width, width + shift)):
            tile, inner = divmod(j - shift, cols)
            for i in range(rows):
                select[shift + 1, i, j, tile, i, inner] = 1
    return select.reshape(3, rows * width, tiles * rows * padded)


def tile_selector(rows, cols, tiles):
    width, padded = tiles * cols, pad8(cols)
    select = np.zeros((tiles, rows, padded, rows, width), np.float32)
    for tile in range(tiles):
        for i in range(rows):
            for inner in range(cols):
                select[tile, i, inner, i, tile * cols + inner] = 1
    return select.reshape(tiles, rows * padded, rows * width)


def start_copies(pairs, sems):
    copies = [
        pltpu.make_async_copy(src, dst, sems.at[i]) for i, (src, dst) in enumerate(pairs)
    ]
    for copy in copies:
        copy.start()
    return copies


def pack_kernel(
    out_grad, pre_silu, queries, keys, values, tile, kv, query, q_ref, k_ref, v_ref, sems
):
    copies = start_copies(
        [
            (values, v_ref),
            (keys, k_ref),
            (queries, q_ref),
            (out_grad, tile.at[0]),
            (pre_silu, tile.at[1]),
        ],
        sems,
    )

    def beside(left, right):
        return jnp.concatenate([left.astype(F32), right.astype(F32)], 0).T.astype(BF16)

    copies[0].wait()
    copies[1].wait()
    kv[0] = beside(v_ref[0], k_ref[0])
    kv[1] = beside(k_ref[1], v_ref[1])
    copies[2].wait()
    query[...] = beside(q_ref[1], q_ref[0]) * jnp.asarray(q_ref.shape[1] ** -0.5, BF16)
    copies[3].wait()
    copies[4].wait()


def rim_kernel(n_col, per_sample, *refs):
    tiles, (*parts, to_core, to_chip, joined, rims) = refs[:n_col], refs[n_col:]
    col = lax.axis_index("col")
    rows = tiles[0].shape[1]
    lanes = to_core.shape[1]
    used = rims.shape[1] * rims.shape[2]
    inner = jnp.where(lax.axis_index("row") % 2 == 1, rows - 1, 0)
    cols = tiles[0].shape[2]
    rims[...] = jnp.zeros_like(rims)
    for side, (row, out) in enumerate(((inner, to_core), (rows - 1 - inner, to_chip))):
        for k, tile in enumerate(tiles):
            rims[side, col ^ k, :cols] = pick(tile[0, row], col // per_sample)
        flat = rims[side].reshape(used, -1).astype(BF16)
        out[...] = jnp.zeros_like(out)
        for part in range(flat.shape[1] // lanes):
            out[part * used : (part + 1) * used] = flat[:, part * lanes : (part + 1) * lanes]
    join_kernel([part.shape[0] for part in parts], *parts, joined)
    joined[joined.shape[0] - 1] = to_chip[...]


def join_kernel(counts, *refs):
    *parts, out = refs
    first = 0
    for part, count in zip(parts, counts):
        for j in range(count):
            out[first + j] = part[j]
        first += count


def load_kernel(*refs):
    *copied, sems = refs
    half = len(copied) // 2
    for copy in start_copies(list(zip(copied[:half], copied[half:])), sems):
        copy.wait()


def pick(cells, sample):
    place = lax.broadcasted_iota(jnp.int32, cells.shape, 1)
    return jnp.sum(jnp.where(place == sample, cells.astype(F32), 0.0), axis=1)


def conv_kernel(n_col, per_sample, *refs):
    tiles, (shifts, conv_weight, conv_ref, gate_ref, grads, silus) = refs[:n_col], refs[n_col:]
    col = lax.axis_index("col")
    sample = col // per_sample
    _, rows, cols, _, channels = tiles[0].shape
    width = n_col * cols
    grads[...] = jnp.zeros_like(grads)
    silus[...] = jnp.zeros_like(silus)
    for k in range(n_col):
        for i in range(rows):
            grads[col ^ k, i, :cols] = pick(tiles[k][0, i], sample)
            silus[col ^ k, i, :cols] = pick(tiles[k][1, i], sample)
    flat = grads[...].reshape(-1, channels).astype(BF16)
    none = jnp.zeros((width, channels), F32)
    conv = jnp.zeros((rows * width, channels), F32)
    for b in (-1, 0, 1):
        here = dot(shifts[b + 1], flat)
        above = jnp.concatenate([none, here[:-width]], 0)
        below = jnp.concatenate([here[width:], none], 0)
        for a, window in ((-1, below), (0, here), (1, above)):
            conv = conv + dot(window.astype(BF16), conv_weight[a + 1, b + 1], 1, 1)
    conv_ref[...] = conv
    z = dot(shifts[1], silus[...].reshape(-1, channels).astype(BF16))
    sigma = 1.0 / (1.0 + jnp.exp(-z))
    gate_ref[...] = sigma * (1.0 + z * (1.0 - sigma))


def rim_conv_kernel(halo_core, halo_last, halo_odd, conv, gate, *refs):
    shifts, conv_weight, out_weight, gz_ref, go_ref = refs
    col, row = lax.axis_index("col"), lax.axis_index("row")
    core, chip = row % 2, row // 2
    strip, channels = gz_ref.shape
    lanes = go_ref.shape[1]
    per_sample = out_weight.shape[0] // lanes
    width = shifts.shape[1]
    used = shifts.shape[2]
    last = halo_last[halo_last.shape[0] - 1]
    missing = jnp.logical_or(row == 1, row == lax.axis_size("row") - 2)
    halo_chip = jnp.where(core == chip % 2, last, halo_odd[...])
    halo_chip = jnp.where(missing, jnp.zeros_like(last), halo_chip)
    inner = halo_core[...]
    parts = channels // lanes

    def spread(halo):
        return jnp.concatenate([halo[p * used : (p + 1) * used] for p in range(parts)], 1)

    rims = (
        spread(jnp.where(core == 1, halo_chip, inner)),
        spread(jnp.where(core == 1, inner, halo_chip)),
    )
    edges = []
    for flat, a in zip(rims, (1, -1)):
        edge = jnp.zeros((width, channels), F32)
        for b in (-1, 0, 1):
            window = dot(shifts[b + 1], flat).astype(BF16)
            edge = edge + dot(window, conv_weight[a + 1, b + 1], 1, 1)
        edges.append(edge)
    between = jnp.zeros((strip - 2 * width, channels), F32)
    total = conv[...] + jnp.concatenate([edges[0], between, edges[1]], 0)
    grad_z = (total * gate[...]).astype(BF16)
    gz_ref[...] = grad_z
    first = pl.multiple_of(col % per_sample * lanes, lanes)
    go_ref[...] = dot(grad_z, out_weight[pl.ds(first, lanes), :], 1, 1).astype(BF16)


def attention_kernel(offsets, kv_sent, kv_kept, go_ref, dkv_sent, dkv_kept, dq_ref):
    strip, lanes = go_ref.shape
    half = lanes // 2
    factor = half**-0.5
    low = lax.broadcasted_iota(jnp.int32, (strip, lanes), 1) < half
    query, grad_out = kv_kept[kv_kept.shape[0] - 1], go_ref[...]
    none = jnp.zeros_like(query)
    asked = (jnp.where(low, none, query), jnp.where(low, query, none))
    cotangent = (jnp.where(low, grad_out, none), jnp.where(low, none, grad_out))
    chunks = []
    for j, offset in enumerate(offsets):
        even = offset != 0 and offset.bit_count() % 2 == 0
        chunks.append((kv_sent, dkv_kept if even else dkv_sent, j, offset))
        chunks.append((kv_kept, dkv_sent if even else dkv_kept, j, offset))

    heads = (0, 1)
    if len(chunks) <= UNROLLED_CHUNKS:
        kvs = [
            jnp.concatenate([src[2 * j + h].astype(F32) for src, _, j, _ in chunks], 0).astype(BF16)
            for h in heads
        ]
        scores = [dot(kvs[h], asked[h], 1, 1) for h in heads]
        probs_grads = [dot(kvs[h], cotangent[h], 1, 1) for h in heads]
        exps = [jnp.exp(s - jnp.max(s, axis=0, keepdims=True)) for s in scores]
        scales = [1.0 / jnp.sum(e, axis=0, keepdims=True) for e in exps]
        row_dots = [
            jnp.sum(e * g, axis=0, keepdims=True) * s for e, g, s in zip(exps, probs_grads, scales)
        ]
        probs = [e * s for e, s in zip(exps, scales)]
        grad_scores = [
            (p * (g - r)).astype(BF16) for p, g, r in zip(probs, probs_grads, row_dots)
        ]
        grad_query = [dot(grad_scores[h], kvs[h], 0, 0) for h in heads]
        for h in heads:
            given = jnp.concatenate([grad_scores[h], probs[h].astype(BF16)], 1)
            dkv = dot(given, jnp.concatenate([asked[h], cotangent[h]], 0))
            for i, (_, dst, _, offset) in enumerate(chunks):
                dst[offset, h] = dkv[i * strip : (i + 1) * strip].astype(BF16)
    else:
        grad_query = []
        for head in heads:
            ask, cot = asked[head], cotangent[head]

            def gather(kv, carry):
                top, norm, weighted = carry
                scores = dot(kv, ask, 1, 1)
                new = jnp.maximum(top, jnp.max(scores, axis=0, keepdims=True))
                exps = jnp.exp(scores - new)
                rescale = jnp.exp(top - new)
                weights = jnp.sum(exps * dot(kv, cot, 1, 1), axis=0, keepdims=True)
                return (
                    new,
                    norm * rescale + jnp.sum(exps, axis=0, keepdims=True),
                    weighted * rescale + weights,
                )

            zero = jnp.zeros((1, strip), F32)
            stats = (jnp.full((1, strip), -jnp.inf, F32), zero, zero)
            for src in (kv_sent, kv_kept):
                stats = lax.fori_loop(
                    0,
                    len(offsets),
                    lambda j, carry, src=src: gather(src[2 * j + head], carry),
                    stats,
                )
            top, norm, weighted = stats
            scale = 1.0 / norm
            total = jnp.zeros((strip, lanes), F32)
            for src, dst, j, offset in chunks:
                kv = src[2 * j + head]
                probs = jnp.exp(dot(kv, ask, 1, 1) - top) * scale
                grad_scores = (probs * (dot(kv, cot, 1, 1) - weighted * scale)).astype(BF16)
                dkv = dot(grad_scores, ask) + dot(probs.astype(BF16), cot)
                dst[offset, head] = dkv.astype(BF16)
                total = total + dot(grad_scores, kv, 0, 0)
            grad_query.append(total)
    dq_ref[...] = jnp.where(low, grad_query[1], grad_query[0]) * factor


def core_sum_kernel(own, received, *outs):
    for j, out in enumerate(outs):
        out[...] = (own[j].astype(F32) + received[j].astype(F32)).astype(BF16)


def project_kernel(n_col, per_sample, *refs):
    *refs, cut = refs
    n_in = len(refs) - n_col
    *parts, dq_ref, gz_ref, input_weight, tiles = refs[:n_in]
    outs = refs[n_in:]
    col = lax.axis_index("col")
    part = col % per_sample
    total = sum(ref[...].astype(F32) for ref in parts)
    strip, lanes = dq_ref.shape
    half = lanes // 2
    channels = gz_ref.shape[1]
    low = lax.broadcasted_iota(jnp.int32, (strip, lanes), 1) < half
    dv = jnp.where(low, total[0], total[1])
    dk = pltpu.roll(jnp.where(low, total[1], total[0]), half, 1)
    dq = pltpu.roll(dq_ref[...], half, 1)
    grad = jnp.where(part == 0, gz_ref[...].astype(F32), 0.0)
    for kind, value in enumerate((dq, dk, dv)):
        first = pl.multiple_of(kind * channels + part * lanes, lanes)
        weight = input_weight[:, pl.ds(first, lanes)]
        grad = grad + dot(value.astype(BF16), weight, 1, 1)
    cut[...] = dot(tiles[...], grad.astype(BF16)).reshape(cut.shape)
    for k, out in enumerate(outs):
        out[...] = cut[col ^ k].astype(BF16)


def output_kernel(per_sample, *refs):
    *parts, far_out, out, sem = refs
    parts = parts[::-1]
    rows, cols, samples, channels = out.shape
    padded = pad8(cols)
    sample = lax.axis_index("col") // per_sample
    place = lax.broadcasted_iota(jnp.int32, (cols, samples, channels), 1)
    for i in range(rows):
        cells = jnp.zeros((cols, samples, channels), F32)
        for group in range(samples):
            total = sum(
                ref[...][i * padded : i * padded + cols].astype(F32)
                for ref in parts[group * per_sample : (group + 1) * per_sample]
            )
            cells = jnp.where(place == (sample ^ group), total[:, None, :], cells)
        out[i] = cells.astype(BF16)
    copy = pltpu.make_async_copy(out, far_out, sem)
    copy.start()
    copy.wait()


def shards(
    pre_silu, out_grad, query_heads, key_heads, value_heads, conv_weight, out_weight, input_weight
):
    samples, rows, cols, channels = pre_silu.shape
    pairs, strip, head_dim = query_heads.shape
    n_row, n_col = lax.axis_size("row"), lax.axis_size("col")
    chips = n_row // 2
    per_sample = HEADS // pairs
    lanes = pairs * head_dim

    def to_col(array, k):
        pairs_of = [
            (r * n_col + c, (r ^ 1) * n_col + (c ^ k)) for r in range(n_row) for c in range(n_col)
        ]
        return lax.ppermute(array, ("row", "col"), pairs_of)

    def to_chip(array, k):
        return lax.ppermute(array, "row", [(i, i ^ (2 * k + 1)) for i in range(n_row)])

    def to_core(array):
        return lax.ppermute(array, "row", [(i, i ^ 1) for i in range(n_row)])

    def to_odd_chip(array):
        both = [(0, 1), (n_row - 2, n_row - 1)]
        for i in range(2, n_row - 2, 4):
            both += [(i, i + 3), (i + 1, i + 2)]
        return lax.ppermute(array, "row", both + [(j, i) for i, j in both])

    def cells(array):
        return jnp.transpose(array, (1, 2, 0, 3))

    def turned(array):
        return jnp.transpose(array, (0, 2, 1))

    saved = pltpu.VMEM((pairs, head_dim, strip), BF16)
    tile, kv, query = call(
        pack_kernel,
        (
            held((2, rows, cols, samples, channels), BF16),
            held((pairs, strip, lanes), BF16),
            held((strip, lanes), BF16),
        ),
        (saved, saved, saved, pltpu.SemaphoreType.DMA((5,))),
        range(5),
    )(cells(out_grad), cells(pre_silu), turned(query_heads), turned(key_heads), turned(value_heads))
    tiles = [to_col(tile, k) for k in range(n_col)]

    padded = pad8(cols)
    far = (
        jnp.asarray(shift_selector(rows, cols, n_col), BF16),
        jnp.asarray(shift_selector(1, cols, n_col), BF16),
        conv_weight,
        out_weight,
    )
    loaded = call(
        load_kernel,
        [held(array.shape, BF16) for array in far],
        [pltpu.SemaphoreType.DMA((len(far),))],
        range(len(far)),
    )(*far)

    def doubled(*parts, counts=None):
        counts = counts or [part.shape[0] for part in parts]
        return call(
            functools.partial(join_kernel, counts), held((sum(counts), strip, lanes), BF16)
        )(*parts)

    distances = [chips >> (i + 1) for i in range(chips.bit_length() - 1)]
    offsets = [0]
    for distance in distances:
        offsets = offsets + [offset + distance for offset in offsets]
    tiles, received, (shifts, rim_shifts, conv_weight, out_weight) = lax.optimization_barrier(
        (tiles, to_chip(kv, distances[0]), loaded)
    )
    parts = (kv, received)
    for distance in distances[1:-1]:
        joined = doubled(*parts)
        parts = (joined, to_chip(joined, distance))

    rim = held((strip, lanes), BF16)
    blocks = sum(part.shape[0] for part in parts)
    rim_core, rim_chip, sent = call(
        functools.partial(rim_kernel, n_col, per_sample),
        (rim, rim, held((blocks + 1, strip, lanes), BF16)),
        [pltpu.VMEM((2, n_col, padded, channels), F32)],
    )(*tiles, *parts)
    received = to_chip(sent, distances[-1])
    halo_odd, halo_core = to_odd_chip(rim_chip), to_core(rim_core)

    whole = held((strip, channels), F32)
    conv, gate = call(
        functools.partial(conv_kernel, n_col, per_sample),
        (whole, whole),
        [pltpu.VMEM((n_col, rows, padded, channels), F32)] * 2,
    )(*tiles, shifts, conv_weight)
    received, conv, halo_odd, halo_core = lax.optimization_barrier(
        (received, conv, halo_odd, halo_core)
    )
    joined = doubled(sent, received, query[None], counts=(blocks, blocks, 1))
    other = to_core(joined)
    grad_z, grad_out = call(
        rim_conv_kernel,
        (held((strip, channels), BF16), held((strip, lanes), BF16)),
    )(halo_core, received, halo_odd, conv, gate, rim_shifts, conv_weight, out_weight)

    block = held((chips, pairs, strip, lanes), BF16)
    dkv_sent, dkv_kept, dq = call(
        functools.partial(attention_kernel, offsets), (block, block, held((strip, lanes), F32))
    )(joined, other, grad_out)

    sums = call(core_sum_kernel, [held((pairs, strip, lanes), BF16) for _ in range(chips)])(
        dkv_kept, to_core(dkv_sent)
    )
    far_near = [k for pair in zip(range(chips - 1, 0, -1), range(1, chips)) for k in pair]
    order = list(dict.fromkeys(far_near))
    parts = [to_chip(sums[k], k) for k in order] + [sums[0]]

    selected = tile_selector(rows, cols, n_col).reshape(n_col * rows * padded, -1)
    cut = call(
        functools.partial(project_kernel, n_col, per_sample),
        [held((rows * padded, channels), BF16)] * n_col,
        [pltpu.VMEM((n_col, rows * padded, channels), F32)],
    )(*parts, dq, grad_z, input_weight, jnp.asarray(selected, BF16))
    grad_input = call(
        functools.partial(output_kernel, per_sample),
        pltpu.HBM((rows, cols, samples, channels), BF16),
        [pltpu.VMEM((rows, cols, samples, channels), BF16), pltpu.SemaphoreType.DMA],
    )(*[to_col(cut[k], k) for k in reversed(range(n_col))])
    return jnp.transpose(grad_input, (2, 0, 1, 3))


def solution(mesh):
    tile = P(None, "row", "col", None)
    heads = P("col", "row", None)
    return jax.shard_map(
        shards,
        mesh=mesh,
        in_specs=(tile, tile, heads, heads, heads, P(), P(), P()),
        out_specs=tile,
        check_vma=False,
    )
```

```python
import functools

import jax
import jax.numpy as jnp
import numpy as np
from jax import lax
from jax.experimental import pallas as pl
from jax.experimental.pallas import tpu as pltpu
from jax.sharding import PartitionSpec as P

HEADS = 4
VMEM_BYTES = 32 * 1024 * 1024
HELD_BYTES = 3 * 512 * 1024
UNROLLED_CHUNKS = 16
F32 = jnp.float32
BF16 = jnp.bfloat16


def dot(left, right, left_dim=1, right_dim=0):
    return lax.dot_general(
        left, right, (((left_dim,), (right_dim,)), ((), ())), preferred_element_type=F32
    )


def call(kernel, out_shape, scratch=(), far=()):
    def run(*operands):
        specs = [pl.BlockSpec(memory_space=pltpu.VMEM)] * len(operands)
        operands = list(operands)
        for i, operand in enumerate(operands):
            if i in far:
                specs[i] = pl.BlockSpec(memory_space=pltpu.HBM)
                operands[i] = pltpu.with_memory_space_constraint(operand, pltpu.HBM)
            elif operand.size * operand.dtype.itemsize <= HELD_BYTES:
                operands[i] = pltpu.with_memory_space_constraint(operand, pltpu.VMEM)
        return pl.pallas_call(
            kernel,
            out_shape=out_shape,
            in_specs=specs,
            out_specs=jax.tree.map(
                lambda out: pl.BlockSpec(
                    memory_space=pltpu.HBM
                    if getattr(out, "memory_space", None) == pltpu.HBM
                    else pltpu.VMEM
                ),
                out_shape,
            ),
            scratch_shapes=list(scratch),
            compiler_params=pltpu.CompilerParams(vmem_limit_bytes=VMEM_BYTES),
        )(*operands)

    return run


def held(shape, dtype):
    small = np.prod(shape) * np.dtype(dtype).itemsize <= HELD_BYTES
    return (pltpu.VMEM if small else jax.ShapeDtypeStruct)(shape, dtype)


def pad8(amount):
    return -(-amount // 8) * 8


def shift_selector(rows, cols, tiles):
    width, padded = tiles * cols, pad8(cols)
    select = np.zeros((3, rows, width, tiles, rows, padded), np.float32)
    for shift in (-1, 0, 1):
        for j in range(max(0, shift), min(width, width + shift)):
            tile, inner = divmod(j - shift, cols)
            for i in range(rows):
                select[shift + 1, i, j, tile, i, inner] = 1
    return select.reshape(3, rows * width, tiles * rows * padded)


def tile_selector(rows, cols, tiles):
    width, padded = tiles * cols, pad8(cols)
    select = np.zeros((tiles, rows, padded, rows, width), np.float32)
    for tile in range(tiles):
        for i in range(rows):
            for inner in range(cols):
                select[tile, i, inner, i, tile * cols + inner] = 1
    return select.reshape(tiles, rows * padded, rows * width)


def start_copies(pairs, sems):
    copies = [
        pltpu.make_async_copy(src, dst, sems.at[i]) for i, (src, dst) in enumerate(pairs)
    ]
    for copy in copies:
        copy.start()
    return copies


def pack_kernel(
    out_grad, pre_silu, queries, keys, values, tile, kv, query, q_ref, k_ref, v_ref, sems
):
    copies = start_copies(
        [
            (values, v_ref),
            (keys, k_ref),
            (queries, q_ref),
            (out_grad, tile.at[0]),
            (pre_silu, tile.at[1]),
        ],
        sems,
    )

    def beside(left, right):
        return jnp.concatenate([left.astype(F32), right.astype(F32)], 0).T.astype(BF16)

    copies[0].wait()
    copies[1].wait()
    kv[0] = beside(v_ref[0], k_ref[0])
    kv[1] = beside(k_ref[1], v_ref[1])
    copies[2].wait()
    query[...] = beside(q_ref[1], q_ref[0]) * jnp.asarray(q_ref.shape[1] ** -0.5, BF16)
    copies[3].wait()
    copies[4].wait()


def rim_kernel(n_col, per_sample, *refs):
    tiles, (*parts, query, to_core, to_chip, joined, rims) = refs[:n_col], refs[n_col:]
    col = lax.axis_index("col")
    rows = tiles[0].shape[1]
    lanes = to_chip.shape[1]
    used = rims.shape[1] * rims.shape[2]
    inner = jnp.where(lax.axis_index("row") % 2 == 1, rows - 1, 0)
    cols = tiles[0].shape[2]
    rims[...] = jnp.zeros_like(rims)
    to_core[1] = query[...]
    for side, (row, out) in enumerate(((inner, to_core.at[0]), (rows - 1 - inner, to_chip))):
        for k, tile in enumerate(tiles):
            rims[side, col ^ k, :cols] = pick(tile[0, row], col // per_sample)
        flat = rims[side].reshape(used, -1).astype(BF16)
        out[...] = jnp.zeros_like(out)
        for part in range(flat.shape[1] // lanes):
            out[part * used : (part + 1) * used] = flat[:, part * lanes : (part + 1) * lanes]
    join_kernel([part.shape[0] for part in parts], *parts, joined)
    joined[joined.shape[0] - 1] = to_chip[...]


def join_kernel(counts, *refs):
    *parts, out = refs
    first = 0
    for part, count in zip(parts, counts):
        for j in range(count):
            out[first + j] = part[j]
        first += count


def load_kernel(*refs):
    *copied, sems = refs
    half = len(copied) // 2
    for copy in start_copies(list(zip(copied[:half], copied[half:])), sems):
        copy.wait()


def pick(cells, sample):
    place = lax.broadcasted_iota(jnp.int32, cells.shape, 1)
    return jnp.sum(jnp.where(place == sample, cells.astype(F32), 0.0), axis=1)


def conv_kernel(n_col, per_sample, *refs):
    tiles, (shifts, conv_weight, conv_ref, gate_ref, grads, silus) = refs[:n_col], refs[n_col:]
    col = lax.axis_index("col")
    sample = col // per_sample
    _, rows, cols, _, channels = tiles[0].shape
    width = n_col * cols
    grads[...] = jnp.zeros_like(grads)
    silus[...] = jnp.zeros_like(silus)
    for k in range(n_col):
        for i in range(rows):
            grads[col ^ k, i, :cols] = pick(tiles[k][0, i], sample)
            silus[col ^ k, i, :cols] = pick(tiles[k][1, i], sample)
    flat = grads[...].reshape(-1, channels).astype(BF16)
    none = jnp.zeros((width, channels), F32)
    conv = jnp.zeros((rows * width, channels), F32)
    for b in (-1, 0, 1):
        here = dot(shifts[b + 1], flat)
        above = jnp.concatenate([none, here[:-width]], 0)
        below = jnp.concatenate([here[width:], none], 0)
        for a, window in ((-1, below), (0, here), (1, above)):
            conv = conv + dot(window.astype(BF16), conv_weight[a + 1, b + 1], 1, 1)
    conv_ref[...] = conv
    z = dot(shifts[1], silus[...].reshape(-1, channels).astype(BF16))
    sigma = 1.0 / (1.0 + jnp.exp(-z))
    gate_ref[...] = sigma * (1.0 + z * (1.0 - sigma))


def rim_conv_kernel(halo_core, halo_last, halo_odd, conv, gate, *refs):
    shifts, conv_weight, out_weight, gz_ref, go_ref = refs
    col, row = lax.axis_index("col"), lax.axis_index("row")
    core, chip = row % 2, row // 2
    strip, channels = gz_ref.shape
    lanes = go_ref.shape[1]
    per_sample = out_weight.shape[0] // lanes
    width = shifts.shape[1]
    used = shifts.shape[2]
    last = halo_last[halo_last.shape[0] - 1]
    missing = jnp.logical_or(row == 1, row == lax.axis_size("row") - 2)
    halo_chip = jnp.where(core == chip % 2, last, halo_odd[...])
    halo_chip = jnp.where(missing, jnp.zeros_like(last), halo_chip)
    inner = halo_core[0]
    parts = channels // lanes

    def spread(halo):
        return jnp.concatenate([halo[p * used : (p + 1) * used] for p in range(parts)], 1)

    rims = (
        spread(jnp.where(core == 1, halo_chip, inner)),
        spread(jnp.where(core == 1, inner, halo_chip)),
    )
    edges = []
    for flat, a in zip(rims, (1, -1)):
        edge = jnp.zeros((width, channels), F32)
        for b in (-1, 0, 1):
            window = dot(shifts[b + 1], flat).astype(BF16)
            edge = edge + dot(window, conv_weight[a + 1, b + 1], 1, 1)
        edges.append(edge)
    between = jnp.zeros((strip - 2 * width, channels), F32)
    total = conv[...] + jnp.concatenate([edges[0], between, edges[1]], 0)
    grad_z = (total * gate[...]).astype(BF16)
    gz_ref[...] = grad_z
    first = pl.multiple_of(col % per_sample * lanes, lanes)
    go_ref[...] = dot(grad_z, out_weight[pl.ds(first, lanes), :], 1, 1).astype(BF16)


def by_head(query, grad_out):
    low = lax.broadcasted_iota(jnp.int32, query.shape, 1) < query.shape[1] // 2
    none = jnp.zeros_like(query)
    asked = (jnp.where(low, none, query), jnp.where(low, query, none))
    return asked, (jnp.where(low, grad_out, none), jnp.where(low, none, grad_out))


def chunks_of(offsets):
    even = [offset != 0 and offset.bit_count() % 2 == 0 for offset in offsets]
    sent = [(e, j, offset) for j, (e, offset) in enumerate(zip(even, offsets))]
    return sent, [(not e, j, offset) for e, j, offset in sent]


def all_keys(kv, head):
    return jnp.concatenate(
        [kv[2 * j + head].astype(F32) for j in range(kv.shape[0] // 2)], 0
    ).astype(BF16)


def score_kernel(kv, asker, grad_out, scores, probs_grads):
    asked, cotangent = by_head(asker[1], grad_out[...])
    for head in (0, 1):
        keys = all_keys(kv, head)
        scores[head] = dot(keys, asked[head], 1, 1)
        probs_grads[head] = dot(keys, cotangent[head], 1, 1)


def softmax_kernel(offsets, kv_kept, asker, grad_out, scores, probs_grads, *outs):
    dkv_sent, grad_scores, kept_probs = outs
    strip = grad_out.shape[0]
    heads = (0, 1)
    asked, cotangent = by_head(asker[1], grad_out[...])
    sent, kept = chunks_of(offsets)

    def arranged(first, second):
        return jnp.concatenate(
            [
                (second if late else first)[j * strip : (j + 1) * strip]
                for late, j, _ in sent + kept
            ],
            0,
        )

    keys = [all_keys(kv_kept, h) for h in heads]
    late_scores = [dot(keys[h], asked[h], 1, 1) for h in heads]
    late_grads = [dot(keys[h], cotangent[h], 1, 1) for h in heads]
    both = [arranged(scores[h], late_scores[h]) for h in heads]
    grads = [arranged(probs_grads[h], late_grads[h]) for h in heads]
    exps = [jnp.exp(x - jnp.max(x, axis=0, keepdims=True)) for x in both]
    scales = [1.0 / jnp.sum(e, axis=0, keepdims=True) for e in exps]
    row_dots = [jnp.sum(e * g, axis=0, keepdims=True) * s for e, g, s in zip(exps, grads, scales)]
    probs = [(e * s) for e, s in zip(exps, scales)]
    middle = len(sent) * strip
    for h in heads:
        grad = (probs[h] * (grads[h] - row_dots[h])).astype(BF16)
        grad_scores[h] = grad
        rounded = probs[h].astype(BF16)
        kept_probs[h] = rounded[middle:]
        given = jnp.concatenate([grad[:middle], rounded[:middle]], 1)
        dkv = dot(given, jnp.concatenate([asked[h], cotangent[h]], 0))
        for i, (_, _, offset) in enumerate(sent):
            dkv_sent[offset, h] = dkv[i * strip : (i + 1) * strip].astype(BF16)


def base(dq, gz_ref, input_weight):
    strip, lanes = dq.shape
    part = lax.axis_index("col") % (gz_ref.shape[1] // lanes)
    first = pl.multiple_of(part * lanes, lanes)
    grad = jnp.where(part == 0, gz_ref[...].astype(F32), 0.0)
    query = pltpu.roll(dq * (lanes // 2) ** -0.5, lanes // 2, 1).astype(BF16)
    return grad + dot(query, input_weight[:, pl.ds(first, lanes)], 1, 1)


def finish_kernel(offsets, *refs):
    kv_sent, kv_kept, asker, grad_out, grad_scores, kept_probs, gz_ref, input_weight = refs[:8]
    dkv_kept, base_ref = refs[8:]
    strip, lanes = grad_out.shape
    asked, cotangent = by_head(asker[1], grad_out[...])
    sent, kept = chunks_of(offsets)
    middle = len(sent) * strip
    query = []
    for h in (0, 1):
        given = jnp.concatenate([grad_scores[h, middle:], kept_probs[h]], 1)
        dkv = dot(given, jnp.concatenate([asked[h], cotangent[h]], 0))
        for i, (_, _, offset) in enumerate(kept):
            dkv_kept[offset, h] = dkv[i * strip : (i + 1) * strip].astype(BF16)
        keys = jnp.concatenate(
            [(kv_kept if late else kv_sent)[2 * j + h].astype(F32) for late, j, _ in sent + kept], 0
        )
        query.append(dot(grad_scores[h], keys.astype(BF16), 0, 0))
    low = lax.broadcasted_iota(jnp.int32, (strip, lanes), 1) < lanes // 2
    base_ref[...] = base(jnp.where(low, query[1], query[0]), gz_ref, input_weight)


def long_kernel(offsets, *refs):
    kv_sent, kv_kept, asker, grad_out, gz_ref, input_weight, dkv_sent, dkv_kept, base_ref = refs
    strip, lanes = grad_out.shape
    asked, cotangent = by_head(asker[1], grad_out[...])
    sent, kept = chunks_of(offsets)
    query = []
    for head in (0, 1):
        ask, cot = asked[head], cotangent[head]

        def gather(kv, carry):
            top, norm, weighted = carry
            scores = dot(kv, ask, 1, 1)
            new = jnp.maximum(top, jnp.max(scores, axis=0, keepdims=True))
            exps = jnp.exp(scores - new)
            rescale = jnp.exp(top - new)
            weights = jnp.sum(exps * dot(kv, cot, 1, 1), axis=0, keepdims=True)
            return (
                new,
                norm * rescale + jnp.sum(exps, axis=0, keepdims=True),
                weighted * rescale + weights,
            )

        zero = jnp.zeros((1, strip), F32)
        stats = (jnp.full((1, strip), -jnp.inf, F32), zero, zero)
        for src in (kv_sent, kv_kept):
            stats = lax.fori_loop(
                0,
                len(offsets),
                lambda j, carry, src=src: gather(src[2 * j + head], carry),
                stats,
            )
        top, norm, weighted = stats
        scale = 1.0 / norm
        total = jnp.zeros((strip, lanes), F32)
        for dst, chunks in ((dkv_sent, sent), (dkv_kept, kept)):
            for late, j, offset in chunks:
                kv = (kv_kept if late else kv_sent)[2 * j + head]
                probs = jnp.exp(dot(kv, ask, 1, 1) - top) * scale
                grad_scores = (probs * (dot(kv, cot, 1, 1) - weighted * scale)).astype(BF16)
                dkv = dot(grad_scores, ask) + dot(probs.astype(BF16), cot)
                dst[offset, head] = dkv.astype(BF16)
                total = total + dot(grad_scores, kv, 0, 0)
        query.append(total)
    low = lax.broadcasted_iota(jnp.int32, (strip, lanes), 1) < lanes // 2
    base_ref[...] = base(jnp.where(low, query[1], query[0]), gz_ref, input_weight)


def core_sum_kernel(own, received, *outs):
    for j, out in enumerate(outs):
        out[...] = (own[j].astype(F32) + received[j].astype(F32)).astype(BF16)


def project_kernel(n_col, per_sample, *refs):
    *refs, cut = refs
    n_in = len(refs) - n_col
    *parts, base_ref, input_weight, tiles = refs[:n_in]
    outs = refs[n_in:]
    col = lax.axis_index("col")
    part = col % per_sample
    total = sum(ref[...].astype(F32) for ref in parts)
    _, strip, lanes = parts[0].shape
    half = lanes // 2
    channels = base_ref.shape[1]
    low = lax.broadcasted_iota(jnp.int32, (strip, lanes), 1) < half
    dv = jnp.where(low, total[0], total[1])
    dk = pltpu.roll(jnp.where(low, total[1], total[0]), half, 1)
    grad = base_ref[...]
    for kind, value in ((1, dk), (2, dv)):
        first = pl.multiple_of(kind * channels + part * lanes, lanes)
        weight = input_weight[:, pl.ds(first, lanes)]
        grad = grad + dot(value.astype(BF16), weight, 1, 1)
    cut[...] = dot(tiles[...], grad.astype(BF16)).reshape(cut.shape)
    for k, out in enumerate(outs):
        out[...] = cut[col ^ k].astype(BF16)


def output_kernel(per_sample, *refs):
    *parts, far_out, out, sem = refs
    parts = parts[::-1]
    rows, cols, samples, channels = out.shape
    padded = pad8(cols)
    sample = lax.axis_index("col") // per_sample
    place = lax.broadcasted_iota(jnp.int32, (cols, samples, channels), 1)
    for i in range(rows):
        cells = jnp.zeros((cols, samples, channels), F32)
        for group in range(samples):
            total = sum(
                ref[...][i * padded : i * padded + cols].astype(F32)
                for ref in parts[group * per_sample : (group + 1) * per_sample]
            )
            cells = jnp.where(place == (sample ^ group), total[:, None, :], cells)
        out[i] = cells.astype(BF16)
    copy = pltpu.make_async_copy(out, far_out, sem)
    copy.start()
    copy.wait()


def shards(
    pre_silu, out_grad, query_heads, key_heads, value_heads, conv_weight, out_weight, input_weight
):
    samples, rows, cols, channels = pre_silu.shape
    pairs, strip, head_dim = query_heads.shape
    n_row, n_col = lax.axis_size("row"), lax.axis_size("col")
    chips = n_row // 2
    per_sample = HEADS // pairs
    lanes = pairs * head_dim

    def to_col(array, k):
        pairs_of = [
            (r * n_col + c, (r ^ 1) * n_col + (c ^ k)) for r in range(n_row) for c in range(n_col)
        ]
        return lax.ppermute(array, ("row", "col"), pairs_of)

    def to_chip(array, k):
        return lax.ppermute(array, "row", [(i, i ^ (2 * k + 1)) for i in range(n_row)])

    def to_core(array):
        return lax.ppermute(array, "row", [(i, i ^ 1) for i in range(n_row)])

    def to_odd_chip(array):
        both = [(0, 1), (n_row - 2, n_row - 1)]
        for i in range(2, n_row - 2, 4):
            both += [(i, i + 3), (i + 1, i + 2)]
        return lax.ppermute(array, "row", both + [(j, i) for i, j in both])

    def cells(array):
        return jnp.transpose(array, (1, 2, 0, 3))

    def turned(array):
        return jnp.transpose(array, (0, 2, 1))

    saved = pltpu.VMEM((pairs, head_dim, strip), BF16)
    tile, kv, query = call(
        pack_kernel,
        (
            held((2, rows, cols, samples, channels), BF16),
            held((pairs, strip, lanes), BF16),
            held((strip, lanes), BF16),
        ),
        (saved, saved, saved, pltpu.SemaphoreType.DMA((5,))),
        range(5),
    )(cells(out_grad), cells(pre_silu), turned(query_heads), turned(key_heads), turned(value_heads))
    tiles = [to_col(tile, k) for k in range(n_col)]

    padded = pad8(cols)
    far = (
        jnp.asarray(shift_selector(rows, cols, n_col), BF16),
        jnp.asarray(shift_selector(1, cols, n_col), BF16),
        conv_weight,
        out_weight,
    )
    loaded = call(
        load_kernel,
        [held(array.shape, BF16) for array in far],
        [pltpu.SemaphoreType.DMA((len(far),))],
        range(len(far)),
    )(*far)

    def doubled(*parts, counts=None):
        counts = counts or [part.shape[0] for part in parts]
        return call(
            functools.partial(join_kernel, counts), held((sum(counts), strip, lanes), BF16)
        )(*parts)

    distances = [chips >> (i + 1) for i in range(chips.bit_length() - 1)]
    offsets = [0]
    for distance in distances:
        offsets = offsets + [offset + distance for offset in offsets]
    tiles, received, (shifts, rim_shifts, conv_weight, out_weight) = lax.optimization_barrier(
        (tiles, to_chip(kv, distances[0]), loaded)
    )
    parts = (kv, received)
    for distance in distances[1:-1]:
        joined = doubled(*parts)
        parts = (joined, to_chip(joined, distance))

    rim = held((strip, lanes), BF16)
    blocks = sum(part.shape[0] for part in parts)
    rim_core, rim_chip, sent = call(
        functools.partial(rim_kernel, n_col, per_sample),
        (held((2, strip, lanes), BF16), rim, held((blocks + 1, strip, lanes), BF16)),
        [pltpu.VMEM((2, n_col, padded, channels), F32)],
    )(*tiles, *parts, query)
    received = to_chip(sent, distances[-1])
    halo_odd, halo_core = to_odd_chip(rim_chip), to_core(rim_core)

    whole = held((strip, channels), F32)
    conv, gate = call(
        functools.partial(conv_kernel, n_col, per_sample),
        (whole, whole),
        [pltpu.VMEM((n_col, rows, padded, channels), F32)] * 2,
    )(*tiles, shifts, conv_weight)
    received, conv, halo_odd, halo_core = lax.optimization_barrier(
        (received, conv, halo_odd, halo_core)
    )
    joined = doubled(sent, received, counts=(blocks, blocks))
    other = to_core(joined)
    grad_z, grad_out = call(
        rim_conv_kernel,
        (held((strip, channels), BF16), held((strip, lanes), BF16)),
    )(halo_core, received, halo_odd, conv, gate, rim_shifts, conv_weight, out_weight)

    block = held((chips, pairs, strip, lanes), BF16)
    if 2 * chips <= UNROLLED_CHUNKS:
        half = held((pairs, chips * strip, strip), F32)
        scores, probs_grads = call(score_kernel, (half, half))(joined, halo_core, grad_out)
        dkv_sent, grad_scores, kept_probs = call(
            functools.partial(softmax_kernel, offsets),
            (
                block,
                held((pairs, 2 * chips * strip, strip), BF16),
                held((pairs, chips * strip, strip), BF16),
            ),
        )(other, halo_core, grad_out, scores, probs_grads)
        from_core = to_core(dkv_sent)
        dkv_kept, complete = call(functools.partial(finish_kernel, offsets), (block, whole))(
            joined, other, halo_core, grad_out, grad_scores, kept_probs, grad_z, input_weight
        )
    else:
        dkv_sent, dkv_kept, complete = call(
            functools.partial(long_kernel, offsets), (block, block, whole)
        )(joined, other, halo_core, grad_out, grad_z, input_weight)
        from_core = to_core(dkv_sent)

    sums = call(core_sum_kernel, [held((pairs, strip, lanes), BF16) for _ in range(chips)])(
        dkv_kept, from_core
    )
    far_near = [k for pair in zip(range(chips - 1, 0, -1), range(1, chips)) for k in pair]
    order = list(dict.fromkeys(far_near))
    parts = [to_chip(sums[k], k) for k in order] + [sums[0]]

    selected = tile_selector(rows, cols, n_col).reshape(n_col * rows * padded, -1)
    cut = call(
        functools.partial(project_kernel, n_col, per_sample),
        [held((rows * padded, channels), BF16)] * n_col,
        [pltpu.VMEM((n_col, rows * padded, channels), F32)],
    )(*parts, complete, input_weight, jnp.asarray(selected, BF16))
    grad_input = call(
        functools.partial(output_kernel, per_sample),
        pltpu.HBM((rows, cols, samples, channels), BF16),
        [pltpu.VMEM((rows, cols, samples, channels), BF16), pltpu.SemaphoreType.DMA],
    )(*[to_col(cut[k], k) for k in reversed(range(n_col))])
    return jnp.transpose(grad_input, (2, 0, 1, 3))


def solution(mesh):
    tile = P(None, "row", "col", None)
    heads = P("col", "row", None)
    return jax.shard_map(
        shards,
        mesh=mesh,
        in_specs=(tile, tile, heads, heads, heads, P(), P(), P()),
        out_specs=tile,
        check_vma=False,
    )
```

```python
import functools

import jax
import jax.numpy as jnp
import numpy as np
from jax import lax
from jax.experimental import pallas as pl
from jax.experimental.pallas import tpu as pltpu
from jax.sharding import PartitionSpec as P

HEADS = 4
VMEM_BYTES = 32 * 1024 * 1024
HELD_BYTES = 3 * 512 * 1024
UNROLLED_CHUNKS = 16
F32 = jnp.float32
BF16 = jnp.bfloat16


def dot(left, right, left_dim=1, right_dim=0):
    return lax.dot_general(
        left, right, (((left_dim,), (right_dim,)), ((), ())), preferred_element_type=F32
    )


def call(kernel, out_shape, scratch=(), far=()):
    def run(*operands):
        specs = [pl.BlockSpec(memory_space=pltpu.VMEM)] * len(operands)
        operands = list(operands)
        for i, operand in enumerate(operands):
            if i in far:
                specs[i] = pl.BlockSpec(memory_space=pltpu.HBM)
                operands[i] = pltpu.with_memory_space_constraint(operand, pltpu.HBM)
            elif operand.size * operand.dtype.itemsize <= HELD_BYTES:
                operands[i] = pltpu.with_memory_space_constraint(operand, pltpu.VMEM)
        return pl.pallas_call(
            kernel,
            out_shape=out_shape,
            in_specs=specs,
            out_specs=jax.tree.map(
                lambda out: pl.BlockSpec(
                    memory_space=pltpu.HBM
                    if getattr(out, "memory_space", None) == pltpu.HBM
                    else pltpu.VMEM
                ),
                out_shape,
            ),
            scratch_shapes=list(scratch),
            compiler_params=pltpu.CompilerParams(vmem_limit_bytes=VMEM_BYTES),
        )(*operands)

    return run


def held(shape, dtype):
    small = np.prod(shape) * np.dtype(dtype).itemsize <= HELD_BYTES
    return (pltpu.VMEM if small else jax.ShapeDtypeStruct)(shape, dtype)


def pad8(amount):
    return -(-amount // 8) * 8


def shift_selector(rows, cols, tiles):
    width, padded = tiles * cols, pad8(cols)
    select = np.zeros((3, rows, width, tiles, rows, padded), np.float32)
    for shift in (-1, 0, 1):
        for j in range(max(0, shift), min(width, width + shift)):
            tile, inner = divmod(j - shift, cols)
            for i in range(rows):
                select[shift + 1, i, j, tile, i, inner] = 1
    return select.reshape(3, rows * width, tiles * rows * padded)


def tile_selector(rows, cols, tiles):
    width, padded = tiles * cols, pad8(cols)
    select = np.zeros((tiles, rows, padded, rows, width), np.float32)
    for tile in range(tiles):
        for i in range(rows):
            for inner in range(cols):
                select[tile, i, inner, i, tile * cols + inner] = 1
    return select.reshape(tiles, rows * padded, rows * width)


def start_copies(pairs, sems):
    copies = [
        pltpu.make_async_copy(src, dst, sems.at[i]) for i, (src, dst) in enumerate(pairs)
    ]
    for copy in copies:
        copy.start()
    return copies


def beside(left, right):
    return jnp.concatenate([left.astype(F32), right.astype(F32)], 0).T.astype(BF16)


def pack_kernel(out_grad, pre_silu, keys, values, tile, kv, k_ref, v_ref, sems):
    copies = start_copies(
        [
            (values, v_ref),
            (keys, k_ref),
            (out_grad, tile.at[0]),
            (pre_silu, tile.at[1]),
        ],
        sems,
    )
    copies[0].wait()
    copies[1].wait()
    kv[0] = beside(v_ref[0], k_ref[0])
    kv[1] = beside(k_ref[1], v_ref[1])
    copies[2].wait()
    copies[3].wait()


def rim_kernel(n_col, per_sample, *refs):
    tiles, (*parts, query, to_core, to_chip, joined, rims) = refs[:n_col], refs[n_col:]
    col = lax.axis_index("col")
    rows = tiles[0].shape[1]
    lanes = to_chip.shape[1]
    used = rims.shape[1] * rims.shape[2]
    inner = jnp.where(lax.axis_index("row") % 2 == 1, rows - 1, 0)
    cols = tiles[0].shape[2]
    rims[...] = jnp.zeros_like(rims)
    to_core[1] = query[...]
    for side, (row, out) in enumerate(((inner, to_core.at[0]), (rows - 1 - inner, to_chip))):
        for k, tile in enumerate(tiles):
            rims[side, col ^ k, :cols] = pick(tile[0, row], col // per_sample)
        flat = rims[side].reshape(used, -1).astype(BF16)
        out[...] = jnp.zeros_like(out)
        for part in range(flat.shape[1] // lanes):
            out[part * used : (part + 1) * used] = flat[:, part * lanes : (part + 1) * lanes]
    join_kernel([part.shape[0] for part in parts], *parts, joined)
    joined[joined.shape[0] - 1] = to_chip[...]


def join_kernel(counts, *refs):
    *parts, out = refs
    first = 0
    for part, count in zip(parts, counts):
        for j in range(count):
            out[first + j] = part[j]
        first += count


def load_kernel(queries, *refs):
    *copied, query, q_ref, sems = refs
    half = len(copied) // 2
    copies = start_copies([(queries, q_ref), *zip(copied[:half], copied[half:])], sems)
    copies[0].wait()
    query[...] = beside(q_ref[1], q_ref[0]) * jnp.asarray(q_ref.shape[1] ** -0.5, BF16)
    for copy in copies[1:]:
        copy.wait()


def pick(cells, sample):
    place = lax.broadcasted_iota(jnp.int32, cells.shape, 1)
    return jnp.sum(jnp.where(place == sample, cells.astype(F32), 0.0), axis=1)


def conv_kernel(n_col, per_sample, *refs):
    tiles, (shifts, conv_weight, conv_ref, gate_ref, grads, silus) = refs[:n_col], refs[n_col:]
    col = lax.axis_index("col")
    sample = col // per_sample
    _, rows, cols, _, channels = tiles[0].shape
    width = n_col * cols
    grads[...] = jnp.zeros_like(grads)
    silus[...] = jnp.zeros_like(silus)
    for k in range(n_col):
        for i in range(rows):
            grads[col ^ k, i, :cols] = pick(tiles[k][0, i], sample)
            silus[col ^ k, i, :cols] = pick(tiles[k][1, i], sample)
    flat = grads[...].reshape(-1, channels).astype(BF16)
    none = jnp.zeros((width, channels), F32)
    conv = jnp.zeros((rows * width, channels), F32)
    for b in (-1, 0, 1):
        here = dot(shifts[b + 1], flat)
        above = jnp.concatenate([none, here[:-width]], 0)
        below = jnp.concatenate([here[width:], none], 0)
        for a, window in ((-1, below), (0, here), (1, above)):
            conv = conv + dot(window.astype(BF16), conv_weight[a + 1, b + 1], 1, 1)
    conv_ref[...] = conv
    z = dot(shifts[1], silus[...].reshape(-1, channels).astype(BF16))
    sigma = 1.0 / (1.0 + jnp.exp(-z))
    gate_ref[...] = sigma * (1.0 + z * (1.0 - sigma))


def rim_conv_kernel(halo_core, halo_last, halo_odd, conv, gate, *refs):
    shifts, conv_weight, out_weight, gz_ref, go_ref = refs
    col, row = lax.axis_index("col"), lax.axis_index("row")
    core, chip = row % 2, row // 2
    strip, channels = gz_ref.shape
    lanes = go_ref.shape[1]
    per_sample = out_weight.shape[0] // lanes
    width = shifts.shape[1]
    used = shifts.shape[2]
    last = halo_last[halo_last.shape[0] - 1]
    missing = jnp.logical_or(row == 1, row == lax.axis_size("row") - 2)
    halo_chip = jnp.where(core == chip % 2, last, halo_odd[...])
    halo_chip = jnp.where(missing, jnp.zeros_like(last), halo_chip)
    inner = halo_core[0]
    parts = channels // lanes

    def spread(halo):
        return jnp.concatenate([halo[p * used : (p + 1) * used] for p in range(parts)], 1)

    rims = (
        spread(jnp.where(core == 1, halo_chip, inner)),
        spread(jnp.where(core == 1, inner, halo_chip)),
    )
    edges = []
    for flat, a in zip(rims, (1, -1)):
        edge = jnp.zeros((width, channels), F32)
        for b in (-1, 0, 1):
            window = dot(shifts[b + 1], flat).astype(BF16)
            edge = edge + dot(window, conv_weight[a + 1, b + 1], 1, 1)
        edges.append(edge)
    between = jnp.zeros((strip - 2 * width, channels), F32)
    total = conv[...] + jnp.concatenate([edges[0], between, edges[1]], 0)
    grad_z = (total * gate[...]).astype(BF16)
    gz_ref[...] = grad_z
    first = pl.multiple_of(col % per_sample * lanes, lanes)
    go_ref[...] = dot(grad_z, out_weight[pl.ds(first, lanes), :], 1, 1).astype(BF16)


def by_head(query, grad_out):
    low = lax.broadcasted_iota(jnp.int32, query.shape, 1) < query.shape[1] // 2
    none = jnp.zeros_like(query)
    asked = (jnp.where(low, none, query), jnp.where(low, query, none))
    return asked, (jnp.where(low, grad_out, none), jnp.where(low, none, grad_out))


def chunks_of(offsets):
    even = [offset != 0 and offset.bit_count() % 2 == 0 for offset in offsets]
    sent = [(e, j, offset) for j, (e, offset) in enumerate(zip(even, offsets))]
    return sent, [(not e, j, offset) for e, j, offset in sent]


def all_keys(kv, head):
    return jnp.concatenate(
        [kv[2 * j + head].astype(F32) for j in range(kv.shape[0] // 2)], 0
    ).astype(BF16)


def score_kernel(kv, asker, grad_out, scores, probs_grads):
    asked, cotangent = by_head(asker[1], grad_out[...])
    for head in (0, 1):
        keys = all_keys(kv, head)
        scores[head] = dot(keys, asked[head], 1, 1)
        probs_grads[head] = dot(keys, cotangent[head], 1, 1)


def softmax_kernel(offsets, kv_kept, asker, grad_out, scores, probs_grads, *outs):
    dkv_sent, grad_scores, kept_probs = outs
    strip = grad_out.shape[0]
    heads = (0, 1)
    asked, cotangent = by_head(asker[1], grad_out[...])
    sent, kept = chunks_of(offsets)

    def arranged(first, second):
        return jnp.concatenate(
            [
                (second if late else first)[j * strip : (j + 1) * strip]
                for late, j, _ in sent + kept
            ],
            0,
        )

    keys = [all_keys(kv_kept, h) for h in heads]
    late_scores = [dot(keys[h], asked[h], 1, 1) for h in heads]
    late_grads = [dot(keys[h], cotangent[h], 1, 1) for h in heads]
    both = [arranged(scores[h], late_scores[h]) for h in heads]
    grads = [arranged(probs_grads[h], late_grads[h]) for h in heads]
    exps = [jnp.exp(x - jnp.max(x, axis=0, keepdims=True)) for x in both]
    scales = [1.0 / jnp.sum(e, axis=0, keepdims=True) for e in exps]
    row_dots = [jnp.sum(e * g, axis=0, keepdims=True) * s for e, g, s in zip(exps, grads, scales)]
    probs = [(e * s) for e, s in zip(exps, scales)]
    middle = len(sent) * strip
    for h in heads:
        grad = (probs[h] * (grads[h] - row_dots[h])).astype(BF16)
        grad_scores[h] = grad
        rounded = probs[h].astype(BF16)
        kept_probs[h] = rounded[middle:]
        given = jnp.concatenate([grad[:middle], rounded[:middle]], 1)
        dkv = dot(given, jnp.concatenate([asked[h], cotangent[h]], 0))
        for i, (_, _, offset) in enumerate(sent):
            dkv_sent[offset, h] = dkv[i * strip : (i + 1) * strip].astype(BF16)


def base(dq, gz_ref, input_weight):
    strip, lanes = dq.shape
    part = lax.axis_index("col") % (gz_ref.shape[1] // lanes)
    first = pl.multiple_of(part * lanes, lanes)
    grad = jnp.where(part == 0, gz_ref[...].astype(F32), 0.0)
    query = pltpu.roll(dq * (lanes // 2) ** -0.5, lanes // 2, 1).astype(BF16)
    return grad + dot(query, input_weight[:, pl.ds(first, lanes)], 1, 1)


def turned_weight(channels, lanes, input_weight):
    part = lax.axis_index("col") % (channels // lanes)
    key, value = (
        input_weight[:, pl.ds(pl.multiple_of(kind * channels + part * lanes, lanes), lanes)]
        for kind in (1, 2)
    )
    key = pltpu.roll(key.astype(F32), lanes // 2, 1)
    return jnp.concatenate([key, value.astype(F32)], 1).T.astype(BF16)


def finish_kernel(offsets, *refs):
    kv_sent, kv_kept, asker, grad_out, grad_scores, kept_probs, gz_ref, input_weight = refs[:8]
    dkv_kept, base_ref, turned_ref = refs[8:]
    turned_ref[...] = turned_weight(gz_ref.shape[1], asker.shape[2], input_weight)
    strip, lanes = grad_out.shape
    asked, cotangent = by_head(asker[1], grad_out[...])
    sent, kept = chunks_of(offsets)
    middle = len(sent) * strip
    query = []
    for h in (0, 1):
        given = jnp.concatenate([grad_scores[h, middle:], kept_probs[h]], 1)
        dkv = dot(given, jnp.concatenate([asked[h], cotangent[h]], 0))
        for i, (_, _, offset) in enumerate(kept):
            dkv_kept[offset, h] = dkv[i * strip : (i + 1) * strip].astype(BF16)
        keys = jnp.concatenate(
            [(kv_kept if late else kv_sent)[2 * j + h].astype(F32) for late, j, _ in sent + kept], 0
        )
        query.append(dot(grad_scores[h], keys.astype(BF16), 0, 0))
    low = lax.broadcasted_iota(jnp.int32, (strip, lanes), 1) < lanes // 2
    base_ref[...] = base(jnp.where(low, query[1], query[0]), gz_ref, input_weight)


def long_kernel(offsets, *refs):
    kv_sent, kv_kept, asker, grad_out, gz_ref, input_weight = refs[:6]
    dkv_sent, dkv_kept, base_ref, turned_ref = refs[6:]
    turned_ref[...] = turned_weight(gz_ref.shape[1], asker.shape[2], input_weight)
    strip, lanes = grad_out.shape
    asked, cotangent = by_head(asker[1], grad_out[...])
    sent, kept = chunks_of(offsets)
    query = []
    for head in (0, 1):
        ask, cot = asked[head], cotangent[head]

        def gather(kv, carry):
            top, norm, weighted = carry
            scores = dot(kv, ask, 1, 1)
            new = jnp.maximum(top, jnp.max(scores, axis=0, keepdims=True))
            exps = jnp.exp(scores - new)
            rescale = jnp.exp(top - new)
            weights = jnp.sum(exps * dot(kv, cot, 1, 1), axis=0, keepdims=True)
            return (
                new,
                norm * rescale + jnp.sum(exps, axis=0, keepdims=True),
                weighted * rescale + weights,
            )

        zero = jnp.zeros((1, strip), F32)
        stats = (jnp.full((1, strip), -jnp.inf, F32), zero, zero)
        for src in (kv_sent, kv_kept):
            stats = lax.fori_loop(
                0,
                len(offsets),
                lambda j, carry, src=src: gather(src[2 * j + head], carry),
                stats,
            )
        top, norm, weighted = stats
        scale = 1.0 / norm
        total = jnp.zeros((strip, lanes), F32)
        for dst, chunks in ((dkv_sent, sent), (dkv_kept, kept)):
            for late, j, offset in chunks:
                kv = (kv_kept if late else kv_sent)[2 * j + head]
                probs = jnp.exp(dot(kv, ask, 1, 1) - top) * scale
                grad_scores = (probs * (dot(kv, cot, 1, 1) - weighted * scale)).astype(BF16)
                dkv = dot(grad_scores, ask) + dot(probs.astype(BF16), cot)
                dst[offset, head] = dkv.astype(BF16)
                total = total + dot(grad_scores, kv, 0, 0)
        query.append(total)
    low = lax.broadcasted_iota(jnp.int32, (strip, lanes), 1) < lanes // 2
    base_ref[...] = base(jnp.where(low, query[1], query[0]), gz_ref, input_weight)


def core_sum_kernel(own, received, *outs):
    for j, out in enumerate(outs):
        out[...] = (own[j].astype(F32) + received[j].astype(F32)).astype(BF16)


def project_kernel(n_col, per_sample, *refs):
    *refs, cut = refs
    n_in = len(refs) - n_col
    *parts, base_ref, weight, tiles = refs[:n_in]
    outs = refs[n_in:]
    col = lax.axis_index("col")
    part = col % per_sample
    total = sum(ref[...].astype(F32) for ref in parts)
    _, strip, lanes = parts[0].shape
    half = lanes // 2
    channels = base_ref.shape[1]
    low = lax.broadcasted_iota(jnp.int32, (strip, lanes), 1) < half
    dv = jnp.where(low, total[0], total[1])
    dk = jnp.where(low, total[1], total[0])
    given = jnp.concatenate([dk, dv], 1).astype(BF16)
    grad = base_ref[...] + dot(given, weight[...])
    cut[...] = dot(tiles[...], grad.astype(BF16)).reshape(cut.shape)
    for k, out in enumerate(outs):
        out[...] = cut[col ^ k].astype(BF16)


def output_kernel(per_sample, *refs):
    *parts, far_out, out, sem = refs
    parts = parts[::-1]
    rows, cols, samples, channels = out.shape
    padded = pad8(cols)
    sample = lax.axis_index("col") // per_sample
    place = lax.broadcasted_iota(jnp.int32, (cols, samples, channels), 1)
    for i in range(rows):
        cells = jnp.zeros((cols, samples, channels), F32)
        for group in range(samples):
            total = sum(
                ref[...][i * padded : i * padded + cols].astype(F32)
                for ref in parts[group * per_sample : (group + 1) * per_sample]
            )
            cells = jnp.where(place == (sample ^ group), total[:, None, :], cells)
        out[i] = cells.astype(BF16)
    copy = pltpu.make_async_copy(out, far_out, sem)
    copy.start()
    copy.wait()


def shards(
    pre_silu, out_grad, query_heads, key_heads, value_heads, conv_weight, out_weight, input_weight
):
    samples, rows, cols, channels = pre_silu.shape
    pairs, strip, head_dim = query_heads.shape
    n_row, n_col = lax.axis_size("row"), lax.axis_size("col")
    chips = n_row // 2
    per_sample = HEADS // pairs
    lanes = pairs * head_dim

    def to_col(array, k):
        pairs_of = [
            (r * n_col + c, (r ^ 1) * n_col + (c ^ k)) for r in range(n_row) for c in range(n_col)
        ]
        return lax.ppermute(array, ("row", "col"), pairs_of)

    def to_chip(array, k):
        return lax.ppermute(array, "row", [(i, i ^ (2 * k + 1)) for i in range(n_row)])

    def to_core(array):
        return lax.ppermute(array, "row", [(i, i ^ 1) for i in range(n_row)])

    def to_odd_chip(array):
        both = [(0, 1), (n_row - 2, n_row - 1)]
        for i in range(2, n_row - 2, 4):
            both += [(i, i + 3), (i + 1, i + 2)]
        return lax.ppermute(array, "row", both + [(j, i) for i, j in both])

    def cells(array):
        return jnp.transpose(array, (1, 2, 0, 3))

    def turned(array):
        return jnp.transpose(array, (0, 2, 1))

    saved = pltpu.VMEM((pairs, head_dim, strip), BF16)
    tile, kv = call(
        pack_kernel,
        (
            held((2, rows, cols, samples, channels), BF16),
            held((pairs, strip, lanes), BF16),
        ),
        (saved, saved, pltpu.SemaphoreType.DMA((4,))),
        range(4),
    )(cells(out_grad), cells(pre_silu), turned(key_heads), turned(value_heads))
    tiles = [to_col(tile, k) for k in range(n_col)]

    padded = pad8(cols)
    far = (
        jnp.asarray(shift_selector(rows, cols, n_col), BF16),
        jnp.asarray(shift_selector(1, cols, n_col), BF16),
        conv_weight,
        out_weight,
    )
    *loaded, query = call(
        load_kernel,
        [held(array.shape, BF16) for array in far] + [held((strip, lanes), BF16)],
        [saved, pltpu.SemaphoreType.DMA((len(far) + 1,))],
        range(len(far) + 1),
    )(turned(query_heads), *far)

    def doubled(*parts, counts=None):
        counts = counts or [part.shape[0] for part in parts]
        return call(
            functools.partial(join_kernel, counts), held((sum(counts), strip, lanes), BF16)
        )(*parts)

    distances = [chips >> (i + 1) for i in range(chips.bit_length() - 1)]
    offsets = [0]
    for distance in distances:
        offsets = offsets + [offset + distance for offset in offsets]
    tiles, received, (shifts, rim_shifts, conv_weight, out_weight) = lax.optimization_barrier(
        (tiles, to_chip(kv, distances[0]), loaded)
    )
    parts = (kv, received)
    for distance in distances[1:-1]:
        joined = doubled(*parts)
        parts = (joined, to_chip(joined, distance))

    rim = held((strip, lanes), BF16)
    blocks = sum(part.shape[0] for part in parts)
    rim_core, rim_chip, sent = call(
        functools.partial(rim_kernel, n_col, per_sample),
        (held((2, strip, lanes), BF16), rim, held((blocks + 1, strip, lanes), BF16)),
        [pltpu.VMEM((2, n_col, padded, channels), F32)],
    )(*tiles, *parts, query)
    received = to_chip(sent, distances[-1])
    halo_odd, halo_core = to_odd_chip(rim_chip), to_core(rim_core)

    whole = held((strip, channels), F32)
    conv, gate = call(
        functools.partial(conv_kernel, n_col, per_sample),
        (whole, whole),
        [pltpu.VMEM((n_col, rows, padded, channels), F32)] * 2,
    )(*tiles, shifts, conv_weight)
    received, conv, halo_odd, halo_core = lax.optimization_barrier(
        (received, conv, halo_odd, halo_core)
    )
    joined = doubled(sent, received, counts=(blocks, blocks))
    other = to_core(joined)
    grad_z, grad_out = call(
        rim_conv_kernel,
        (held((strip, channels), BF16), held((strip, lanes), BF16)),
    )(halo_core, received, halo_odd, conv, gate, rim_shifts, conv_weight, out_weight)

    block = held((chips, pairs, strip, lanes), BF16)
    given = held((2 * lanes, channels), BF16)
    if 2 * chips <= UNROLLED_CHUNKS:
        half = held((pairs, chips * strip, strip), F32)
        scores, probs_grads = call(score_kernel, (half, half))(joined, halo_core, grad_out)
        dkv_sent, grad_scores, kept_probs = call(
            functools.partial(softmax_kernel, offsets),
            (
                block,
                held((pairs, 2 * chips * strip, strip), BF16),
                held((pairs, chips * strip, strip), BF16),
            ),
        )(other, halo_core, grad_out, scores, probs_grads)
        from_core = to_core(dkv_sent)
        dkv_kept, complete, weight = call(
            functools.partial(finish_kernel, offsets), (block, whole, given)
        )(
            joined, other, halo_core, grad_out, grad_scores, kept_probs, grad_z, input_weight
        )
    else:
        dkv_sent, dkv_kept, complete, weight = call(
            functools.partial(long_kernel, offsets), (block, block, whole, given)
        )(joined, other, halo_core, grad_out, grad_z, input_weight)
        from_core = to_core(dkv_sent)

    sums = call(core_sum_kernel, [held((pairs, strip, lanes), BF16) for _ in range(chips)])(
        dkv_kept, from_core
    )
    far_near = [k for pair in zip(range(chips - 1, 0, -1), range(1, chips)) for k in pair]
    order = list(dict.fromkeys(far_near))
    parts = [to_chip(sums[k], k) for k in order] + [sums[0]]

    selected = tile_selector(rows, cols, n_col).reshape(n_col * rows * padded, -1)
    cut = call(
        functools.partial(project_kernel, n_col, per_sample),
        [held((rows * padded, channels), BF16)] * n_col,
        [pltpu.VMEM((n_col, rows * padded, channels), F32)],
    )(*parts, complete, weight, jnp.asarray(selected, BF16))
    grad_input = call(
        functools.partial(output_kernel, per_sample),
        pltpu.HBM((rows, cols, samples, channels), BF16),
        [pltpu.VMEM((rows, cols, samples, channels), BF16), pltpu.SemaphoreType.DMA],
    )(*[to_col(cut[k], k) for k in reversed(range(n_col))])
    return jnp.transpose(grad_input, (2, 0, 1, 3))


def solution(mesh):
    tile = P(None, "row", "col", None)
    heads = P("col", "row", None)
    return jax.shard_map(
        shards,
        mesh=mesh,
        in_specs=(tile, tile, heads, heads, heads, P(), P(), P()),
        out_specs=tile,
        check_vma=False,
    )
```

```python
import functools

import jax
import jax.numpy as jnp
import numpy as np
from jax import lax
from jax.experimental import pallas as pl
from jax.experimental.pallas import tpu as pltpu
from jax.sharding import PartitionSpec as P

HEADS = 4
VMEM_BYTES = 32 * 1024 * 1024
HELD_BYTES = 3 * 512 * 1024
UNROLLED_CHUNKS = 16
F32 = jnp.float32
BF16 = jnp.bfloat16


def dot(left, right, left_dim=1, right_dim=0):
    return lax.dot_general(
        left, right, (((left_dim,), (right_dim,)), ((), ())), preferred_element_type=F32
    )


def call(kernel, out_shape, scratch=(), far=()):
    def run(*operands):
        specs = [pl.BlockSpec(memory_space=pltpu.VMEM)] * len(operands)
        operands = list(operands)
        for i, operand in enumerate(operands):
            if i in far:
                specs[i] = pl.BlockSpec(memory_space=pltpu.HBM)
                operands[i] = pltpu.with_memory_space_constraint(operand, pltpu.HBM)
            elif operand.size * operand.dtype.itemsize <= HELD_BYTES:
                operands[i] = pltpu.with_memory_space_constraint(operand, pltpu.VMEM)
        return pl.pallas_call(
            kernel,
            out_shape=out_shape,
            in_specs=specs,
            out_specs=jax.tree.map(
                lambda out: pl.BlockSpec(
                    memory_space=pltpu.HBM
                    if getattr(out, "memory_space", None) == pltpu.HBM
                    else pltpu.VMEM
                ),
                out_shape,
            ),
            scratch_shapes=list(scratch),
            compiler_params=pltpu.CompilerParams(vmem_limit_bytes=VMEM_BYTES),
        )(*operands)

    return run


def held(shape, dtype):
    small = np.prod(shape) * np.dtype(dtype).itemsize <= HELD_BYTES
    return (pltpu.VMEM if small else jax.ShapeDtypeStruct)(shape, dtype)


def pad8(amount):
    return -(-amount // 8) * 8


def shift_selector(rows, cols, tiles):
    width, padded = tiles * cols, pad8(cols)
    select = np.zeros((3, rows, width, tiles, rows, padded), np.float32)
    for shift in (-1, 0, 1):
        for j in range(max(0, shift), min(width, width + shift)):
            tile, inner = divmod(j - shift, cols)
            for i in range(rows):
                select[shift + 1, i, j, tile, i, inner] = 1
    return select.reshape(3, rows * width, tiles * rows * padded)


def tile_selector(rows, cols, tiles):
    width, padded = tiles * cols, pad8(cols)
    select = np.zeros((tiles, rows, padded, rows, width), np.float32)
    for tile in range(tiles):
        for i in range(rows):
            for inner in range(cols):
                select[tile, i, inner, i, tile * cols + inner] = 1
    return select.reshape(tiles, rows * padded, rows * width)


def start_copies(pairs, sems):
    copies = [
        pltpu.make_async_copy(src, dst, sems.at[i]) for i, (src, dst) in enumerate(pairs)
    ]
    for copy in copies:
        copy.start()
    return copies


def beside(left, right):
    return jnp.concatenate([left.astype(F32), right.astype(F32)], 0).T.astype(BF16)


def pack_kernel(out_grad, pre_silu, keys, values, tile, kv, k_ref, v_ref, sems):
    copies = start_copies(
        [
            (values, v_ref),
            (keys, k_ref),
            (out_grad, tile.at[0]),
            (pre_silu, tile.at[1]),
        ],
        sems,
    )
    copies[0].wait()
    copies[1].wait()
    kv[0] = beside(v_ref[0], k_ref[0])
    kv[1] = beside(k_ref[1], v_ref[1])
    copies[2].wait()
    copies[3].wait()


def rim_kernel(n_col, per_sample, *refs):
    tiles, (*parts, query, to_core, to_chip, joined, rims) = refs[:n_col], refs[n_col:]
    col = lax.axis_index("col")
    rows = tiles[0].shape[1]
    lanes = to_chip.shape[1]
    used = rims.shape[1] * rims.shape[2]
    inner = jnp.where(lax.axis_index("row") % 2 == 1, rows - 1, 0)
    cols = tiles[0].shape[2]
    rims[...] = jnp.zeros_like(rims)
    to_core[1] = query[...]
    for side, (row, out) in enumerate(((inner, to_core.at[0]), (rows - 1 - inner, to_chip))):
        for k, tile in enumerate(tiles):
            rims[side, col ^ k, :cols] = pick(tile[0, row], col // per_sample)
        flat = rims[side].reshape(used, -1).astype(BF16)
        out[...] = jnp.zeros_like(out)
        for part in range(flat.shape[1] // lanes):
            out[part * used : (part + 1) * used] = flat[:, part * lanes : (part + 1) * lanes]
    join_kernel([part.shape[0] for part in parts], *parts, joined)
    joined[joined.shape[0] - 1] = to_chip[...]


def join_kernel(counts, *refs):
    *parts, out = refs
    first = 0
    for part, count in zip(parts, counts):
        for j in range(count):
            out[first + j] = part[j]
        first += count


def load_kernel(queries, *refs):
    *copied, query, q_ref, sems = refs
    half = len(copied) // 2
    copies = start_copies([(queries, q_ref), *zip(copied[:half], copied[half:])], sems)
    copies[0].wait()
    query[...] = beside(q_ref[1], q_ref[0]) * jnp.asarray(q_ref.shape[1] ** -0.5, BF16)
    for copy in copies[1:]:
        copy.wait()


def pick(cells, sample):
    place = lax.broadcasted_iota(jnp.int32, cells.shape, 1)
    return jnp.sum(jnp.where(place == sample, cells.astype(F32), 0.0), axis=1)


def conv_kernel(n_col, per_sample, *refs):
    tiles, (shifts, conv_weight, conv_ref, gate_ref, grads, silus) = refs[:n_col], refs[n_col:]
    col = lax.axis_index("col")
    sample = col // per_sample
    _, rows, cols, _, channels = tiles[0].shape
    width = n_col * cols
    grads[...] = jnp.zeros_like(grads)
    silus[...] = jnp.zeros_like(silus)
    for k in range(n_col):
        for i in range(rows):
            grads[col ^ k, i, :cols] = pick(tiles[k][0, i], sample)
            silus[col ^ k, i, :cols] = pick(tiles[k][1, i], sample)
    flat = grads[...].reshape(-1, channels).astype(BF16)
    none = jnp.zeros((width, channels), F32)
    conv = jnp.zeros((rows * width, channels), F32)
    for b in (-1, 0, 1):
        here = dot(shifts[b + 1], flat)
        above = jnp.concatenate([none, here[:-width]], 0)
        below = jnp.concatenate([here[width:], none], 0)
        for a, window in ((-1, below), (0, here), (1, above)):
            conv = conv + dot(window.astype(BF16), conv_weight[a + 1, b + 1], 1, 1)
    conv_ref[...] = conv
    z = dot(shifts[1], silus[...].reshape(-1, channels).astype(BF16))
    sigma = 1.0 / (1.0 + jnp.exp(-z))
    gate_ref[...] = sigma * (1.0 + z * (1.0 - sigma))


def rim_conv_kernel(halo_core, halo_last, halo_odd, conv, gate, *refs):
    shifts, conv_weight, out_weight, gz_ref, go_ref = refs
    col, row = lax.axis_index("col"), lax.axis_index("row")
    core, chip = row % 2, row // 2
    strip, channels = gz_ref.shape
    lanes = go_ref.shape[1]
    per_sample = out_weight.shape[0] // lanes
    width = shifts.shape[1]
    used = shifts.shape[2]
    last = halo_last[halo_last.shape[0] - 1]
    missing = jnp.logical_or(row == 1, row == lax.axis_size("row") - 2)
    halo_chip = jnp.where(core == chip % 2, last, halo_odd[...])
    halo_chip = jnp.where(missing, jnp.zeros_like(last), halo_chip)
    inner = halo_core[0]
    parts = channels // lanes

    def spread(halo):
        return jnp.concatenate([halo[p * used : (p + 1) * used] for p in range(parts)], 1)

    rims = (
        spread(jnp.where(core == 1, halo_chip, inner)),
        spread(jnp.where(core == 1, inner, halo_chip)),
    )
    edges = []
    for flat, a in zip(rims, (1, -1)):
        edge = jnp.zeros((width, channels), F32)
        for b in (-1, 0, 1):
            window = dot(shifts[b + 1], flat).astype(BF16)
            edge = edge + dot(window, conv_weight[a + 1, b + 1], 1, 1)
        edges.append(edge)
    between = jnp.zeros((strip - 2 * width, channels), F32)
    total = conv[...] + jnp.concatenate([edges[0], between, edges[1]], 0)
    grad_z = (total * gate[...]).astype(BF16)
    gz_ref[...] = grad_z
    first = pl.multiple_of(col % per_sample * lanes, lanes)
    go_ref[...] = dot(grad_z, out_weight[pl.ds(first, lanes), :], 1, 1).astype(BF16)


def by_head(query, grad_out):
    low = lax.broadcasted_iota(jnp.int32, query.shape, 1) < query.shape[1] // 2
    none = jnp.zeros_like(query)
    asked = (jnp.where(low, none, query), jnp.where(low, query, none))
    return asked, (jnp.where(low, grad_out, none), jnp.where(low, none, grad_out))


def chunks_of(offsets):
    even = [offset != 0 and offset.bit_count() % 2 == 0 for offset in offsets]
    sent = [(e, j, offset) for j, (e, offset) in enumerate(zip(even, offsets))]
    return sent, [(not e, j, offset) for e, j, offset in sent]


def all_keys(arrays, head):
    return jnp.concatenate(
        [kv[2 * j + head].astype(F32) for kv in arrays for j in range(kv.shape[0] // 2)], 0
    ).astype(BF16)


def score_kernel(*refs):
    *arrays, asker, grad_out, scores, probs_grads = refs
    asked, cotangent = by_head(asker[1], grad_out[...])
    for head in (0, 1):
        keys = all_keys(arrays, head)
        scores[head] = dot(keys, asked[head], 1, 1)
        probs_grads[head] = dot(keys, cotangent[head], 1, 1)


def softmax_kernel(offsets, late, asker, grad_out, scores, probs_grads, *outs):
    dkv_sent, grad_scores, kept_probs = outs
    strip = grad_out.shape[0]
    heads = (0, 1)
    asked, cotangent = by_head(asker[1], grad_out[...])
    sent, kept = chunks_of(offsets)

    def arranged(first, second):
        both = jnp.concatenate([first, second], 0)
        places = [(len(offsets) if kept_here else 0) + j for kept_here, j, _ in sent + kept]
        return jnp.concatenate([both[i * strip : (i + 1) * strip] for i in places], 0)

    keys = [all_keys([late], h) for h in heads]
    late_scores = [dot(keys[h], asked[h], 1, 1) for h in heads]
    late_grads = [dot(keys[h], cotangent[h], 1, 1) for h in heads]
    both = [arranged(scores[h], late_scores[h]) for h in heads]
    grads = [arranged(probs_grads[h], late_grads[h]) for h in heads]
    exps = [jnp.exp(x - jnp.max(x, axis=0, keepdims=True)) for x in both]
    scales = [1.0 / jnp.sum(e, axis=0, keepdims=True) for e in exps]
    row_dots = [jnp.sum(e * g, axis=0, keepdims=True) * s for e, g, s in zip(exps, grads, scales)]
    probs = [(e * s) for e, s in zip(exps, scales)]
    middle = len(sent) * strip
    for h in heads:
        grad = (probs[h] * (grads[h] - row_dots[h])).astype(BF16)
        grad_scores[h] = grad
        rounded = probs[h].astype(BF16)
        kept_probs[h] = rounded[middle:]
        given = jnp.concatenate([grad[:middle], rounded[:middle]], 1)
        dkv = dot(given, jnp.concatenate([asked[h], cotangent[h]], 0))
        for i, (_, _, offset) in enumerate(sent):
            dkv_sent[offset, h] = dkv[i * strip : (i + 1) * strip].astype(BF16)


def base(dq, gz_ref, input_weight):
    strip, lanes = dq.shape
    part = lax.axis_index("col") % (gz_ref.shape[1] // lanes)
    first = pl.multiple_of(part * lanes, lanes)
    grad = jnp.where(part == 0, gz_ref[...].astype(F32), 0.0)
    query = pltpu.roll(dq * (lanes // 2) ** -0.5, lanes // 2, 1).astype(BF16)
    return grad + dot(query, input_weight[:, pl.ds(first, lanes)], 1, 1)


def turned_weight(channels, lanes, input_weight):
    part = lax.axis_index("col") % (channels // lanes)
    key, value = (
        input_weight[:, pl.ds(pl.multiple_of(kind * channels + part * lanes, lanes), lanes)]
        for kind in (1, 2)
    )
    key = pltpu.roll(key.astype(F32), lanes // 2, 1)
    return jnp.concatenate([key, value.astype(F32)], 1).T.astype(BF16)


def finish_kernel(offsets, *refs):
    arrays, (asker, grad_out, grad_scores, kept_probs, gz_ref, input_weight) = refs[:4], refs[4:10]
    dkv_kept, base_ref, turned_ref = refs[10:]
    turned_ref[...] = turned_weight(gz_ref.shape[1], asker.shape[2], input_weight)
    strip, lanes = grad_out.shape
    asked, cotangent = by_head(asker[1], grad_out[...])
    sent, kept = chunks_of(offsets)
    middle = len(sent) * strip
    query = []
    for h in (0, 1):
        given = jnp.concatenate([grad_scores[h, middle:], kept_probs[h]], 1)
        dkv = dot(given, jnp.concatenate([asked[h], cotangent[h]], 0))
        for i, (_, _, offset) in enumerate(kept):
            dkv_kept[offset, h] = dkv[i * strip : (i + 1) * strip].astype(BF16)
        keys = all_keys(arrays, h)
        places = [(len(offsets) if kept_here else 0) + j for kept_here, j, _ in sent + kept]
        keys = jnp.concatenate([keys.astype(F32)[i * strip : (i + 1) * strip] for i in places], 0)
        query.append(dot(grad_scores[h], keys.astype(BF16), 0, 0))
    low = lax.broadcasted_iota(jnp.int32, (strip, lanes), 1) < lanes // 2
    base_ref[...] = base(jnp.where(low, query[1], query[0]), gz_ref, input_weight)


def long_kernel(offsets, *refs):
    kv_sent, kv_kept, asker, grad_out, gz_ref, input_weight = refs[:6]
    dkv_sent, dkv_kept, base_ref, turned_ref = refs[6:]
    turned_ref[...] = turned_weight(gz_ref.shape[1], asker.shape[2], input_weight)
    strip, lanes = grad_out.shape
    asked, cotangent = by_head(asker[1], grad_out[...])
    sent, kept = chunks_of(offsets)
    query = []
    for head in (0, 1):
        ask, cot = asked[head], cotangent[head]

        def gather(kv, carry):
            top, norm, weighted = carry
            scores = dot(kv, ask, 1, 1)
            new = jnp.maximum(top, jnp.max(scores, axis=0, keepdims=True))
            exps = jnp.exp(scores - new)
            rescale = jnp.exp(top - new)
            weights = jnp.sum(exps * dot(kv, cot, 1, 1), axis=0, keepdims=True)
            return (
                new,
                norm * rescale + jnp.sum(exps, axis=0, keepdims=True),
                weighted * rescale + weights,
            )

        zero = jnp.zeros((1, strip), F32)
        stats = (jnp.full((1, strip), -jnp.inf, F32), zero, zero)
        for src in (kv_sent, kv_kept):
            stats = lax.fori_loop(
                0,
                len(offsets),
                lambda j, carry, src=src: gather(src[2 * j + head], carry),
                stats,
            )
        top, norm, weighted = stats
        scale = 1.0 / norm
        total = jnp.zeros((strip, lanes), F32)
        for dst, chunks in ((dkv_sent, sent), (dkv_kept, kept)):
            for late, j, offset in chunks:
                kv = (kv_kept if late else kv_sent)[2 * j + head]
                probs = jnp.exp(dot(kv, ask, 1, 1) - top) * scale
                grad_scores = (probs * (dot(kv, cot, 1, 1) - weighted * scale)).astype(BF16)
                dkv = dot(grad_scores, ask) + dot(probs.astype(BF16), cot)
                dst[offset, head] = dkv.astype(BF16)
                total = total + dot(grad_scores, kv, 0, 0)
        query.append(total)
    low = lax.broadcasted_iota(jnp.int32, (strip, lanes), 1) < lanes // 2
    base_ref[...] = base(jnp.where(low, query[1], query[0]), gz_ref, input_weight)


def core_sum_kernel(own, received, *outs):
    for j, out in enumerate(outs):
        out[...] = (own[j].astype(F32) + received[j].astype(F32)).astype(BF16)


def project_kernel(n_col, per_sample, *refs):
    *refs, cut = refs
    n_in = len(refs) - n_col
    *parts, base_ref, weight, tiles = refs[:n_in]
    outs = refs[n_in:]
    col = lax.axis_index("col")
    part = col % per_sample
    total = sum(ref[...].astype(F32) for ref in parts)
    _, strip, lanes = parts[0].shape
    half = lanes // 2
    channels = base_ref.shape[1]
    low = lax.broadcasted_iota(jnp.int32, (strip, lanes), 1) < half
    dv = jnp.where(low, total[0], total[1])
    dk = jnp.where(low, total[1], total[0])
    given = jnp.concatenate([dk, dv], 1).astype(BF16)
    grad = base_ref[...] + dot(given, weight[...])
    cut[...] = dot(tiles[...], grad.astype(BF16)).reshape(cut.shape)
    for k, out in enumerate(outs):
        out[...] = cut[col ^ k].astype(BF16)


def output_kernel(per_sample, *refs):
    *parts, far_out, out, sem = refs
    parts = parts[::-1]
    rows, cols, samples, channels = out.shape
    padded = pad8(cols)
    sample = lax.axis_index("col") // per_sample
    place = lax.broadcasted_iota(jnp.int32, (cols, samples, channels), 1)
    for i in range(rows):
        cells = jnp.zeros((cols, samples, channels), F32)
        for group in range(samples):
            total = sum(
                ref[...][i * padded : i * padded + cols].astype(F32)
                for ref in parts[group * per_sample : (group + 1) * per_sample]
            )
            cells = jnp.where(place == (sample ^ group), total[:, None, :], cells)
        out[i] = cells.astype(BF16)
    copy = pltpu.make_async_copy(out, far_out, sem)
    copy.start()
    copy.wait()


def shards(
    pre_silu, out_grad, query_heads, key_heads, value_heads, conv_weight, out_weight, input_weight
):
    samples, rows, cols, channels = pre_silu.shape
    pairs, strip, head_dim = query_heads.shape
    n_row, n_col = lax.axis_size("row"), lax.axis_size("col")
    chips = n_row // 2
    per_sample = HEADS // pairs
    lanes = pairs * head_dim

    def to_col(array, k):
        pairs_of = [
            (r * n_col + c, (r ^ 1) * n_col + (c ^ k)) for r in range(n_row) for c in range(n_col)
        ]
        return lax.ppermute(array, ("row", "col"), pairs_of)

    def to_chip(array, k):
        return lax.ppermute(array, "row", [(i, i ^ (2 * k + 1)) for i in range(n_row)])

    def to_core(array):
        return lax.ppermute(array, "row", [(i, i ^ 1) for i in range(n_row)])

    def to_odd_chip(array):
        both = [(0, 1), (n_row - 2, n_row - 1)]
        for i in range(2, n_row - 2, 4):
            both += [(i, i + 3), (i + 1, i + 2)]
        return lax.ppermute(array, "row", both + [(j, i) for i, j in both])

    def cells(array):
        return jnp.transpose(array, (1, 2, 0, 3))

    def turned(array):
        return jnp.transpose(array, (0, 2, 1))

    saved = pltpu.VMEM((pairs, head_dim, strip), BF16)
    tile, kv = call(
        pack_kernel,
        (
            held((2, rows, cols, samples, channels), BF16),
            held((pairs, strip, lanes), BF16),
        ),
        (saved, saved, pltpu.SemaphoreType.DMA((4,))),
        range(4),
    )(cells(out_grad), cells(pre_silu), turned(key_heads), turned(value_heads))
    tiles = [to_col(tile, k) for k in range(n_col)]

    padded = pad8(cols)
    far = (
        jnp.asarray(shift_selector(rows, cols, n_col), BF16),
        jnp.asarray(shift_selector(1, cols, n_col), BF16),
        conv_weight,
        out_weight,
    )
    *loaded, query = call(
        load_kernel,
        [held(array.shape, BF16) for array in far] + [held((strip, lanes), BF16)],
        [saved, pltpu.SemaphoreType.DMA((len(far) + 1,))],
        range(len(far) + 1),
    )(turned(query_heads), *far)

    def doubled(*parts, counts=None):
        counts = counts or [part.shape[0] for part in parts]
        return call(
            functools.partial(join_kernel, counts), held((sum(counts), strip, lanes), BF16)
        )(*parts)

    distances = [chips >> (i + 1) for i in range(chips.bit_length() - 1)]
    offsets = [0]
    for distance in distances:
        offsets = offsets + [offset + distance for offset in offsets]
    tiles, received, (shifts, rim_shifts, conv_weight, out_weight) = lax.optimization_barrier(
        (tiles, to_chip(kv, distances[0]), loaded)
    )
    parts = (kv, received)
    for distance in distances[1:-1]:
        joined = doubled(*parts)
        parts = (joined, to_chip(joined, distance))

    rim = held((strip, lanes), BF16)
    blocks = sum(part.shape[0] for part in parts)
    rim_core, rim_chip, sent = call(
        functools.partial(rim_kernel, n_col, per_sample),
        (held((2, strip, lanes), BF16), rim, held((blocks + 1, strip, lanes), BF16)),
        [pltpu.VMEM((2, n_col, padded, channels), F32)],
    )(*tiles, *parts, query)
    received = to_chip(sent, distances[-1])
    halo_odd, halo_core, early = to_odd_chip(rim_chip), to_core(rim_core), to_core(sent)

    whole = held((strip, channels), F32)
    conv, gate = call(
        functools.partial(conv_kernel, n_col, per_sample),
        (whole, whole),
        [pltpu.VMEM((n_col, rows, padded, channels), F32)] * 2,
    )(*tiles, shifts, conv_weight)
    received, conv, halo_odd, halo_core, early = lax.optimization_barrier(
        (received, conv, halo_odd, halo_core, early)
    )
    late = to_core(received)
    grad_z, grad_out = call(
        rim_conv_kernel,
        (held((strip, channels), BF16), held((strip, lanes), BF16)),
    )(halo_core, received, halo_odd, conv, gate, rim_shifts, conv_weight, out_weight)

    block = held((chips, pairs, strip, lanes), BF16)
    given = held((2 * lanes, channels), BF16)
    if 2 * chips <= UNROLLED_CHUNKS:
        most = held((pairs, (2 * chips - blocks // 2) * strip, strip), F32)
        scores, probs_grads = call(score_kernel, (most, most))(
            sent, received, early, halo_core, grad_out
        )
        dkv_sent, grad_scores, kept_probs = call(
            functools.partial(softmax_kernel, offsets),
            (
                block,
                held((pairs, 2 * chips * strip, strip), BF16),
                held((pairs, chips * strip, strip), BF16),
            ),
        )(late, halo_core, grad_out, scores, probs_grads)
        from_core = to_core(dkv_sent)
        dkv_kept, complete, weight = call(
            functools.partial(finish_kernel, offsets), (block, whole, given)
        )(
            sent,
            received,
            early,
            late,
            halo_core,
            grad_out,
            grad_scores,
            kept_probs,
            grad_z,
            input_weight,
        )
    else:
        joined = doubled(sent, received, counts=(blocks, blocks))
        other = doubled(early, late, counts=(blocks, blocks))
        dkv_sent, dkv_kept, complete, weight = call(
            functools.partial(long_kernel, offsets), (block, block, whole, given)
        )(joined, other, halo_core, grad_out, grad_z, input_weight)
        from_core = to_core(dkv_sent)

    sums = call(core_sum_kernel, [held((pairs, strip, lanes), BF16) for _ in range(chips)])(
        dkv_kept, from_core
    )
    far_near = [k for pair in zip(range(chips - 1, 0, -1), range(1, chips)) for k in pair]
    order = list(dict.fromkeys(far_near))
    parts = [to_chip(sums[k], k) for k in order] + [sums[0]]

    selected = tile_selector(rows, cols, n_col).reshape(n_col * rows * padded, -1)
    cut = call(
        functools.partial(project_kernel, n_col, per_sample),
        [held((rows * padded, channels), BF16)] * n_col,
        [pltpu.VMEM((n_col, rows * padded, channels), F32)],
    )(*parts, complete, weight, jnp.asarray(selected, BF16))
    grad_input = call(
        functools.partial(output_kernel, per_sample),
        pltpu.HBM((rows, cols, samples, channels), BF16),
        [pltpu.VMEM((rows, cols, samples, channels), BF16), pltpu.SemaphoreType.DMA],
    )(*[to_col(cut[k], k) for k in reversed(range(n_col))])
    return jnp.transpose(grad_input, (2, 0, 1, 3))


def solution(mesh):
    tile = P(None, "row", "col", None)
    heads = P("col", "row", None)
    return jax.shard_map(
        shards,
        mesh=mesh,
        in_specs=(tile, tile, heads, heads, heads, P(), P(), P()),
        out_specs=tile,
        check_vma=False,
    )
```

```python
import functools

import jax
import jax.numpy as jnp
import numpy as np
from jax import lax
from jax.experimental import pallas as pl
from jax.experimental.pallas import tpu as pltpu
from jax.sharding import PartitionSpec as P

HEADS = 4
VMEM_BYTES = 32 * 1024 * 1024
HELD_BYTES = 3 * 512 * 1024
UNROLLED_CHUNKS = 16
F32 = jnp.float32
BF16 = jnp.bfloat16


def dot(left, right, left_dim=1, right_dim=0):
    return lax.dot_general(
        left, right, (((left_dim,), (right_dim,)), ((), ())), preferred_element_type=F32
    )


def call(kernel, out_shape, scratch=(), far=()):
    def run(*operands):
        specs = [pl.BlockSpec(memory_space=pltpu.VMEM)] * len(operands)
        operands = list(operands)
        for i, operand in enumerate(operands):
            if i in far:
                specs[i] = pl.BlockSpec(memory_space=pltpu.HBM)
                operands[i] = pltpu.with_memory_space_constraint(operand, pltpu.HBM)
            elif operand.size * operand.dtype.itemsize <= HELD_BYTES:
                operands[i] = pltpu.with_memory_space_constraint(operand, pltpu.VMEM)
        return pl.pallas_call(
            kernel,
            out_shape=out_shape,
            in_specs=specs,
            out_specs=jax.tree.map(
                lambda out: pl.BlockSpec(
                    memory_space=pltpu.HBM
                    if getattr(out, "memory_space", None) == pltpu.HBM
                    else pltpu.VMEM
                ),
                out_shape,
            ),
            scratch_shapes=list(scratch),
            compiler_params=pltpu.CompilerParams(vmem_limit_bytes=VMEM_BYTES),
        )(*operands)

    return run


def held(shape, dtype):
    small = np.prod(shape) * np.dtype(dtype).itemsize <= HELD_BYTES
    return (pltpu.VMEM if small else jax.ShapeDtypeStruct)(shape, dtype)


def pad8(amount):
    return -(-amount // 8) * 8


def shift_selector(rows, cols, tiles):
    width, padded = tiles * cols, pad8(cols)
    select = np.zeros((3, rows, width, tiles, rows, padded), np.float32)
    for shift in (-1, 0, 1):
        for j in range(max(0, shift), min(width, width + shift)):
            tile, inner = divmod(j - shift, cols)
            for i in range(rows):
                select[shift + 1, i, j, tile, i, inner] = 1
    return select.reshape(3, rows * width, tiles * rows * padded)


def tile_selector(rows, cols, tiles):
    width, padded = tiles * cols, pad8(cols)
    select = np.zeros((tiles, rows, padded, rows, width), np.float32)
    for tile in range(tiles):
        for i in range(rows):
            for inner in range(cols):
                select[tile, i, inner, i, tile * cols + inner] = 1
    return select.reshape(tiles, rows * padded, rows * width)


def start_copies(pairs, sems):
    copies = [
        pltpu.make_async_copy(src, dst, sems.at[i]) for i, (src, dst) in enumerate(pairs)
    ]
    for copy in copies:
        copy.start()
    return copies


def beside(left, right):
    return jnp.concatenate([left, right], 0).T


def pack_kernel(out_grad, pre_silu, keys, values, tile, kv, k_ref, v_ref, sems):
    copies = start_copies(
        [
            (values, v_ref),
            (keys, k_ref),
            (out_grad, tile.at[0]),
            (pre_silu, tile.at[1]),
        ],
        sems,
    )
    copies[0].wait()
    copies[1].wait()
    kv[0] = beside(v_ref[0], k_ref[0])
    kv[1] = beside(k_ref[1], v_ref[1])
    copies[2].wait()
    copies[3].wait()


def rim_kernel(n_col, per_sample, *refs):
    tiles, (*parts, query, to_core, to_chip, joined, rims) = refs[:n_col], refs[n_col:]
    col = lax.axis_index("col")
    rows = tiles[0].shape[1]
    lanes = to_chip.shape[1]
    used = rims.shape[1] * rims.shape[2]
    inner = jnp.where(lax.axis_index("row") % 2 == 1, rows - 1, 0)
    cols = tiles[0].shape[2]
    rest = jnp.zeros((rims.shape[2] - cols, rims.shape[3]), F32)
    to_core[1] = query[...]
    for side, (row, out) in enumerate(((inner, to_core.at[0]), (rows - 1 - inner, to_chip))):
        for k, tile in enumerate(tiles):
            rims[side, col ^ k] = jnp.concatenate([pick(tile[0, row], col // per_sample), rest], 0)
        flat = rims[side].reshape(used, -1).astype(BF16)
        out[...] = jnp.zeros_like(out)
        for part in range(flat.shape[1] // lanes):
            out[part * used : (part + 1) * used] = flat[:, part * lanes : (part + 1) * lanes]
    join_kernel([part.shape[0] for part in parts], *parts, joined)
    joined[joined.shape[0] - 1] = to_chip[...]


def join_kernel(counts, *refs):
    *parts, out = refs
    first = 0
    for part, count in zip(parts, counts):
        for j in range(count):
            out[first + j] = part[j]
        first += count


def load_kernel(queries, *refs):
    *copied, query, q_ref, sems = refs
    half = len(copied) // 2
    copies = start_copies([(queries, q_ref), *zip(copied[:half], copied[half:])], sems)
    copies[0].wait()
    query[...] = beside(q_ref[1], q_ref[0]) * jnp.asarray(q_ref.shape[1] ** -0.5, BF16)
    for copy in copies[1:]:
        copy.wait()


def pick(cells, sample):
    place = lax.broadcasted_iota(jnp.int32, cells.shape, 1)
    return jnp.sum(jnp.where(place == sample, cells.astype(F32), 0.0), axis=1)


def conv_kernel(n_col, per_sample, *refs):
    tiles, (shifts, conv_weight, conv_ref, gate_ref, grads, silus) = refs[:n_col], refs[n_col:]
    col = lax.axis_index("col")
    sample = col // per_sample
    _, rows, cols, _, channels = tiles[0].shape
    width = n_col * cols
    grads[...] = jnp.zeros_like(grads)
    silus[...] = jnp.zeros_like(silus)
    for k in range(n_col):
        for i in range(rows):
            grads[col ^ k, i, :cols] = pick(tiles[k][0, i], sample)
            silus[col ^ k, i, :cols] = pick(tiles[k][1, i], sample)
    flat = grads[...].reshape(-1, channels).astype(BF16)
    none = jnp.zeros((width, channels), F32)
    conv = jnp.zeros((rows * width, channels), F32)
    for b in (-1, 0, 1):
        here = dot(shifts[b + 1], flat)
        above = jnp.concatenate([none, here[:-width]], 0)
        below = jnp.concatenate([here[width:], none], 0)
        for a, window in ((-1, below), (0, here), (1, above)):
            conv = conv + dot(window.astype(BF16), conv_weight[a + 1, b + 1], 1, 1)
    conv_ref[...] = conv
    z = dot(shifts[1], silus[...].reshape(-1, channels).astype(BF16))
    sigma = 1.0 / (1.0 + jnp.exp(-z))
    gate_ref[...] = sigma * (1.0 + z * (1.0 - sigma))


def rim_conv_kernel(halo_core, halo_last, halo_odd, conv, gate, *refs):
    shifts, conv_weight, out_weight, gz_ref, go_ref = refs
    col, row = lax.axis_index("col"), lax.axis_index("row")
    core, chip = row % 2, row // 2
    strip, channels = gz_ref.shape
    lanes = go_ref.shape[1]
    per_sample = out_weight.shape[0] // lanes
    width = shifts.shape[1]
    used = shifts.shape[2]
    last = halo_last[halo_last.shape[0] - 1]
    missing = jnp.logical_or(row == 1, row == lax.axis_size("row") - 2)
    halo_chip = jnp.where(core == chip % 2, last, halo_odd[...])
    halo_chip = jnp.where(missing, jnp.zeros_like(last), halo_chip)
    inner = halo_core[0]
    parts = channels // lanes

    def spread(halo):
        return jnp.concatenate([halo[p * used : (p + 1) * used] for p in range(parts)], 1)

    rims = (
        spread(jnp.where(core == 1, halo_chip, inner)),
        spread(jnp.where(core == 1, inner, halo_chip)),
    )
    edges = []
    for flat, a in zip(rims, (1, -1)):
        edge = jnp.zeros((width, channels), F32)
        for b in (-1, 0, 1):
            window = dot(shifts[b + 1], flat).astype(BF16)
            edge = edge + dot(window, conv_weight[a + 1, b + 1], 1, 1)
        edges.append(edge)
    between = jnp.zeros((strip - 2 * width, channels), F32)
    total = conv[...] + jnp.concatenate([edges[0], between, edges[1]], 0)
    grad_z = (total * gate[...]).astype(BF16)
    gz_ref[...] = grad_z
    first = pl.multiple_of(col % per_sample * lanes, lanes)
    go_ref[...] = dot(grad_z, out_weight[pl.ds(first, lanes), :], 1, 1).astype(BF16)


def by_head(query, grad_out):
    low = lax.broadcasted_iota(jnp.int32, query.shape, 1) < query.shape[1] // 2
    none = jnp.zeros_like(query)
    asked = (jnp.where(low, none, query), jnp.where(low, query, none))
    return asked, (jnp.where(low, grad_out, none), jnp.where(low, none, grad_out))


def chunks_of(offsets):
    even = [offset != 0 and offset.bit_count() % 2 == 0 for offset in offsets]
    sent = [(e, j, offset) for j, (e, offset) in enumerate(zip(even, offsets))]
    return sent, [(not e, j, offset) for e, j, offset in sent]


def all_keys(arrays, head):
    return jnp.concatenate(
        [kv[2 * j + head].astype(F32) for kv in arrays for j in range(kv.shape[0] // 2)], 0
    ).astype(BF16)


def score_kernel(*refs):
    *arrays, asker, grad_out, scores, probs_grads = refs
    asked, cotangent = by_head(asker[1], grad_out[...])
    for head in (0, 1):
        keys = all_keys(arrays, head)
        scores[head] = dot(keys, asked[head], 1, 1)
        probs_grads[head] = dot(keys, cotangent[head], 1, 1)


def softmax_kernel(offsets, late, asker, grad_out, scores, probs_grads, *outs):
    dkv_sent, grad_scores, kept_probs = outs
    strip = grad_out.shape[0]
    heads = (0, 1)
    asked, cotangent = by_head(asker[1], grad_out[...])
    sent, kept = chunks_of(offsets)

    def arranged(first, second):
        both = jnp.concatenate([first, second], 0)
        places = [(len(offsets) if kept_here else 0) + j for kept_here, j, _ in sent + kept]
        return jnp.concatenate([both[i * strip : (i + 1) * strip] for i in places], 0)

    keys = [all_keys([late], h) for h in heads]
    late_scores = [dot(keys[h], asked[h], 1, 1) for h in heads]
    late_grads = [dot(keys[h], cotangent[h], 1, 1) for h in heads]
    both = [arranged(scores[h], late_scores[h]) for h in heads]
    grads = [arranged(probs_grads[h], late_grads[h]) for h in heads]
    exps = [jnp.exp(x - jnp.max(x, axis=0, keepdims=True)) for x in both]
    scales = [1.0 / jnp.sum(e, axis=0, keepdims=True) for e in exps]
    row_dots = [jnp.sum(e * g, axis=0, keepdims=True) * s for e, g, s in zip(exps, grads, scales)]
    probs = [(e * s) for e, s in zip(exps, scales)]
    middle = len(sent) * strip
    for h in heads:
        grad = (probs[h] * (grads[h] - row_dots[h])).astype(BF16)
        grad_scores[h] = grad
        rounded = probs[h].astype(BF16)
        kept_probs[h] = rounded[middle:]
        given = jnp.concatenate([grad[:middle], rounded[:middle]], 1)
        dkv = dot(given, jnp.concatenate([asked[h], cotangent[h]], 0))
        for i, (_, _, offset) in enumerate(sent):
            dkv_sent[offset, h] = dkv[i * strip : (i + 1) * strip].astype(BF16)


def base(dq, gz_ref, input_weight):
    strip, lanes = dq.shape
    part = lax.axis_index("col") % (gz_ref.shape[1] // lanes)
    first = pl.multiple_of(part * lanes, lanes)
    grad = jnp.where(part == 0, gz_ref[...].astype(F32), 0.0)
    query = pltpu.roll(dq * (lanes // 2) ** -0.5, lanes // 2, 1).astype(BF16)
    return grad + dot(query, input_weight[:, pl.ds(first, lanes)], 1, 1)


def turned_weight(channels, lanes, input_weight):
    part = lax.axis_index("col") % (channels // lanes)
    key, value = (
        input_weight[:, pl.ds(pl.multiple_of(kind * channels + part * lanes, lanes), lanes)]
        for kind in (1, 2)
    )
    key = pltpu.roll(key.astype(F32), lanes // 2, 1)
    return jnp.concatenate([key, value.astype(F32)], 1).T.astype(BF16)


def finish_kernel(offsets, *refs):
    arrays, (asker, grad_out, grad_scores, kept_probs, gz_ref, input_weight) = refs[:4], refs[4:10]
    dkv_kept, base_ref, turned_ref = refs[10:]
    turned_ref[...] = turned_weight(gz_ref.shape[1], asker.shape[2], input_weight)
    strip, lanes = grad_out.shape
    asked, cotangent = by_head(asker[1], grad_out[...])
    sent, kept = chunks_of(offsets)
    middle = len(sent) * strip
    query = []
    for h in (0, 1):
        given = jnp.concatenate([grad_scores[h, middle:], kept_probs[h]], 1)
        dkv = dot(given, jnp.concatenate([asked[h], cotangent[h]], 0))
        for i, (_, _, offset) in enumerate(kept):
            dkv_kept[offset, h] = dkv[i * strip : (i + 1) * strip].astype(BF16)
        keys = all_keys(arrays, h)
        places = [(len(offsets) if kept_here else 0) + j for kept_here, j, _ in sent + kept]
        keys = jnp.concatenate([keys.astype(F32)[i * strip : (i + 1) * strip] for i in places], 0)
        query.append(dot(grad_scores[h], keys.astype(BF16), 0, 0))
    low = lax.broadcasted_iota(jnp.int32, (strip, lanes), 1) < lanes // 2
    base_ref[...] = base(jnp.where(low, query[1], query[0]), gz_ref, input_weight)


def long_kernel(offsets, *refs):
    kv_sent, kv_kept, asker, grad_out, gz_ref, input_weight = refs[:6]
    dkv_sent, dkv_kept, base_ref, turned_ref = refs[6:]
    turned_ref[...] = turned_weight(gz_ref.shape[1], asker.shape[2], input_weight)
    strip, lanes = grad_out.shape
    asked, cotangent = by_head(asker[1], grad_out[...])
    sent, kept = chunks_of(offsets)
    query = []
    for head in (0, 1):
        ask, cot = asked[head], cotangent[head]

        def gather(kv, carry):
            top, norm, weighted = carry
            scores = dot(kv, ask, 1, 1)
            new = jnp.maximum(top, jnp.max(scores, axis=0, keepdims=True))
            exps = jnp.exp(scores - new)
            rescale = jnp.exp(top - new)
            weights = jnp.sum(exps * dot(kv, cot, 1, 1), axis=0, keepdims=True)
            return (
                new,
                norm * rescale + jnp.sum(exps, axis=0, keepdims=True),
                weighted * rescale + weights,
            )

        zero = jnp.zeros((1, strip), F32)
        stats = (jnp.full((1, strip), -jnp.inf, F32), zero, zero)
        for src in (kv_sent, kv_kept):
            stats = lax.fori_loop(
                0,
                len(offsets),
                lambda j, carry, src=src: gather(src[2 * j + head], carry),
                stats,
            )
        top, norm, weighted = stats
        scale = 1.0 / norm
        total = jnp.zeros((strip, lanes), F32)
        for dst, chunks in ((dkv_sent, sent), (dkv_kept, kept)):
            for late, j, offset in chunks:
                kv = (kv_kept if late else kv_sent)[2 * j + head]
                probs = jnp.exp(dot(kv, ask, 1, 1) - top) * scale
                grad_scores = (probs * (dot(kv, cot, 1, 1) - weighted * scale)).astype(BF16)
                dkv = dot(grad_scores, ask) + dot(probs.astype(BF16), cot)
                dst[offset, head] = dkv.astype(BF16)
                total = total + dot(grad_scores, kv, 0, 0)
        query.append(total)
    low = lax.broadcasted_iota(jnp.int32, (strip, lanes), 1) < lanes // 2
    base_ref[...] = base(jnp.where(low, query[1], query[0]), gz_ref, input_weight)


def core_sum_kernel(own, received, *outs):
    for j, out in enumerate(outs):
        out[...] = (own[j].astype(F32) + received[j].astype(F32)).astype(BF16)


def project_kernel(n_col, per_sample, *refs):
    *refs, cut = refs
    n_in = len(refs) - n_col
    *parts, base_ref, weight, tiles = refs[:n_in]
    outs = refs[n_in:]
    col = lax.axis_index("col")
    part = col % per_sample
    total = sum(ref[...].astype(F32) for ref in parts)
    _, strip, lanes = parts[0].shape
    half = lanes // 2
    channels = base_ref.shape[1]
    low = lax.broadcasted_iota(jnp.int32, (strip, lanes), 1) < half
    dv = jnp.where(low, total[0], total[1])
    dk = jnp.where(low, total[1], total[0])
    given = jnp.concatenate([dk, dv], 1).astype(BF16)
    grad = base_ref[...] + dot(given, weight[...])
    cut[...] = dot(tiles[...], grad.astype(BF16)).reshape(cut.shape)
    for k, out in enumerate(outs):
        out[...] = cut[col ^ k].astype(BF16)


def output_kernel(per_sample, *refs):
    *parts, far_out, out, sem = refs
    parts = parts[::-1]
    rows, cols, samples, channels = out.shape
    padded = pad8(cols)
    sample = lax.axis_index("col") // per_sample
    place = lax.broadcasted_iota(jnp.int32, (cols, samples, channels), 1)
    for i in range(rows):
        cells = jnp.zeros((cols, samples, channels), F32)
        for group in range(samples):
            total = sum(
                ref[...][i * padded : i * padded + cols].astype(F32)
                for ref in parts[group * per_sample : (group + 1) * per_sample]
            )
            cells = jnp.where(place == (sample ^ group), total[:, None, :], cells)
        out[i] = cells.astype(BF16)
    copy = pltpu.make_async_copy(out, far_out, sem)
    copy.start()
    copy.wait()


def shards(
    pre_silu, out_grad, query_heads, key_heads, value_heads, conv_weight, out_weight, input_weight
):
    samples, rows, cols, channels = pre_silu.shape
    pairs, strip, head_dim = query_heads.shape
    n_row, n_col = lax.axis_size("row"), lax.axis_size("col")
    chips = n_row // 2
    per_sample = HEADS // pairs
    lanes = pairs * head_dim

    def to_col(array, k):
        pairs_of = [
            (r * n_col + c, (r ^ 1) * n_col + (c ^ k)) for r in range(n_row) for c in range(n_col)
        ]
        return lax.ppermute(array, ("row", "col"), pairs_of)

    def to_chip(array, k):
        return lax.ppermute(array, "row", [(i, i ^ (2 * k + 1)) for i in range(n_row)])

    def to_core(array):
        return lax.ppermute(array, "row", [(i, i ^ 1) for i in range(n_row)])

    def to_odd_chip(array):
        both = [(0, 1), (n_row - 2, n_row - 1)]
        for i in range(2, n_row - 2, 4):
            both += [(i, i + 3), (i + 1, i + 2)]
        return lax.ppermute(array, "row", both + [(j, i) for i, j in both])

    def cells(array):
        return jnp.transpose(array, (1, 2, 0, 3))

    def turned(array):
        return jnp.transpose(array, (0, 2, 1))

    saved = pltpu.VMEM((pairs, head_dim, strip), BF16)
    tile, kv = call(
        pack_kernel,
        (
            held((2, rows, cols, samples, channels), BF16),
            held((pairs, strip, lanes), BF16),
        ),
        (saved, saved, pltpu.SemaphoreType.DMA((4,))),
        range(4),
    )(cells(out_grad), cells(pre_silu), turned(key_heads), turned(value_heads))
    tiles = [to_col(tile, k) for k in range(n_col)]

    padded = pad8(cols)
    far = (
        jnp.asarray(shift_selector(rows, cols, n_col), BF16),
        jnp.asarray(shift_selector(1, cols, n_col), BF16),
        conv_weight,
        out_weight,
    )
    *loaded, query = call(
        load_kernel,
        [held(array.shape, BF16) for array in far] + [held((strip, lanes), BF16)],
        [saved, pltpu.SemaphoreType.DMA((len(far) + 1,))],
        range(len(far) + 1),
    )(turned(query_heads), *far)

    def doubled(*parts, counts=None):
        counts = counts or [part.shape[0] for part in parts]
        return call(
            functools.partial(join_kernel, counts), held((sum(counts), strip, lanes), BF16)
        )(*parts)

    distances = [chips >> (i + 1) for i in range(chips.bit_length() - 1)]
    offsets = [0]
    for distance in distances:
        offsets = offsets + [offset + distance for offset in offsets]
    tiles, received, (shifts, rim_shifts, conv_weight, out_weight) = lax.optimization_barrier(
        (tiles, to_chip(kv, distances[0]), loaded)
    )
    parts = (kv, received)
    for distance in distances[1:-1]:
        joined = doubled(*parts)
        parts = (joined, to_chip(joined, distance))

    rim = held((strip, lanes), BF16)
    blocks = sum(part.shape[0] for part in parts)
    rim_core, rim_chip, sent = call(
        functools.partial(rim_kernel, n_col, per_sample),
        (held((2, strip, lanes), BF16), rim, held((blocks + 1, strip, lanes), BF16)),
        [pltpu.VMEM((2, n_col, padded, channels), F32)],
    )(*tiles, *parts, query)
    received = to_chip(sent, distances[-1])
    halo_odd, halo_core, early = to_odd_chip(rim_chip), to_core(rim_core), to_core(sent)

    whole = held((strip, channels), F32)
    conv, gate = call(
        functools.partial(conv_kernel, n_col, per_sample),
        (whole, whole),
        [pltpu.VMEM((n_col, rows, padded, channels), F32)] * 2,
    )(*tiles, shifts, conv_weight)
    received, conv, halo_odd, halo_core, early = lax.optimization_barrier(
        (received, conv, halo_odd, halo_core, early)
    )
    late = to_core(received)
    grad_z, grad_out = call(
        rim_conv_kernel,
        (held((strip, channels), BF16), held((strip, lanes), BF16)),
    )(halo_core, received, halo_odd, conv, gate, rim_shifts, conv_weight, out_weight)

    block = held((chips, pairs, strip, lanes), BF16)
    given = held((2 * lanes, channels), BF16)
    if 2 * chips <= UNROLLED_CHUNKS:
        most = held((pairs, (2 * chips - blocks // 2) * strip, strip), F32)
        scores, probs_grads = call(score_kernel, (most, most))(
            sent, received, early, halo_core, grad_out
        )
        dkv_sent, grad_scores, kept_probs = call(
            functools.partial(softmax_kernel, offsets),
            (
                block,
                held((pairs, 2 * chips * strip, strip), BF16),
                held((pairs, chips * strip, strip), BF16),
            ),
        )(late, halo_core, grad_out, scores, probs_grads)
        from_core = to_core(dkv_sent)
        dkv_kept, complete, weight = call(
            functools.partial(finish_kernel, offsets), (block, whole, given)
        )(
            sent,
            received,
            early,
            late,
            halo_core,
            grad_out,
            grad_scores,
            kept_probs,
            grad_z,
            input_weight,
        )
    else:
        joined = doubled(sent, received, counts=(blocks, blocks))
        other = doubled(early, late, counts=(blocks, blocks))
        dkv_sent, dkv_kept, complete, weight = call(
            functools.partial(long_kernel, offsets), (block, block, whole, given)
        )(joined, other, halo_core, grad_out, grad_z, input_weight)
        from_core = to_core(dkv_sent)

    sums = call(core_sum_kernel, [held((pairs, strip, lanes), BF16) for _ in range(chips)])(
        dkv_kept, from_core
    )
    far_near = [k for pair in zip(range(chips - 1, 0, -1), range(1, chips)) for k in pair]
    order = list(dict.fromkeys(far_near))
    parts = [to_chip(sums[k], k) for k in order] + [sums[0]]

    selected = tile_selector(rows, cols, n_col).reshape(n_col * rows * padded, -1)
    cut = call(
        functools.partial(project_kernel, n_col, per_sample),
        [held((rows * padded, channels), BF16)] * n_col,
        [pltpu.VMEM((n_col, rows * padded, channels), F32)],
    )(*parts, complete, weight, jnp.asarray(selected, BF16))
    grad_input = call(
        functools.partial(output_kernel, per_sample),
        pltpu.HBM((rows, cols, samples, channels), BF16),
        [pltpu.VMEM((rows, cols, samples, channels), BF16), pltpu.SemaphoreType.DMA],
    )(*[to_col(cut[k], k) for k in reversed(range(n_col))])
    return jnp.transpose(grad_input, (2, 0, 1, 3))


def solution(mesh):
    tile = P(None, "row", "col", None)
    heads = P("col", "row", None)
    return jax.shard_map(
        shards,
        mesh=mesh,
        in_specs=(tile, tile, heads, heads, heads, P(), P(), P()),
        out_specs=tile,
        check_vma=False,
    )
```

```python
import functools

import jax
import jax.numpy as jnp
import numpy as np
from jax import lax
from jax.experimental import pallas as pl
from jax.experimental.pallas import tpu as pltpu
from jax.sharding import PartitionSpec as P

HEADS = 4
VMEM_BYTES = 32 * 1024 * 1024
HELD_BYTES = 3 * 512 * 1024
UNROLLED_CHUNKS = 16
F32 = jnp.float32
BF16 = jnp.bfloat16


def dot(left, right, left_dim=1, right_dim=0):
    return lax.dot_general(
        left, right, (((left_dim,), (right_dim,)), ((), ())), preferred_element_type=F32
    )


def call(kernel, out_shape, scratch=(), far=()):
    def run(*operands):
        specs = [pl.BlockSpec(memory_space=pltpu.VMEM)] * len(operands)
        operands = list(operands)
        for i, operand in enumerate(operands):
            if i in far:
                specs[i] = pl.BlockSpec(memory_space=pltpu.HBM)
                operands[i] = pltpu.with_memory_space_constraint(operand, pltpu.HBM)
            elif operand.size * operand.dtype.itemsize <= HELD_BYTES:
                operands[i] = pltpu.with_memory_space_constraint(operand, pltpu.VMEM)
        return pl.pallas_call(
            kernel,
            out_shape=out_shape,
            in_specs=specs,
            out_specs=jax.tree.map(
                lambda out: pl.BlockSpec(
                    memory_space=pltpu.HBM
                    if getattr(out, "memory_space", None) == pltpu.HBM
                    else pltpu.VMEM
                ),
                out_shape,
            ),
            scratch_shapes=list(scratch),
            compiler_params=pltpu.CompilerParams(vmem_limit_bytes=VMEM_BYTES),
        )(*operands)

    return run


def held(shape, dtype):
    small = np.prod(shape) * np.dtype(dtype).itemsize <= HELD_BYTES
    return (pltpu.VMEM if small else jax.ShapeDtypeStruct)(shape, dtype)


def pad8(amount):
    return -(-amount // 8) * 8


def shift_selector(rows, cols, tiles):
    width, padded = tiles * cols, pad8(cols)
    select = np.zeros((3, rows, width, tiles, rows, padded), np.float32)
    for shift in (-1, 0, 1):
        for j in range(max(0, shift), min(width, width + shift)):
            tile, inner = divmod(j - shift, cols)
            for i in range(rows):
                select[shift + 1, i, j, tile, i, inner] = 1
    return select.reshape(3, rows * width, tiles * rows * padded)


def tile_selector(rows, cols, tiles):
    width, padded = tiles * cols, pad8(cols)
    select = np.zeros((tiles, rows, padded, rows, width), np.float32)
    for tile in range(tiles):
        for i in range(rows):
            for inner in range(cols):
                select[tile, i, inner, i, tile * cols + inner] = 1
    return select.reshape(tiles, rows * padded, rows * width)


def start_copies(pairs, sems):
    copies = [
        pltpu.make_async_copy(src, dst, sems.at[i]) for i, (src, dst) in enumerate(pairs)
    ]
    for copy in copies:
        copy.start()
    return copies


def beside(left, right):
    return jnp.concatenate([left, right], 0).T


def pack_kernel(out_grad, pre_silu, keys, values, tile, kv, k_ref, v_ref, sems):
    copies = start_copies(
        [
            (values, v_ref),
            (keys, k_ref),
            (out_grad, tile.at[0]),
            (pre_silu, tile.at[1]),
        ],
        sems,
    )
    copies[0].wait()
    copies[1].wait()
    kv[0] = beside(v_ref[0], k_ref[0])
    kv[1] = beside(k_ref[1], v_ref[1])
    copies[2].wait()
    copies[3].wait()


def rim_kernel(n_col, per_sample, *refs):
    tiles, (*parts, query, to_core, to_chip, joined, ours, rims) = refs[:n_col], refs[n_col:]
    col = lax.axis_index("col")
    rows = tiles[0].shape[1]
    lanes = to_chip.shape[1]
    used = rims.shape[1] * rims.shape[2]
    inner = jnp.where(lax.axis_index("row") % 2 == 1, rows - 1, 0)
    cols = tiles[0].shape[2]
    rest = jnp.zeros((rims.shape[2] - cols, rims.shape[3]), F32)
    to_core[1] = query[...]
    for side, (row, out) in enumerate(((inner, to_core.at[0]), (rows - 1 - inner, to_chip))):
        for k, tile in enumerate(tiles):
            rims[side, col ^ k] = jnp.concatenate([pick(tile[0, row], col // per_sample), rest], 0)
        flat = rims[side].reshape(used, -1).astype(BF16)
        out[...] = jnp.zeros_like(out)
        for part in range(flat.shape[1] // lanes):
            out[part * used : (part + 1) * used] = flat[:, part * lanes : (part + 1) * lanes]
    join_kernel([part.shape[0] for part in parts], *parts, joined)
    join_kernel([part.shape[0] for part in parts], *parts, ours)
    joined[joined.shape[0] - 1] = to_chip[...]


def join_kernel(counts, *refs):
    *parts, out = refs
    first = 0
    for part, count in zip(parts, counts):
        for j in range(count):
            out[first + j] = part[j]
        first += count


def load_kernel(queries, *refs):
    *copied, query, q_ref, sems = refs
    half = len(copied) // 2
    copies = start_copies([(queries, q_ref), *zip(copied[:half], copied[half:])], sems)
    copies[0].wait()
    query[...] = beside(q_ref[1], q_ref[0]) * jnp.asarray(q_ref.shape[1] ** -0.5, BF16)
    for copy in copies[1:]:
        copy.wait()


def pick(cells, sample):
    place = lax.broadcasted_iota(jnp.int32, cells.shape, 1)
    return jnp.sum(jnp.where(place == sample, cells.astype(F32), 0.0), axis=1)


def conv_kernel(n_col, per_sample, *refs):
    tiles, (shifts, conv_weight, conv_ref, gate_ref, grads, silus) = refs[:n_col], refs[n_col:]
    col = lax.axis_index("col")
    sample = col // per_sample
    _, rows, cols, _, channels = tiles[0].shape
    width = n_col * cols
    grads[...] = jnp.zeros_like(grads)
    silus[...] = jnp.zeros_like(silus)
    for k in range(n_col):
        for i in range(rows):
            grads[col ^ k, i, :cols] = pick(tiles[k][0, i], sample)
            silus[col ^ k, i, :cols] = pick(tiles[k][1, i], sample)
    flat = grads[...].reshape(-1, channels).astype(BF16)
    none = jnp.zeros((width, channels), F32)
    conv = jnp.zeros((rows * width, channels), F32)
    for b in (-1, 0, 1):
        here = dot(shifts[b + 1], flat)
        above = jnp.concatenate([none, here[:-width]], 0)
        below = jnp.concatenate([here[width:], none], 0)
        for a, window in ((-1, below), (0, here), (1, above)):
            conv = conv + dot(window.astype(BF16), conv_weight[a + 1, b + 1], 1, 1)
    conv_ref[...] = conv
    z = dot(shifts[1], silus[...].reshape(-1, channels).astype(BF16))
    sigma = 1.0 / (1.0 + jnp.exp(-z))
    gate_ref[...] = sigma * (1.0 + z * (1.0 - sigma))


def rim_conv_kernel(halo_core, halo_last, halo_odd, conv, gate, *refs):
    shifts, conv_weight, out_weight, gz_ref, go_ref = refs
    col, row = lax.axis_index("col"), lax.axis_index("row")
    core, chip = row % 2, row // 2
    strip, channels = gz_ref.shape
    lanes = go_ref.shape[1]
    per_sample = out_weight.shape[0] // lanes
    width = shifts.shape[1]
    used = shifts.shape[2]
    last = halo_last[halo_last.shape[0] - 1]
    missing = jnp.logical_or(row == 1, row == lax.axis_size("row") - 2)
    halo_chip = jnp.where(core == chip % 2, last, halo_odd[...])
    halo_chip = jnp.where(missing, jnp.zeros_like(last), halo_chip)
    inner = halo_core[0]
    parts = channels // lanes

    def spread(halo):
        return jnp.concatenate([halo[p * used : (p + 1) * used] for p in range(parts)], 1)

    rims = (
        spread(jnp.where(core == 1, halo_chip, inner)),
        spread(jnp.where(core == 1, inner, halo_chip)),
    )
    edges = []
    for flat, a in zip(rims, (1, -1)):
        edge = jnp.zeros((width, channels), F32)
        for b in (-1, 0, 1):
            window = dot(shifts[b + 1], flat).astype(BF16)
            edge = edge + dot(window, conv_weight[a + 1, b + 1], 1, 1)
        edges.append(edge)
    between = jnp.zeros((strip - 2 * width, channels), F32)
    total = conv[...] + jnp.concatenate([edges[0], between, edges[1]], 0)
    grad_z = (total * gate[...]).astype(BF16)
    gz_ref[...] = grad_z
    first = pl.multiple_of(col % per_sample * lanes, lanes)
    go_ref[...] = dot(grad_z, out_weight[pl.ds(first, lanes), :], 1, 1).astype(BF16)


def by_head(query, grad_out):
    low = lax.broadcasted_iota(jnp.int32, query.shape, 1) < query.shape[1] // 2
    none = jnp.zeros_like(query)
    asked = (jnp.where(low, none, query), jnp.where(low, query, none))
    return asked, (jnp.where(low, grad_out, none), jnp.where(low, none, grad_out))


def chunks_of(offsets):
    even = [offset != 0 and offset.bit_count() % 2 == 0 for offset in offsets]
    sent = [(e, j, offset) for j, (e, offset) in enumerate(zip(even, offsets))]
    return sent, [(not e, j, offset) for e, j, offset in sent]


def all_keys(arrays, head):
    return jnp.concatenate(
        [kv[2 * j + head].astype(F32) for kv in arrays for j in range(kv.shape[0] // 2)], 0
    ).astype(BF16)


def score_kernel(*refs):
    *arrays, asker, grad_out, scores, probs_grads = refs
    asked, cotangent = by_head(asker[1], grad_out[...])
    for head in (0, 1):
        keys = all_keys(arrays, head)
        scores[head] = dot(keys, asked[head], 1, 1)
        probs_grads[head] = dot(keys, cotangent[head], 1, 1)


def softmax_kernel(offsets, late, asker, grad_out, scores, probs_grads, *outs):
    dkv_sent, grad_scores, kept_probs = outs
    strip = grad_out.shape[0]
    heads = (0, 1)
    asked, cotangent = by_head(asker[1], grad_out[...])
    sent, kept = chunks_of(offsets)

    def arranged(first, second):
        both = jnp.concatenate([first, second], 0)
        places = [(len(offsets) if kept_here else 0) + j for kept_here, j, _ in sent + kept]
        return jnp.concatenate([both[i * strip : (i + 1) * strip] for i in places], 0)

    keys = [all_keys([late], h) for h in heads]
    late_scores = [dot(keys[h], asked[h], 1, 1) for h in heads]
    late_grads = [dot(keys[h], cotangent[h], 1, 1) for h in heads]
    both = [arranged(scores[h], late_scores[h]) for h in heads]
    grads = [arranged(probs_grads[h], late_grads[h]) for h in heads]
    exps = [jnp.exp(x - jnp.max(x, axis=0, keepdims=True)) for x in both]
    scales = [1.0 / jnp.sum(e, axis=0, keepdims=True) for e in exps]
    row_dots = [jnp.sum(e * g, axis=0, keepdims=True) * s for e, g, s in zip(exps, grads, scales)]
    probs = [(e * s) for e, s in zip(exps, scales)]
    middle = len(sent) * strip
    for h in heads:
        grad = (probs[h] * (grads[h] - row_dots[h])).astype(BF16)
        grad_scores[h] = grad
        rounded = probs[h].astype(BF16)
        kept_probs[h] = rounded[middle:]
        given = jnp.concatenate([grad[:middle], rounded[:middle]], 1)
        dkv = dot(given, jnp.concatenate([asked[h], cotangent[h]], 0))
        for i, (_, _, offset) in enumerate(sent):
            dkv_sent[offset, h] = dkv[i * strip : (i + 1) * strip].astype(BF16)


def base(dq, gz_ref, input_weight):
    strip, lanes = dq.shape
    part = lax.axis_index("col") % (gz_ref.shape[1] // lanes)
    first = pl.multiple_of(part * lanes, lanes)
    grad = jnp.where(part == 0, gz_ref[...].astype(F32), 0.0)
    query = pltpu.roll(dq * (lanes // 2) ** -0.5, lanes // 2, 1).astype(BF16)
    return grad + dot(query, input_weight[:, pl.ds(first, lanes)], 1, 1)


def turned_weight(channels, lanes, input_weight):
    part = lax.axis_index("col") % (channels // lanes)
    key, value = (
        input_weight[:, pl.ds(pl.multiple_of(kind * channels + part * lanes, lanes), lanes)]
        for kind in (1, 2)
    )
    key = pltpu.roll(key.astype(F32), lanes // 2, 1)
    return jnp.concatenate([key, value.astype(F32)], 1).T.astype(BF16)


def finish_kernel(offsets, *refs):
    arrays, (asker, grad_out, grad_scores, kept_probs, gz_ref, input_weight) = refs[:4], refs[4:10]
    dkv_kept, base_ref, turned_ref = refs[10:]
    turned_ref[...] = turned_weight(gz_ref.shape[1], asker.shape[2], input_weight)
    strip, lanes = grad_out.shape
    asked, cotangent = by_head(asker[1], grad_out[...])
    sent, kept = chunks_of(offsets)
    middle = len(sent) * strip
    query = []
    for h in (0, 1):
        given = jnp.concatenate([grad_scores[h, middle:], kept_probs[h]], 1)
        dkv = dot(given, jnp.concatenate([asked[h], cotangent[h]], 0))
        for i, (_, _, offset) in enumerate(kept):
            dkv_kept[offset, h] = dkv[i * strip : (i + 1) * strip].astype(BF16)
        keys = all_keys(arrays, h)
        places = [(len(offsets) if kept_here else 0) + j for kept_here, j, _ in sent + kept]
        keys = jnp.concatenate([keys.astype(F32)[i * strip : (i + 1) * strip] for i in places], 0)
        query.append(dot(grad_scores[h], keys.astype(BF16), 0, 0))
    low = lax.broadcasted_iota(jnp.int32, (strip, lanes), 1) < lanes // 2
    base_ref[...] = base(jnp.where(low, query[1], query[0]), gz_ref, input_weight)


def long_kernel(offsets, *refs):
    kv_sent, kv_kept, asker, grad_out, gz_ref, input_weight = refs[:6]
    dkv_sent, dkv_kept, base_ref, turned_ref = refs[6:]
    turned_ref[...] = turned_weight(gz_ref.shape[1], asker.shape[2], input_weight)
    strip, lanes = grad_out.shape
    asked, cotangent = by_head(asker[1], grad_out[...])
    sent, kept = chunks_of(offsets)
    query = []
    for head in (0, 1):
        ask, cot = asked[head], cotangent[head]

        def gather(kv, carry):
            top, norm, weighted = carry
            scores = dot(kv, ask, 1, 1)
            new = jnp.maximum(top, jnp.max(scores, axis=0, keepdims=True))
            exps = jnp.exp(scores - new)
            rescale = jnp.exp(top - new)
            weights = jnp.sum(exps * dot(kv, cot, 1, 1), axis=0, keepdims=True)
            return (
                new,
                norm * rescale + jnp.sum(exps, axis=0, keepdims=True),
                weighted * rescale + weights,
            )

        zero = jnp.zeros((1, strip), F32)
        stats = (jnp.full((1, strip), -jnp.inf, F32), zero, zero)
        for src in (kv_sent, kv_kept):
            stats = lax.fori_loop(
                0,
                len(offsets),
                lambda j, carry, src=src: gather(src[2 * j + head], carry),
                stats,
            )
        top, norm, weighted = stats
        scale = 1.0 / norm
        total = jnp.zeros((strip, lanes), F32)
        for dst, chunks in ((dkv_sent, sent), (dkv_kept, kept)):
            for late, j, offset in chunks:
                kv = (kv_kept if late else kv_sent)[2 * j + head]
                probs = jnp.exp(dot(kv, ask, 1, 1) - top) * scale
                grad_scores = (probs * (dot(kv, cot, 1, 1) - weighted * scale)).astype(BF16)
                dkv = dot(grad_scores, ask) + dot(probs.astype(BF16), cot)
                dst[offset, head] = dkv.astype(BF16)
                total = total + dot(grad_scores, kv, 0, 0)
        query.append(total)
    low = lax.broadcasted_iota(jnp.int32, (strip, lanes), 1) < lanes // 2
    base_ref[...] = base(jnp.where(low, query[1], query[0]), gz_ref, input_weight)


def core_sum_kernel(own, received, *outs):
    for j, out in enumerate(outs):
        out[...] = (own[j].astype(F32) + received[j].astype(F32)).astype(BF16)


def project_kernel(n_col, per_sample, *refs):
    *refs, cut = refs
    n_in = len(refs) - n_col
    *parts, base_ref, weight, tiles = refs[:n_in]
    outs = refs[n_in:]
    col = lax.axis_index("col")
    part = col % per_sample
    total = sum(ref[...].astype(F32) for ref in parts)
    _, strip, lanes = parts[0].shape
    half = lanes // 2
    channels = base_ref.shape[1]
    low = lax.broadcasted_iota(jnp.int32, (strip, lanes), 1) < half
    dv = jnp.where(low, total[0], total[1])
    dk = jnp.where(low, total[1], total[0])
    given = jnp.concatenate([dk, dv], 1).astype(BF16)
    grad = base_ref[...] + dot(given, weight[...])
    cut[...] = dot(tiles[...], grad.astype(BF16)).reshape(cut.shape)
    for k, out in enumerate(outs):
        out[...] = cut[col ^ k].astype(BF16)


def output_kernel(per_sample, *refs):
    *parts, far_out, out, sem = refs
    parts = parts[::-1]
    rows, cols, samples, channels = out.shape
    padded = pad8(cols)
    sample = lax.axis_index("col") // per_sample
    place = lax.broadcasted_iota(jnp.int32, (cols, samples, channels), 1)
    for i in range(rows):
        cells = jnp.zeros((cols, samples, channels), F32)
        for group in range(samples):
            total = sum(
                ref[...][i * padded : i * padded + cols].astype(F32)
                for ref in parts[group * per_sample : (group + 1) * per_sample]
            )
            cells = jnp.where(place == (sample ^ group), total[:, None, :], cells)
        out[i] = cells.astype(BF16)
    copy = pltpu.make_async_copy(out, far_out, sem)
    copy.start()
    copy.wait()


def shards(
    pre_silu, out_grad, query_heads, key_heads, value_heads, conv_weight, out_weight, input_weight
):
    samples, rows, cols, channels = pre_silu.shape
    pairs, strip, head_dim = query_heads.shape
    n_row, n_col = lax.axis_size("row"), lax.axis_size("col")
    chips = n_row // 2
    per_sample = HEADS // pairs
    lanes = pairs * head_dim

    def to_col(array, k):
        pairs_of = [
            (r * n_col + c, (r ^ 1) * n_col + (c ^ k)) for r in range(n_row) for c in range(n_col)
        ]
        return lax.ppermute(array, ("row", "col"), pairs_of)

    def to_chip(array, k):
        return lax.ppermute(array, "row", [(i, i ^ (2 * k + 1)) for i in range(n_row)])

    def to_core(array):
        return lax.ppermute(array, "row", [(i, i ^ 1) for i in range(n_row)])

    def to_odd_chip(array):
        both = [(0, 1), (n_row - 2, n_row - 1)]
        for i in range(2, n_row - 2, 4):
            both += [(i, i + 3), (i + 1, i + 2)]
        return lax.ppermute(array, "row", both + [(j, i) for i, j in both])

    def cells(array):
        return jnp.transpose(array, (1, 2, 0, 3))

    def turned(array):
        return jnp.transpose(array, (0, 2, 1))

    saved = pltpu.VMEM((pairs, head_dim, strip), BF16)
    tile, kv = call(
        pack_kernel,
        (
            held((2, rows, cols, samples, channels), BF16),
            held((pairs, strip, lanes), BF16),
        ),
        (saved, saved, pltpu.SemaphoreType.DMA((4,))),
        range(4),
    )(cells(out_grad), cells(pre_silu), turned(key_heads), turned(value_heads))
    tiles = [to_col(tile, k) for k in range(n_col)]

    padded = pad8(cols)
    far = (
        jnp.asarray(shift_selector(rows, cols, n_col), BF16),
        jnp.asarray(shift_selector(1, cols, n_col), BF16),
        conv_weight,
        out_weight,
    )
    *loaded, query = call(
        load_kernel,
        [held(array.shape, BF16) for array in far] + [held((strip, lanes), BF16)],
        [saved, pltpu.SemaphoreType.DMA((len(far) + 1,))],
        range(len(far) + 1),
    )(turned(query_heads), *far)

    def doubled(*parts, counts=None):
        counts = counts or [part.shape[0] for part in parts]
        return call(
            functools.partial(join_kernel, counts), held((sum(counts), strip, lanes), BF16)
        )(*parts)

    distances = [chips >> (i + 1) for i in range(chips.bit_length() - 1)]
    offsets = [0]
    for distance in distances:
        offsets = offsets + [offset + distance for offset in offsets]
    tiles, received, (shifts, rim_shifts, conv_weight, out_weight) = lax.optimization_barrier(
        (tiles, to_chip(kv, distances[0]), loaded)
    )
    parts = (kv, received)
    for distance in distances[1:-1]:
        joined = doubled(*parts)
        parts = (joined, to_chip(joined, distance))

    rim = held((strip, lanes), BF16)
    blocks = sum(part.shape[0] for part in parts)
    rim_core, rim_chip, sent, ours = call(
        functools.partial(rim_kernel, n_col, per_sample),
        (held((2, strip, lanes), BF16), rim, held((blocks + 1, strip, lanes), BF16), held((blocks, strip, lanes), BF16)),
        [pltpu.VMEM((2, n_col, padded, channels), F32)],
    )(*tiles, *parts, query)
    received = to_chip(sent, distances[-1])
    halo_odd, halo_core, early = to_odd_chip(rim_chip), to_core(rim_core), to_core(ours)

    whole = held((strip, channels), F32)
    conv, gate = call(
        functools.partial(conv_kernel, n_col, per_sample),
        (whole, whole),
        [pltpu.VMEM((n_col, rows, padded, channels), F32)] * 2,
    )(*tiles, shifts, conv_weight)
    received, conv, halo_odd, halo_core, early = lax.optimization_barrier(
        (received, conv, halo_odd, halo_core, early)
    )
    late = to_core(received)
    grad_z, grad_out = call(
        rim_conv_kernel,
        (held((strip, channels), BF16), held((strip, lanes), BF16)),
    )(halo_core, received, halo_odd, conv, gate, rim_shifts, conv_weight, out_weight)

    block = held((chips, pairs, strip, lanes), BF16)
    given = held((2 * lanes, channels), BF16)
    if 2 * chips <= UNROLLED_CHUNKS:
        most = held((pairs, (2 * chips - blocks // 2) * strip, strip), F32)
        scores, probs_grads = call(score_kernel, (most, most))(
            sent, received, early, halo_core, grad_out
        )
        dkv_sent, grad_scores, kept_probs = call(
            functools.partial(softmax_kernel, offsets),
            (
                block,
                held((pairs, 2 * chips * strip, strip), BF16),
                held((pairs, chips * strip, strip), BF16),
            ),
        )(late, halo_core, grad_out, scores, probs_grads)
        from_core = to_core(dkv_sent)
        dkv_kept, complete, weight = call(
            functools.partial(finish_kernel, offsets), (block, whole, given)
        )(
            sent,
            received,
            early,
            late,
            halo_core,
            grad_out,
            grad_scores,
            kept_probs,
            grad_z,
            input_weight,
        )
    else:
        joined = doubled(sent, received, counts=(blocks, blocks))
        other = doubled(early, late, counts=(blocks, blocks))
        dkv_sent, dkv_kept, complete, weight = call(
            functools.partial(long_kernel, offsets), (block, block, whole, given)
        )(joined, other, halo_core, grad_out, grad_z, input_weight)
        from_core = to_core(dkv_sent)

    sums = call(core_sum_kernel, [held((pairs, strip, lanes), BF16) for _ in range(chips)])(
        dkv_kept, from_core
    )
    far_near = [k for pair in zip(range(chips - 1, 0, -1), range(1, chips)) for k in pair]
    order = list(dict.fromkeys(far_near))
    parts = [to_chip(sums[k], k) for k in order] + [sums[0]]

    selected = tile_selector(rows, cols, n_col).reshape(n_col * rows * padded, -1)
    cut = call(
        functools.partial(project_kernel, n_col, per_sample),
        [held((rows * padded, channels), BF16)] * n_col,
        [pltpu.VMEM((n_col, rows * padded, channels), F32)],
    )(*parts, complete, weight, jnp.asarray(selected, BF16))
    grad_input = call(
        functools.partial(output_kernel, per_sample),
        pltpu.HBM((rows, cols, samples, channels), BF16),
        [pltpu.VMEM((rows, cols, samples, channels), BF16), pltpu.SemaphoreType.DMA],
    )(*[to_col(cut[k], k) for k in reversed(range(n_col))])
    return jnp.transpose(grad_input, (2, 0, 1, 3))


def solution(mesh):
    tile = P(None, "row", "col", None)
    heads = P("col", "row", None)
    return jax.shard_map(
        shards,
        mesh=mesh,
        in_specs=(tile, tile, heads, heads, heads, P(), P(), P()),
        out_specs=tile,
        check_vma=False,
    )
```
